32 devices in a mesh: phi: 8 (over y, x, core), band: 4 (over z).
Axes of the slice: x: 2, y: 2, z: 4, core: 2. Of those that a mesh axis runs over, the one named last changes fastest.
Arguments:
- density: float32 [128, 64, 256], P('phi', 'band'), may hold values from 0.5 to 2
- velocity: float32 [3, 128, 64, 256], P(None, 'phi', 'band'), may hold values from -3 to 3
- magnetic_vector: float32 [3, 128, 64, 256], P(None, 'phi', 'band'), may hold values from -3 to 3
- pressure: float32 [128, 64, 256], P('phi', 'band'), may hold values from 0.2 to 2
- fluid_courant_number: float32 [], replicated, may hold values from 0.3 to 0.6
- cosmic_ray_density: float32 [64, 128, 64, 128], P('band', 'phi'), may hold values from 0.3 to 3
- diffusion_per_bin: float32 [64], replicated, may hold values from 0.15 to 0.5
- super_step_scale: float32 [], replicated, may hold values from 2 to 4
Outputs:
- fluid_state: float32 [8, 128, 64, 256], P(None, 'phi', 'band')
- cosmic_ray_next: float32 [64, 128, 64, 128], P('band', 'phi')
The draws below stay inside these ranges and needn't reach their ends.
All inputs are finite; a program needn't handle non-finite values.
Results may differ from the reference program's by a relative error of at most 0.00125.
Values may be sent and summed in bfloat16 or wider, within the bound.
A program may use at most 256 MiB of HBM per device.

```python
import math
import jax
import jax.numpy as jnp
from jax import lax

RADIAL_CELLS = 256
OUTER_SHELLS = 128
MOMENTUM_BINS = 64
AZIMUTH_CELLS = 128
COLAT_CELLS = 64


def draw_magnetic_vector(key, part):
    transverse_key, strength_key, polarity_key = jax.random.split(key, 3)
    transverse = jnp.clip(0.35 * jax.random.normal(transverse_key, (2, AZIMUTH_CELLS, COLAT_CELLS, RADIAL_CELLS), jnp.float32), -1.2, 1.2)
    strength = jax.random.uniform(strength_key, (AZIMUTH_CELLS, COLAT_CELLS, RADIAL_CELLS), jnp.float32, 1.2, 2.8)
    polarity = 2.0 * jax.random.randint(polarity_key, (AZIMUTH_CELLS, COLAT_CELLS, RADIAL_CELLS), 0, 2).astype(jnp.float32) - 1.0
    return jnp.concatenate([transverse, (polarity * strength)[None]], axis=0)


def block_levels(key, shape, pieces, low, top_value):
    def one(axis_at, parts):
        steps = jax.random.uniform(jax.random.fold_in(jax.random.fold_in(key, 6), axis_at), (parts,), jnp.float32, low / len(pieces), top_value / len(pieces))
        return jnp.repeat(jnp.exp(steps), shape[axis_at] // parts).reshape((-1,) + (1,) * (len(shape) - axis_at - 1))

    gain = one(*pieces[0])
    for cut in pieces[1:]:
        gain = gain * one(*cut)
    return gain


def scatter_about(stream_key, dims, width, limit, pieces=(), kind=jnp.bfloat16):
    entries = jax.random.normal(stream_key, dims, jnp.float32) * width
    if len(pieces) > 0:
        entries = block_levels(stream_key, dims, pieces, -0.22, 0.18) * entries
    return jnp.clip(entries, min=-limit, max=limit).astype(kind)


def setup_inputs(seed: int = 0) -> dict:
    key_list = jax.random.split(jax.random.key(seed), 9)
    return {
        "density": jnp.clip(jnp.exp(math.log(2.0) - 1.3862944 * jax.random.uniform(key_list[0], (AZIMUTH_CELLS, COLAT_CELLS, RADIAL_CELLS), jnp.float32) ** block_levels(key_list[0], (AZIMUTH_CELLS, COLAT_CELLS, RADIAL_CELLS), ((0, 8), (1, 4)), -0.2, 0.2)), 0.5, 2.0),
        "velocity": scatter_about(key_list[1], (3, AZIMUTH_CELLS, COLAT_CELLS, RADIAL_CELLS), 0.5, 3.0, ((1, 8), (2, 4)), jnp.float32),
        "magnetic_vector": draw_magnetic_vector(jax.random.fold_in(key_list[8], 71), 0),
        "pressure": jnp.clip(jnp.exp(math.log(2.0) - 2.3025851 * jax.random.uniform(key_list[3], (AZIMUTH_CELLS, COLAT_CELLS, RADIAL_CELLS), jnp.float32) ** block_levels(key_list[3], (AZIMUTH_CELLS, COLAT_CELLS, RADIAL_CELLS), ((0, 8), (1, 4)), -0.2, 0.2)), 0.2, 2.0),
        "fluid_courant_number": jnp.clip(jax.random.uniform(key_list[4], (), jnp.float32, 0.3, 0.6), 0.3, 0.6),
        "cosmic_ray_density": jnp.clip(jnp.exp(math.log(3.0) - 2.3025851 * jax.random.uniform(key_list[5], (MOMENTUM_BINS, AZIMUTH_CELLS, COLAT_CELLS, OUTER_SHELLS), jnp.float32) ** block_levels(key_list[5], (MOMENTUM_BINS, AZIMUTH_CELLS, COLAT_CELLS, OUTER_SHELLS), ((0, 4), (1, 8)), -0.2, 0.2)), 0.3, 3.0),
        "diffusion_per_bin": jnp.clip(jnp.exp(jax.random.uniform(key_list[6], (MOMENTUM_BINS,), jnp.float32, math.log(0.15), math.log(0.5))), 0.15, 0.5),
        "super_step_scale": jnp.clip(jax.random.uniform(key_list[7], (), jnp.float32, 2.0, 4.0), 2.0, 4.0),
    }


ADIABATIC = 5.0 / 3.0
INNER_RADIUS = 0.1
R_RATIO = 30.0
COLAT_LOW = math.pi / 6.0
COLAT_SPAN = 2.0 * math.pi / 3.0
P_RATIO = 1000.0
K_RATIO = 0.1
B_FLOOR = 0.1
V_BOUND = 3.0
B_BOUND = 3.0
P_HIGH = 2.0
RHO_LOW = 0.5
KAPPA_HIGH = 0.5

def grid_steps(n_radial, n_colat, n_azim, n_bins):
    return (math.log(R_RATIO) / n_radial, COLAT_SPAN / n_colat, 2.0 * math.pi / n_azim, math.log(P_RATIO) / n_bins)

def rate_limits(n_radial, n_shells, n_colat, n_azim, n_bins):
    radial_spacing, colatitude_spacing, azimuth_spacing, step_m = grid_steps(n_radial, n_colat, n_azim, n_bins)
    sine_lower = math.sin(COLAT_LOW + 0.5 * colatitude_spacing)
    fluid_radius = INNER_RADIUS * math.exp(0.5 * radial_spacing)
    fastest_limit = V_BOUND + math.sqrt((ADIABATIC * P_HIGH + 3.0 * B_BOUND ** 2) / RHO_LOW)
    fluid_rate = fastest_limit * (1.0 / (fluid_radius * radial_spacing) + 1.0 / (fluid_radius * colatitude_spacing) + 1.0 / (fluid_radius * sine_lower * azimuth_spacing))
    shell_low = INNER_RADIUS * math.exp(radial_spacing * (n_radial - n_shells + 0.5))
    inv_r = 1.0 / (shell_low * radial_spacing)
    inv_t = 1.0 / (shell_low * colatitude_spacing)
    inv_p = 1.0 / (shell_low * sine_lower * azimuth_spacing)
    cosmic_ray_rate = 2.0 * KAPPA_HIGH * (inv_r ** 2 + inv_t ** 2 + inv_p ** 2) + V_BOUND * (inv_r + inv_t + inv_p) + V_BOUND * (inv_r + inv_t + inv_p + 4.0 / shell_low) / (3.0 * step_m)
    return (fluid_rate, cosmic_ray_rate)

def shell_radii(start_index, cell_count, n_radial):
    cell_index = jnp.arange(cell_count, dtype=jnp.float32) + (start_index + 0.5)
    return INNER_RADIUS * jnp.exp(math.log(R_RATIO) / n_radial * cell_index)

def colatitudes(start_index, cell_count, n_colat):
    cell_index = jnp.arange(cell_count, dtype=jnp.float32) + 0.5
    return COLAT_LOW + COLAT_SPAN * (cell_index + start_index) / n_colat

def rounded(values):
    return lax.optimization_barrier(values.astype(jnp.bfloat16)).astype(jnp.float32)

def conserved(primitive):
    density = primitive[0]
    velocity = primitive[1:4]
    magnetic_vector = primitive[4:7]
    pressure = primitive[7]
    energy = pressure / (ADIABATIC - 1.0) + 0.5 * density * lax.optimization_barrier(jnp.sum(velocity * velocity, axis=0)) + 0.5 * lax.optimization_barrier(jnp.sum(magnetic_vector * magnetic_vector, axis=0))
    return jnp.concatenate([density[None], density[None] * velocity, magnetic_vector, energy[None]], axis=0)

def face_terms(primitive, cell_state, normal):
    density = primitive[0]
    velocity = primitive[1:4]
    magnetic_vector = primitive[4:7]
    pressure = primitive[7]
    v_normal = velocity[normal]
    b_normal = magnetic_vector[normal]
    magnetic = 0.5 * lax.optimization_barrier(jnp.sum(magnetic_vector * magnetic_vector, axis=0))
    total_p = pressure + magnetic
    momentum = [density * velocity[k] * v_normal - magnetic_vector[k] * b_normal for k in range(3)]
    momentum[normal] = momentum[normal] + total_p
    induction = [v_normal * magnetic_vector[k] - b_normal * velocity[k] for k in range(3)]
    energy_flux = (cell_state[7] + total_p) * v_normal - b_normal * lax.optimization_barrier(jnp.sum(velocity * magnetic_vector, axis=0))
    fluxes = jnp.stack([density * v_normal] + momentum + induction + [energy_flux], axis=0)
    speeds = jnp.abs(v_normal) + jnp.sqrt((ADIABATIC * pressure + 2.0 * magnetic) / density)
    return (fluxes, speeds)

def rusanov(primitive, cell_state, normal, along_axis, spacing):
    fluxes, speeds = face_terms(primitive, cell_state, normal)
    length = speeds.shape[along_axis]
    wave_speed = jnp.maximum(lax.slice_in_dim(speeds, 0, length - 1, axis=along_axis), lax.slice_in_dim(speeds, 1, length, axis=along_axis))
    flux_low = lax.slice_in_dim(fluxes, 0, length - 1, axis=along_axis + 1)
    flux_high = lax.slice_in_dim(fluxes, 1, length, axis=along_axis + 1)
    state_low = lax.slice_in_dim(cell_state, 0, length - 1, axis=along_axis + 1)
    state_high = lax.slice_in_dim(cell_state, 1, length, axis=along_axis + 1)
    face_flux = 0.5 * (flux_low + flux_high) - 0.5 * wave_speed[None] * (state_high - state_low)
    upper = lax.slice_in_dim(face_flux, 1, length - 1, axis=along_axis + 1)
    lower = lax.slice_in_dim(face_flux, 0, length - 2, axis=along_axis + 1)
    return (upper - lower) / spacing

def fluid_update(padded_array, radius_values, colatitude_mesh, timestep_length, mesh_spacing):
    ghosted = jnp.pad(padded_array, ((0, 0), (0, 0), (0, 0), (1, 1)), mode='edge')
    cell_state = conserved(ghosted)
    width_r = radius_values * mesh_spacing[0]
    width_t = radius_values * mesh_spacing[1]
    width_p = jnp.sin(colatitude_mesh)[:, None] * radius_values * mesh_spacing[2]
    radial = rusanov(ghosted[:, 1:-1, 1:-1, :], cell_state[:, 1:-1, 1:-1, :], 0, 2, width_r)
    polar = rusanov(ghosted[:, 1:-1, :, 1:-1], cell_state[:, 1:-1, :, 1:-1], 1, 1, width_t)
    azimuthal = rusanov(ghosted[:, :, 1:-1, 1:-1], cell_state[:, :, 1:-1, 1:-1], 2, 0, width_p)
    return cell_state[:, 1:-1, 1:-1, 1:-1] - timestep_length * (radial + polar + azimuthal)

def divergence(radial_pad, polar_pad, azim_pad, radius_values, colatitude_mesh, mesh_spacing):
    sin_colat = jnp.sin(colatitude_mesh)[:, None]
    cotangent = (jnp.cos(colatitude_mesh) / jnp.sin(colatitude_mesh))[:, None]
    radial_mid = radial_pad[:, :, 1:-1]
    polar_mid = polar_pad[:, 1:-1, :]
    d_radial = (radial_pad[:, :, 2:] - radial_pad[:, :, :-2]) / (2.0 * radius_values * mesh_spacing[0])
    d_polar = (polar_pad[:, 2:, :] - polar_pad[:, :-2, :]) / (2.0 * radius_values * mesh_spacing[1])
    d_azim = (azim_pad[2:] - azim_pad[:-2]) / (2.0 * radius_values * sin_colat * mesh_spacing[2])
    return d_radial + 2.0 * radial_mid / radius_values + d_polar + cotangent * polar_mid / radius_values + d_azim

def transport_coefficients(wind_vel, mag_wind, spread, radius_values, colatitude_mesh, mesh_spacing):
    width_r = radius_values * mesh_spacing[0]
    width_t = radius_values * mesh_spacing[1]
    width_p = jnp.sin(colatitude_mesh)[:, None] * radius_values * mesh_spacing[2]
    widths = (width_r, width_t, width_p)
    mag_sq = lax.optimization_barrier(jnp.sum(mag_wind * mag_wind, axis=0)) + B_FLOOR
    b_share = K_RATIO + (1.0 - K_RATIO) * mag_wind * mag_wind / mag_sq
    coef_list = [b_share[k] / (widths[k] * widths[k]) for k in range(3)]
    up_list = [jnp.maximum(wind_vel[k], 0.0) / widths[k] for k in range(3)]
    down_list = [jnp.minimum(wind_vel[k], 0.0) / widths[k] for k in range(3)]
    drift_rate = spread / 3.0
    return (coef_list, up_list, down_list, jnp.maximum(drift_rate, 0.0), jnp.minimum(drift_rate, 0.0))

def transport_rate(extended, coef_set, kappa_col, step_m):
    coef_list, up_list, down_list, drift_up, drift_down = coef_set
    center = extended[1:-1, 1:-1, 1:-1, 1:-1]
    low_cells = (extended[1:-1, 1:-1, 1:-1, :-2], extended[1:-1, 1:-1, :-2, 1:-1], extended[1:-1, :-2, 1:-1, 1:-1])
    high_cells = (extended[1:-1, 1:-1, 1:-1, 2:], extended[1:-1, 1:-1, 2:, 1:-1], extended[1:-1, 2:, 1:-1, 1:-1])
    curvature = coef_list[0] * (high_cells[0] - 2.0 * center + low_cells[0])
    curvature = curvature + coef_list[1] * (high_cells[1] - 2.0 * center + low_cells[1])
    curvature = curvature + coef_list[2] * (high_cells[2] - 2.0 * center + low_cells[2])
    diffusion = kappa_col[:, None, None, None] * curvature
    advection = up_list[0] * (center - low_cells[0]) + down_list[0] * (high_cells[0] - center)
    advection = advection + up_list[1] * (center - low_cells[1]) + down_list[1] * (high_cells[1] - center)
    advection = advection + up_list[2] * (center - low_cells[2]) + down_list[2] * (high_cells[2] - center)
    bin_low = extended[:-2, 1:-1, 1:-1, 1:-1]
    bin_high = extended[2:, 1:-1, 1:-1, 1:-1]
    momentum = (drift_up * (bin_high - center) + drift_down * (center - bin_low)) / step_m
    return diffusion - advection + momentum

def full_pad(values):
    extended = jnp.pad(values, ((1, 1), (0, 0), (1, 1), (1, 1)), mode='edge')
    return jnp.pad(extended, ((0, 0), (1, 1), (0, 0), (0, 0)), mode='wrap')

def reference(density, velocity, magnetic_vector, pressure, fluid_courant_number, cosmic_ray_density, diffusion_per_bin, super_step_scale):
    mesh_spacing = grid_steps(RADIAL_CELLS, COLAT_CELLS, AZIMUTH_CELLS, MOMENTUM_BINS)
    fluid_rate, cosmic_ray_rate = rate_limits(RADIAL_CELLS, OUTER_SHELLS, COLAT_CELLS, AZIMUTH_CELLS, MOMENTUM_BINS)
    primitive = jnp.concatenate([density[None], velocity, magnetic_vector, pressure[None]], axis=0)
    padded_array = jnp.pad(primitive, ((0, 0), (1, 1), (0, 0), (0, 0)), mode='wrap')
    padded_array = jnp.pad(padded_array, ((0, 0), (0, 0), (1, 1), (0, 0)), mode='edge')
    radius_full = shell_radii(0, RADIAL_CELLS, RADIAL_CELLS)
    colatitude_full = colatitudes(0, COLAT_CELLS, COLAT_CELLS)
    fluid_state = fluid_update(padded_array, radius_full, colatitude_full, fluid_courant_number / fluid_rate, mesh_spacing)
    first_shell = RADIAL_CELLS - OUTER_SHELLS
    wind_vel = rounded(velocity[:, :, :, first_shell:])
    mag_wind = rounded(magnetic_vector[:, :, :, first_shell:])
    radius_sh = shell_radii(first_shell, OUTER_SHELLS, RADIAL_CELLS)
    radial_pad = jnp.pad(wind_vel[0], ((0, 0), (0, 0), (1, 1)), mode='edge')
    polar_pad = jnp.pad(wind_vel[1], ((0, 0), (1, 1), (0, 0)), mode='edge')
    azim_pad = jnp.pad(wind_vel[2], ((1, 1), (0, 0), (0, 0)), mode='wrap')
    spread = rounded(divergence(radial_pad, polar_pad, azim_pad, radius_sh, colatitude_full, mesh_spacing))
    coef_set = transport_coefficients(wind_vel, mag_wind, spread, radius_sh, colatitude_full, mesh_spacing)
    sts_step = super_step_scale / cosmic_ray_rate
    first_section = cosmic_ray_density + sts_step / 3.0 * transport_rate(full_pad(cosmic_ray_density), coef_set, diffusion_per_bin, mesh_spacing[3])
    cosmic_ray_next = 1.5 * first_section - 0.5 * cosmic_ray_density + sts_step / 2.0 * transport_rate(full_pad(first_section), coef_set, diffusion_per_bin, mesh_spacing[3])
    return (fluid_state, cosmic_ray_next)
```

```python
import functools
import math

import jax
import jax.numpy as jnp
import numpy as np
from jax import lax
from jax.experimental import pallas as pl
from jax.experimental.pallas import tpu as pltpu
from jax.sharding import PartitionSpec as P

ADIABATIC = 5.0 / 3.0
INNER_RADIUS = 0.1
R_RATIO = 30.0
COLAT_LOW = math.pi / 6.0
COLAT_SPAN = 2.0 * math.pi / 3.0
P_RATIO = 1000.0
K_RATIO = 0.1
B_FLOOR = 0.1
V_BOUND = 3.0
B_BOUND = 3.0
P_HIGH = 2.0
RHO_LOW = 0.5
KAPPA_HIGH = 0.5


def padded(value, sides, width):
    for axis, dim in sides:
        size, length = (lax.axis_size(axis), value.shape[dim])
        up = [(i, (i + 1) % size) for i in range(size)]
        down = [(j, i) for i, j in up]
        last = lax.slice_in_dim(value, length - width, length, axis=dim)
        leading = lax.slice_in_dim(value, 0, width, axis=dim)
        before = lax.ppermute(last, axis, up)
        after = lax.ppermute(leading, axis, down)
        value = jnp.concatenate([before, value, after], axis=dim)
    return value


def grid_steps(n_radial, n_colat, n_azim, n_bins):
    return (
        math.log(R_RATIO) / n_radial,
        COLAT_SPAN / n_colat,
        2.0 * math.pi / n_azim,
        math.log(P_RATIO) / n_bins,
    )


def rate_limits(n_radial, n_shells, n_colat, n_azim, n_bins):
    radial_spacing, colatitude_spacing, azimuth_spacing, step_m = grid_steps(
        n_radial, n_colat, n_azim, n_bins
    )
    sine_lower = math.sin(COLAT_LOW + 0.5 * colatitude_spacing)
    fluid_radius = INNER_RADIUS * math.exp(0.5 * radial_spacing)
    fastest_limit = V_BOUND + math.sqrt((ADIABATIC * P_HIGH + 3.0 * B_BOUND**2) / RHO_LOW)
    fluid_rate = fastest_limit * (
        1.0 / (fluid_radius * radial_spacing)
        + 1.0 / (fluid_radius * colatitude_spacing)
        + 1.0 / (fluid_radius * sine_lower * azimuth_spacing)
    )
    shell_low = INNER_RADIUS * math.exp(radial_spacing * (n_radial - n_shells + 0.5))
    inv_r = 1.0 / (shell_low * radial_spacing)
    inv_t = 1.0 / (shell_low * colatitude_spacing)
    inv_p = 1.0 / (shell_low * sine_lower * azimuth_spacing)
    cosmic_ray_rate = (
        2.0 * KAPPA_HIGH * (inv_r**2 + inv_t**2 + inv_p**2)
        + V_BOUND * (inv_r + inv_t + inv_p)
        + V_BOUND * (inv_r + inv_t + inv_p + 4.0 / shell_low) / (3.0 * step_m)
    )
    return (fluid_rate, cosmic_ray_rate)


def shell_radii(start_index, cell_count, n_radial):
    cell_index = jnp.arange(cell_count, dtype=jnp.float32) + (start_index + 0.5)
    return INNER_RADIUS * jnp.exp(math.log(R_RATIO) / n_radial * cell_index)


def colatitudes(start_index, cell_count, n_colat):
    cell_index = jnp.arange(cell_count, dtype=jnp.float32) + 0.5
    return COLAT_LOW + COLAT_SPAN * (cell_index + start_index) / n_colat


def edge_fix(values, along_axis, depth, band_pos, axis_count):
    extent = values.shape[along_axis]
    low_ghost = lax.slice_in_dim(values, 0, depth, axis=along_axis)
    high_ghost = lax.slice_in_dim(values, extent - depth, extent, axis=along_axis)
    first_own = lax.slice_in_dim(values, depth, depth + 1, axis=along_axis)
    last_own = lax.slice_in_dim(values, extent - depth - 1, extent - depth, axis=along_axis)
    low_rim = jnp.where(band_pos == 0, first_own, low_ghost)
    high_rim = jnp.where(band_pos == axis_count - 1, last_own, high_ghost)
    middle = lax.slice_in_dim(values, depth, extent - depth, axis=along_axis)
    return jnp.concatenate([low_rim, middle, high_rim], axis=along_axis)


def conserved(primitive):
    density = primitive[0]
    velocity = primitive[1:4]
    magnetic_vector = primitive[4:7]
    pressure = primitive[7]
    energy = (
        pressure / (ADIABATIC - 1.0)
        + 0.5 * density * jnp.sum(velocity * velocity, axis=0)
        + 0.5 * jnp.sum(magnetic_vector * magnetic_vector, axis=0)
    )
    return jnp.concatenate(
        [density[None], density[None] * velocity, magnetic_vector, energy[None]], axis=0
    )


def face_terms(primitive, cell_state, normal):
    density = primitive[0]
    velocity = primitive[1:4]
    magnetic_vector = primitive[4:7]
    pressure = primitive[7]
    v_normal = velocity[normal]
    b_normal = magnetic_vector[normal]
    magnetic = 0.5 * jnp.sum(magnetic_vector * magnetic_vector, axis=0)
    total_p = pressure + magnetic
    momentum = [density * velocity[k] * v_normal - magnetic_vector[k] * b_normal for k in range(3)]
    momentum[normal] = momentum[normal] + total_p
    induction = [v_normal * magnetic_vector[k] - b_normal * velocity[k] for k in range(3)]
    energy_flux = (cell_state[7] + total_p) * v_normal - b_normal * jnp.sum(
        velocity * magnetic_vector, axis=0
    )
    fluxes = jnp.stack([density * v_normal] + momentum + induction + [energy_flux], axis=0)
    speeds = jnp.abs(v_normal) + jnp.sqrt((ADIABATIC * pressure + 2.0 * magnetic) / density)
    return (fluxes, speeds)


def rusanov(primitive, cell_state, normal, along_axis, spacing):
    fluxes, speeds = face_terms(primitive, cell_state, normal)
    length = speeds.shape[along_axis]
    wave_speed = jnp.maximum(
        lax.slice_in_dim(speeds, 0, length - 1, axis=along_axis),
        lax.slice_in_dim(speeds, 1, length, axis=along_axis),
    )
    flux_low = lax.slice_in_dim(fluxes, 0, length - 1, axis=along_axis + 1)
    flux_high = lax.slice_in_dim(fluxes, 1, length, axis=along_axis + 1)
    state_low = lax.slice_in_dim(cell_state, 0, length - 1, axis=along_axis + 1)
    state_high = lax.slice_in_dim(cell_state, 1, length, axis=along_axis + 1)
    face_flux = 0.5 * (flux_low + flux_high) - 0.5 * wave_speed[None] * (state_high - state_low)
    upper = lax.slice_in_dim(face_flux, 1, length - 1, axis=along_axis + 1)
    lower = lax.slice_in_dim(face_flux, 0, length - 2, axis=along_axis + 1)
    return (upper - lower) / spacing


def fluid_update(padded_array, radius_values, colatitude_mesh, timestep_length, mesh_spacing):
    ghosted = jnp.pad(padded_array, ((0, 0), (0, 0), (0, 0), (1, 1)), mode="edge")
    cell_state = conserved(ghosted)
    width_r = radius_values * mesh_spacing[0]
    width_t = radius_values * mesh_spacing[1]
    width_p = jnp.sin(colatitude_mesh)[:, None] * radius_values * mesh_spacing[2]
    radial = rusanov(ghosted[:, 1:-1, 1:-1, :], cell_state[:, 1:-1, 1:-1, :], 0, 2, width_r)
    polar = rusanov(ghosted[:, 1:-1, :, 1:-1], cell_state[:, 1:-1, :, 1:-1], 1, 1, width_t)
    azimuthal = rusanov(ghosted[:, :, 1:-1, 1:-1], cell_state[:, :, 1:-1, 1:-1], 2, 0, width_p)
    return cell_state[:, 1:-1, 1:-1, 1:-1] - timestep_length * (radial + polar + azimuthal)


MESH = pl.DeviceIdType.MESH
PAD = 8


def cosmic_ray_kernel(
    bands,
    phis,
    spacing,
    kappa_ref,
    tau_ref,
    vel_ref,
    mag_ref,
    inv_r_ref,
    inv_sin_ref,
    cot_ref,
    f_hbm,
    out_hbm,
    cells,
    firsts,
    coefs,
    wind,
    edge_t,
    edge_p,
    send_phi,
    send_bin,
    recv_phi,
    recv_bin,
    load_sem,
    store_sem,
    wind_send,
    wind_recv,
    edge_t_send,
    edge_t_recv,
    edge_p_send,
    edge_p_recv,
    halo_send,
    halo_recv,
    next_send,
    next_recv,
):
    bins = f_hbm.shape[0]
    azim = f_hbm.shape[1]
    colat = f_hbm.shape[2]
    shells = f_hbm.shape[3]
    rows = colat // bands
    first_shell = vel_ref.shape[3] - shells
    step_r, step_t, step_p, step_m = spacing
    band = lax.axis_index("band")
    phi = lax.axis_index("phi")
    right = lax.rem(phi + 1, phis)
    left = lax.rem(phi + phis - 1, phis)

    load = pltpu.make_async_copy(
        f_hbm, cells.at[1 : bins + 1, 1 : azim + 1, PAD : PAD + colat], load_sem
    )
    load.start()

    barrier = pltpu.get_barrier_semaphore()
    for b in range(bands):
        for side in (left, right):
            pl.semaphore_signal(
                barrier, inc=1, device_id={"phi": side, "band": b}, device_id_type=MESH
            )
    for s in range(1, bands):
        pl.semaphore_signal(
            barrier,
            inc=1,
            device_id={"band": lax.rem(band + s, bands)},
            device_id_type=MESH,
        )

    def take(p, _):
        for c in range(3):
            wind[band, c, p] = vel_ref[c, p, :, first_shell:].astype(jnp.bfloat16)
            wind[band, 3 + c, p] = mag_ref[c, p, :, first_shell:].astype(jnp.bfloat16)
        u_t = wind[band, 1, p].astype(jnp.float32)
        edge_t[band, 0, pl.ds(p, 1), :] = u_t[0:1]
        edge_t[band, 1, pl.ds(p, 1), :] = u_t[rows - 1 : rows]
        return 0

    lax.fori_loop(0, azim, take, 0)
    edge_p[2, band] = wind[band, 2, azim - 1].astype(jnp.float32)
    edge_p[3, band] = wind[band, 2, 0].astype(jnp.float32)
    pl.semaphore_wait(barrier, 3 * bands - 1)

    def wind_copy(way, s, block):
        return pltpu.make_async_remote_copy(
            src_ref=wind.at[block],
            dst_ref=wind.at[block],
            send_sem=wind_send.at[way, s],
            recv_sem=wind_recv.at[way, s],
            device_id={"band": band + (1 if way == 0 else -1)},
            device_id_type=MESH,
        )

    def edge_t_copy(s):
        return pltpu.make_async_remote_copy(
            src_ref=edge_t.at[band],
            dst_ref=edge_t.at[band],
            send_sem=edge_t_send.at[s - 1],
            recv_sem=edge_t_recv.at[s - 1],
            device_id={"band": lax.rem(band + s, bands)},
            device_id_type=MESH,
        )

    def edge_p_copy(way, b):
        return pltpu.make_async_remote_copy(
            src_ref=edge_p.at[2 + way, band],
            dst_ref=edge_p.at[way, band],
            send_sem=edge_p_send.at[way, b],
            recv_sem=edge_p_recv.at[way, band],
            device_id={"phi": right if way == 0 else left, "band": b},
            device_id_type=MESH,
        )

    @pl.when(band < bands - 1)
    def _():
        wind_copy(0, 0, band).start()

    @pl.when(band > 0)
    def _():
        wind_copy(1, 0, band).start()

    for s in range(1, bands):
        edge_t_copy(s).start()
    for b in range(bands):
        for way in range(2):
            edge_p_copy(way, b).start()

    def phi_copy(stage, way, block):
        part = pl.ds(pl.multiple_of(block * rows, rows), rows)
        sems = (next_send, next_recv)
        return pltpu.make_async_remote_copy(
            src_ref=send_phi.at[stage, way, :, part],
            dst_ref=recv_phi.at[stage, way, :, part],
            send_sem=sems[0].at[way, block],
            recv_sem=sems[1].at[way, block],
            device_id={"phi": right if way == 0 else left},
            device_id_type=MESH,
        )

    def bin_copy(stage, way, block):
        part = pl.ds(pl.multiple_of(block * rows, rows), rows)
        return pltpu.make_async_remote_copy(
            src_ref=send_bin.at[stage, way, :, part],
            dst_ref=recv_bin.at[stage, way, :, part],
            send_sem=next_send.at[2 + way, block],
            recv_sem=next_recv.at[2 + way, block],
            device_id={"band": band + (1 if way == 0 else -1)},
            device_id_type=MESH,
        )

    def whole_phi(way):
        return pltpu.make_async_remote_copy(
            src_ref=send_phi.at[0, way],
            dst_ref=recv_phi.at[0, way],
            send_sem=halo_send.at[way],
            recv_sem=halo_recv.at[way],
            device_id={"phi": right if way == 0 else left},
            device_id_type=MESH,
        )

    def whole_bin(way):
        return pltpu.make_async_remote_copy(
            src_ref=send_bin.at[0, way],
            dst_ref=recv_bin.at[0, way],
            send_sem=halo_send.at[2 + way],
            recv_sem=halo_recv.at[2 + way],
            device_id={"band": band + (1 if way == 0 else -1)},
            device_id_type=MESH,
        )

    def has(way):
        return band < bands - 1 if way == 0 else band > 0

    def comes(way):
        return band > 0 if way == 0 else band < bands - 1

    def stage_out(stage, source, start, count):
        own = pl.ds(start, count)
        inner = pl.ds(PAD + start, count)

        def phi_part(k, _):
            send_phi[stage, 0, k, own] = source[k + 1, azim, inner].astype(jnp.bfloat16)
            send_phi[stage, 1, k, own] = source[k + 1, 1, inner].astype(jnp.bfloat16)
            return 0

        def bin_part(p, _):
            send_bin[stage, 0, p, own] = source[bins, p + 1, inner].astype(jnp.bfloat16)
            send_bin[stage, 1, p, own] = source[1, p + 1, inner].astype(jnp.bfloat16)
            return 0

        lax.fori_loop(0, bins, phi_part, 0)
        lax.fori_loop(0, azim, bin_part, 0)

    def stage_in(stage, target):
        inner = pl.ds(PAD, colat)

        def phi_part(k, _):
            target[k + 1, 0, inner] = recv_phi[stage, 0, k].astype(jnp.float32)
            target[k + 1, azim + 1, inner] = recv_phi[stage, 1, k].astype(jnp.float32)
            return 0

        lax.fori_loop(0, bins, phi_part, 0)
        for way, ghost, edge in ((0, 0, 1), (1, bins + 1, bins)):

            @pl.when(comes(way))
            def _(way=way, ghost=ghost):
                def bin_part(p, _):
                    target[ghost, p + 1, inner] = recv_bin[stage, way, p].astype(jnp.float32)
                    return 0

                lax.fori_loop(0, azim, bin_part, 0)

            @pl.when(jnp.logical_not(comes(way)))
            def _(ghost=ghost, edge=edge):
                def bin_part(p, _):
                    target[ghost, p + 1, inner] = target[edge, p + 1, inner]
                    return 0

                lax.fori_loop(0, azim, bin_part, 0)

    def pad_colat(target):
        def part(p, _):
            for k in range(bins):
                target[k + 1, p + 1, PAD - 1 : PAD] = target[k + 1, p + 1, PAD : PAD + 1]
                target[k + 1, p + 1, PAD + colat : PAD + colat + 1] = target[
                    k + 1, p + 1, PAD + colat - 1 : PAD + colat
                ]
            return 0

        lax.fori_loop(0, azim, part, 0)

    load.wait()
    stage_out(0, cells, 0, colat)
    for way in range(2):

        @pl.when(has(way))
        def _(way=way):
            whole_bin(way).start()

        whole_phi(way).start()
    pad_colat(cells)

    lane = lax.broadcasted_iota(jnp.int32, (rows, shells), 1)
    row = lax.broadcasted_iota(jnp.int32, (rows, shells), 0)
    tau = tau_ref[0]
    inv_r = jnp.broadcast_to(inv_r_ref[0:1, :], (rows, shells))
    inv_hr = inv_r * (1.0 / step_r)
    inv_ht = inv_r * (1.0 / step_t)

    def make_coefs(block):
        start = pl.multiple_of(block * rows, rows)
        part = pl.ds(start, rows)
        inv_hp = inv_r * inv_sin_ref[part, :] * (1.0 / step_p)
        cot_r = inv_r * cot_ref[part, :]
        below = jnp.maximum(block - 1, 0)
        above = jnp.minimum(block + 1, bands - 1)

        def one(p, _):
            u_r, u_t, u_p, b_r, b_t, b_p = [
                wind[block, c, p].astype(jnp.float32) for c in range(6)
            ]
            r_hi = jnp.where(lane == shells - 1, u_r, pltpu.roll(u_r, shells - 1, 1))
            r_lo = jnp.where(lane == 0, u_r, pltpu.roll(u_r, 1, 1))
            t_hi_row = jnp.where(
                block == bands - 1, u_t[rows - 1 : rows], edge_t[above, 0, pl.ds(p, 1), :]
            )
            t_lo_row = jnp.where(block == 0, u_t[0:1], edge_t[below, 1, pl.ds(p, 1), :])
            t_hi = jnp.where(row == rows - 1, t_hi_row, pltpu.roll(u_t, rows - 1, 0))
            t_lo = jnp.where(row == 0, t_lo_row, pltpu.roll(u_t, 1, 0))
            p_hi = jnp.where(
                p == azim - 1,
                edge_p[1, block],
                wind[block, 2, jnp.minimum(p + 1, azim - 1)].astype(jnp.float32),
            )
            p_lo = jnp.where(
                p == 0,
                edge_p[0, block],
                wind[block, 2, jnp.maximum(p - 1, 0)].astype(jnp.float32),
            )
            spread = (
                (r_hi - r_lo) * (0.5 * inv_hr)
                + 2.0 * u_r * inv_r
                + (t_hi - t_lo) * (0.5 * inv_ht)
                + cot_r * u_t
                + (p_hi - p_lo) * (0.5 * inv_hp)
            )
            spread = spread.astype(jnp.bfloat16).astype(jnp.float32)
            share = (1.0 - K_RATIO) / (b_r * b_r + b_t * b_t + b_p * b_p + B_FLOOR)
            c_r = tau * (K_RATIO + share * b_r * b_r) * inv_hr * inv_hr
            c_t = tau * (K_RATIO + share * b_t * b_t) * inv_ht * inv_ht
            c_p = tau * (K_RATIO + share * b_p * b_p) * inv_hp * inv_hp
            c_rp = jnp.where(lane == shells - 1, 0.0, c_r)
            c_rm = jnp.where(lane == 0, 0.0, c_r)
            a_r = tau * u_r * inv_hr
            a_r = jnp.where((lane == 0) & (a_r > 0.0), 0.0, a_r)
            a_r = jnp.where((lane == shells - 1) & (a_r < 0.0), 0.0, a_r)
            a_t = tau * u_t * inv_ht
            a_p = tau * u_p * inv_hp
            mu = tau * spread * (1.0 / (3.0 * step_m))
            c_sum = c_rp + c_rm + 2.0 * c_t + 2.0 * c_p
            a_sum = 1.0 - (jnp.abs(a_r) + jnp.abs(a_t) + jnp.abs(a_p) + jnp.abs(mu))
            for n, value in enumerate(
                (c_rp, c_rm, c_t, c_p, a_r, a_t, a_p, mu, c_sum, a_sum)
            ):
                coefs[n, p, part] = value
            return 0

        lax.fori_loop(0, azim, one, 0)

    def apply(source, p, start, finish):
        part = pl.ds(start, 8)
        mid = pl.ds(PAD + start, 8)
        low = pl.ds(PAD + start - 1, 8)
        high = pl.ds(PAD + start + 1, 8)
        c_rp, c_rm, c_t, c_p, a_r, a_t, a_p, mu, c_sum, a_sum = [
            coefs[n, p, part] for n in range(10)
        ]
        w_r, w_t, w_p, w_m = jnp.abs(a_r), jnp.abs(a_t), jnp.abs(a_p), jnp.abs(mu)
        out_r, out_t, out_p, up_m = a_r > 0.0, a_t > 0.0, a_p > 0.0, mu > 0.0
        before = source[0, p + 1, mid]
        here = source[1, p + 1, mid]
        for k in range(bins):
            after = source[k + 2, p + 1, mid]
            kappa = kappa_ref[band * bins + k]
            r_hi = pltpu.roll(here, shells - 1, 1)
            r_lo = pltpu.roll(here, 1, 1)
            t_hi = source[k + 1, p + 1, high]
            t_lo = source[k + 1, p + 1, low]
            p_hi = source[k + 1, p + 2, mid]
            p_lo = source[k + 1, p, mid]
            curve = (
                (c_rp * r_hi + c_rm * r_lo)
                + (c_t * (t_hi + t_lo) + c_p * (p_hi + p_lo))
                - c_sum * here
            )
            flow = (
                (w_r * jnp.where(out_r, r_lo, r_hi) + w_t * jnp.where(out_t, t_lo, t_hi))
                + (w_p * jnp.where(out_p, p_lo, p_hi) + w_m * jnp.where(up_m, after, before))
                + a_sum * here
            )
            finish(k, p, mid, kappa * curve + flow)
            before, here = here, after

    def finish_first(k, p, mid, value):
        firsts[k + 1, p + 1, mid] = value

    def finish_second(k, p, mid, value):
        cells[k + 1, p + 1, mid] = 1.5 * value - 0.5 * cells[k + 1, p + 1, mid]

    for s in range(1, bands):
        edge_t_copy(s).wait()
    for b in range(bands):
        for way in range(2):
            edge_p_copy(way, b).wait_send()
            pltpu.make_async_remote_copy(
                src_ref=edge_p.at[2 + way, b],
                dst_ref=edge_p.at[way, b],
                send_sem=edge_p_send.at[way, b],
                recv_sem=edge_p_recv.at[way, b],
                device_id={"phi": right if way == 0 else left, "band": b},
                device_id_type=MESH,
            ).wait_recv()
    make_coefs(band)
    for way in range(2):

        @pl.when(has(way))
        def _(way=way):
            whole_bin(way).wait_send()

        @pl.when(comes(way))
        def _(way=way):
            whole_bin(way).wait_recv()

        whole_phi(way).wait()
    stage_in(0, cells)

    def visit(i, _):
        s = (i + 1) // 2
        below = lax.rem(i, 2) == 1
        block = jnp.where(below, band - s, band + s)
        valid = (block >= 0) & (block < bands)

        @pl.when(valid & below)
        def _():
            wind_copy(0, s - 1, block).wait_recv()

            @pl.when(band < bands - 1)
            def _():
                wind_copy(0, s, block).start()

        @pl.when(valid & jnp.logical_not(below) & (s > 0))
        def _():
            wind_copy(1, s - 1, block).wait_recv()

            @pl.when(band > 0)
            def _():
                wind_copy(1, s, block).start()

        @pl.when(valid)
        def _():
            @pl.when(s > 0)
            def _():
                make_coefs(block)

            start = pl.multiple_of(block * rows, rows)

            def one(p, _):
                for part in range(rows // 8):
                    apply(cells, p, start + 8 * part, finish_first)
                return 0

            lax.fori_loop(0, azim, one, 0)
            stage_out(1, firsts, start, rows)
            for way in range(2):

                @pl.when(has(way))
                def _(way=way):
                    bin_copy(1, way, block).start()

                phi_copy(1, way, block).start()

        return 0

    lax.fori_loop(0, 2 * bands - 1, visit, 0)
    pad_colat(firsts)
    for block in range(bands):
        for way in range(2):

            @pl.when(has(way))
            def _(way=way, block=block):
                bin_copy(1, way, block).wait_send()

            @pl.when(comes(way))
            def _(way=way, block=block):
                bin_copy(1, way, block).wait_recv()

            phi_copy(1, way, block).wait()
    stage_in(1, firsts)

    def store(p):
        return pltpu.make_async_copy(
            cells.at[1 : bins + 1, p + 1, PAD : PAD + colat], out_hbm.at[:, p], store_sem.at[p]
        )

    def second(p, _):
        def one(j, _):
            apply(firsts, p, pl.multiple_of(j * 8, 8), finish_second)
            return 0

        lax.fori_loop(0, colat // 8, one, 0)
        store(p).start()
        return 0

    lax.fori_loop(0, azim, second, 0)

    def stored(p, _):
        store(p).wait()
        return 0

    lax.fori_loop(0, azim, stored, 0)
    for s in range(bands - 1):

        @pl.when((band - s >= 0) & (band < bands - 1))
        def _(s=s):
            wind_copy(0, s, band - s).wait_send()

        @pl.when((band + s < bands) & (band > 0))
        def _(s=s):
            wind_copy(1, s, band + s).wait_send()


def cosmic_ray_step(velocity, mag, density, kappa, tau, bands, phis, spacing):
    bins, azim, colat, shells = density.shape
    radial = velocity.shape[3]
    rows = colat // bands
    radius = INNER_RADIUS * np.exp(
        math.log(R_RATIO) / radial * (np.arange(shells) + radial - shells + 0.5)
    )
    theta = COLAT_LOW + COLAT_SPAN * (np.arange(colat) + 0.5) / colat
    wide = np.ones((colat, shells))
    inv_r = jnp.asarray(np.broadcast_to(1.0 / radius, (8, shells)), jnp.float32)
    inv_sin = jnp.asarray(wide / np.sin(theta)[:, None], jnp.float32)
    cot = jnp.asarray(wide * (np.cos(theta) / np.sin(theta))[:, None], jnp.float32)
    dma = pltpu.SemaphoreType.DMA
    vmem = pl.BlockSpec(memory_space=pltpu.VMEM)
    smem = pl.BlockSpec(memory_space=pltpu.SMEM)
    hbm = pl.BlockSpec(memory_space=pl.ANY)
    padded_shape = (bins + 2, azim + 2, colat + 2 * PAD, shells)
    return pl.pallas_call(
        functools.partial(cosmic_ray_kernel, bands, phis, spacing),
        out_shape=jax.ShapeDtypeStruct(density.shape, jnp.float32),
        in_specs=[smem, smem, vmem, vmem, vmem, vmem, vmem, hbm],
        out_specs=hbm,
        scratch_shapes=[
            pltpu.VMEM(padded_shape, jnp.float32),
            pltpu.VMEM(padded_shape, jnp.float32),
            pltpu.VMEM((10, azim, colat, shells), jnp.float32),
            pltpu.VMEM((bands, 6, azim, rows, shells), jnp.bfloat16),
            pltpu.VMEM((bands, 2, azim, shells), jnp.float32),
            pltpu.VMEM((4, bands, rows, shells), jnp.float32),
            pltpu.VMEM((2, 2, bins, colat, shells), jnp.bfloat16),
            pltpu.VMEM((2, 2, azim, colat, shells), jnp.bfloat16),
            pltpu.VMEM((2, 2, bins, colat, shells), jnp.bfloat16),
            pltpu.VMEM((2, 2, azim, colat, shells), jnp.bfloat16),
            dma,
            dma((azim,)),
            dma((2, bands)),
            dma((2, bands)),
            dma((bands,)),
            dma((bands,)),
            dma((2, bands)),
            dma((2, bands)),
            dma((4,)),
            dma((4,)),
            dma((4, bands)),
            dma((4, bands)),
        ],
        compiler_params=pltpu.CompilerParams(
            collective_id=0, has_side_effects=True, vmem_limit_bytes=56 * 1024 * 1024
        ),
        cost_estimate=pl.CostEstimate(
            flops=80 * density.size, bytes_accessed=8 * density.size, transcendentals=0
        ),
        name="cosmic_ray",
    )(kappa, tau, velocity, mag, inv_r, inv_sin, cot, density)


def body(
    density,
    velocity,
    magnetic_vector,
    pressure,
    fluid_courant_number,
    cosmic_ray_density,
    diffusion_per_bin,
    super_step_scale,
):
    azim_dev = density.shape[0]
    colat_dev = density.shape[1]
    radial_cell_count = density.shape[2]
    band_count = lax.axis_size("band")
    phi_count = lax.axis_size("phi")
    colatitude_count = colat_dev * band_count
    azimuth_cell_count = azim_dev * phi_count
    bin_dev = cosmic_ray_density.shape[0]
    momentum_bin_count = bin_dev * band_count
    outer_shell_count = cosmic_ray_density.shape[3]
    band_pos = lax.axis_index("band")
    mesh_spacing = grid_steps(
        radial_cell_count, colatitude_count, azimuth_cell_count, momentum_bin_count
    )
    fluid_rate, cosmic_ray_rate = rate_limits(
        radial_cell_count,
        outer_shell_count,
        colatitude_count,
        azimuth_cell_count,
        momentum_bin_count,
    )
    primitive = jnp.concatenate([density[None], velocity, magnetic_vector, pressure[None]], axis=0)
    padded_array = padded(primitive, (("phi", 1), ("band", 2)), 1)
    padded_array = edge_fix(padded_array, 2, 1, band_pos, band_count)
    radius_full = shell_radii(0, radial_cell_count, radial_cell_count)
    colatitude_local = colatitudes(band_pos * colat_dev, colat_dev, colatitude_count)
    fluid_state = fluid_update(
        padded_array, radius_full, colatitude_local, fluid_courant_number / fluid_rate, mesh_spacing
    )
    cosmic_ray_next = cosmic_ray_step(
        velocity,
        magnetic_vector,
        cosmic_ray_density,
        diffusion_per_bin,
        (super_step_scale / (3.0 * cosmic_ray_rate)).reshape(1),
        band_count,
        phi_count,
        mesh_spacing,
    )
    return (fluid_state, cosmic_ray_next)


def solution(mesh):
    placed = (
        P("phi", "band", None),
        P(None, "phi", "band", None),
        P(None, "phi", "band", None),
        P("phi", "band", None),
        P(),
        P("band", "phi", None, None),
        P(),
        P(),
    )
    return jax.shard_map(
        body,
        mesh=mesh,
        in_specs=placed,
        out_specs=(P(None, "phi", "band", None), P("band", "phi", None, None)),
        check_vma=False,
    )
```

```python
import functools
import math

import jax
import jax.numpy as jnp
import numpy as np
from jax import lax
from jax.experimental import pallas as pl
from jax.experimental.pallas import tpu as pltpu
from jax.sharding import PartitionSpec as P

ADIABATIC = 5.0 / 3.0
INNER_RADIUS = 0.1
R_RATIO = 30.0
COLAT_LOW = math.pi / 6.0
COLAT_SPAN = 2.0 * math.pi / 3.0
P_RATIO = 1000.0
K_RATIO = 0.1
B_FLOOR = 0.1
V_BOUND = 3.0
B_BOUND = 3.0
P_HIGH = 2.0
RHO_LOW = 0.5
KAPPA_HIGH = 0.5


def grid_steps(n_radial, n_colat, n_azim, n_bins):
    return (
        math.log(R_RATIO) / n_radial,
        COLAT_SPAN / n_colat,
        2.0 * math.pi / n_azim,
        math.log(P_RATIO) / n_bins,
    )


def rate_limits(n_radial, n_shells, n_colat, n_azim, n_bins):
    radial_spacing, colatitude_spacing, azimuth_spacing, step_m = grid_steps(
        n_radial, n_colat, n_azim, n_bins
    )
    sine_lower = math.sin(COLAT_LOW + 0.5 * colatitude_spacing)
    fluid_radius = INNER_RADIUS * math.exp(0.5 * radial_spacing)
    fastest_limit = V_BOUND + math.sqrt((ADIABATIC * P_HIGH + 3.0 * B_BOUND**2) / RHO_LOW)
    fluid_rate = fastest_limit * (
        1.0 / (fluid_radius * radial_spacing)
        + 1.0 / (fluid_radius * colatitude_spacing)
        + 1.0 / (fluid_radius * sine_lower * azimuth_spacing)
    )
    shell_low = INNER_RADIUS * math.exp(radial_spacing * (n_radial - n_shells + 0.5))
    inv_r = 1.0 / (shell_low * radial_spacing)
    inv_t = 1.0 / (shell_low * colatitude_spacing)
    inv_p = 1.0 / (shell_low * sine_lower * azimuth_spacing)
    cosmic_ray_rate = (
        2.0 * KAPPA_HIGH * (inv_r**2 + inv_t**2 + inv_p**2)
        + V_BOUND * (inv_r + inv_t + inv_p)
        + V_BOUND * (inv_r + inv_t + inv_p + 4.0 / shell_low) / (3.0 * step_m)
    )
    return (fluid_rate, cosmic_ray_rate)


def fluid_cells(prim, normal):
    rho, v, b, pres = prim[0], prim[1:4], prim[4:7], prim[7]
    v_n, b_n = v[normal], b[normal]
    b_sq = b[0] * b[0] + b[1] * b[1] + b[2] * b[2]
    v_sq = v[0] * v[0] + v[1] * v[1] + v[2] * v[2]
    energy = pres * (1.0 / (ADIABATIC - 1.0)) + 0.5 * rho * v_sq + 0.5 * b_sq
    total_p = pres + 0.5 * b_sq
    mom = [rho * v[k] for k in range(3)]
    state = [rho] + mom + list(b) + [energy]
    push = [mom[k] * v_n - b[k] * b_n for k in range(3)]
    push[normal] = push[normal] + total_p
    turn = [v_n * b[k] - b_n * v[k] for k in range(3)]
    work = (energy + total_p) * v_n - b_n * (v[0] * b[0] + v[1] * b[1] + v[2] * b[2])
    speed = jnp.abs(v_n) + jnp.sqrt((ADIABATIC * pres + b_sq) / rho)
    return state, [mom[normal]] + push + turn + [work], speed


def face_flux(low, high):
    wave = jnp.maximum(low[2], high[2])
    return [
        0.5 * ((low[1][n] + high[1][n]) - wave * (high[0][n] - low[0][n])) for n in range(8)
    ]


MESH = pl.DeviceIdType.MESH
PAD = 8


def cosmic_ray_kernel(
    bands,
    phis,
    spacing,
    kappa_ref,
    tau_ref,
    dt_ref,
    rho_ref,
    vel_ref,
    mag_ref,
    pres_ref,
    inv_r_ref,
    inv_sin_ref,
    cot_ref,
    f_hbm,
    out_hbm,
    fluid_hbm,
    cells,
    firsts,
    coefs,
    wind,
    edge_t,
    edge_p,
    send_phi,
    send_bin,
    recv_phi,
    recv_bin,
    prims,
    fluid,
    edge_f,
    send_f,
    recv_f,
    fluid_sem,
    fluid_send,
    fluid_recv,
    load_sem,
    store_sem,
    wind_send,
    wind_recv,
    edge_t_send,
    edge_t_recv,
    edge_p_send,
    edge_p_recv,
    halo_send,
    halo_recv,
    next_send,
    next_recv,
):
    bins = f_hbm.shape[0]
    azim = f_hbm.shape[1]
    colat = f_hbm.shape[2]
    shells = f_hbm.shape[3]
    rows = colat // bands
    first_shell = vel_ref.shape[3] - shells
    step_r, step_t, step_p, step_m = spacing
    band = lax.axis_index("band")
    phi = lax.axis_index("phi")
    right = lax.rem(phi + 1, phis)
    left = lax.rem(phi + phis - 1, phis)

    load = pltpu.make_async_copy(
        f_hbm, cells.at[1 : bins + 1, 1 : azim + 1, PAD : PAD + colat], load_sem
    )
    load.start()

    barrier = pltpu.get_barrier_semaphore()
    for b in range(bands):
        for side in (left, right):
            pl.semaphore_signal(
                barrier, inc=1, device_id={"phi": side, "band": b}, device_id_type=MESH
            )
    for s in range(1, bands):
        pl.semaphore_signal(
            barrier,
            inc=1,
            device_id={"band": lax.rem(band + s, bands)},
            device_id_type=MESH,
        )

    own_rows = pl.ds(PAD, rows)

    def take(p, _):
        for c in range(3):
            wind[band, c, p] = vel_ref[c, p, :, first_shell:].astype(jnp.bfloat16)
            wind[band, 3 + c, p] = mag_ref[c, p, :, first_shell:].astype(jnp.bfloat16)
            prims[1 + c, p + 1, own_rows] = vel_ref[c, p]
            prims[4 + c, p + 1, own_rows] = mag_ref[c, p]
        prims[0, p + 1, own_rows] = rho_ref[p]
        prims[7, p + 1, own_rows] = pres_ref[p]
        for n in range(8):
            edge_f[0, n, p] = prims[n, p + 1, PAD + rows - 1 : PAD + rows]
            edge_f[1, n, p] = prims[n, p + 1, PAD : PAD + 1]
        u_t = wind[band, 1, p].astype(jnp.float32)
        edge_t[band, 0, pl.ds(p, 1), :] = u_t[0:1]
        edge_t[band, 1, pl.ds(p, 1), :] = u_t[rows - 1 : rows]
        return 0

    lax.fori_loop(0, azim, take, 0)
    edge_p[2, band] = wind[band, 2, azim - 1].astype(jnp.float32)
    edge_p[3, band] = wind[band, 2, 0].astype(jnp.float32)
    for n in range(8):
        send_f[0, n] = prims[n, azim, own_rows].astype(jnp.bfloat16)
        send_f[1, n] = prims[n, 1, own_rows].astype(jnp.bfloat16)
        for way in range(2):
            send_f[2 + way, n] = edge_f[way, n].reshape(azim, -1).astype(jnp.bfloat16)
    pl.semaphore_wait(barrier, 3 * bands - 1)

    def fluid_copy(way):
        if way < 2:
            target = {"phi": right if way == 0 else left}
        else:
            target = {"band": band + (1 if way == 2 else -1)}
        return pltpu.make_async_remote_copy(
            src_ref=send_f.at[way],
            dst_ref=recv_f.at[way],
            send_sem=fluid_send.at[way],
            recv_sem=fluid_recv.at[way],
            device_id=target,
            device_id_type=MESH,
        )

    def has(way):
        return band < bands - 1 if way == 0 else band > 0

    def comes(way):
        return band > 0 if way == 0 else band < bands - 1

    def wind_copy(way, s, block):
        return pltpu.make_async_remote_copy(
            src_ref=wind.at[block],
            dst_ref=wind.at[block],
            send_sem=wind_send.at[way, s],
            recv_sem=wind_recv.at[way, s],
            device_id={"band": band + (1 if way == 0 else -1)},
            device_id_type=MESH,
        )

    def edge_t_copy(s):
        return pltpu.make_async_remote_copy(
            src_ref=edge_t.at[band],
            dst_ref=edge_t.at[band],
            send_sem=edge_t_send.at[s - 1],
            recv_sem=edge_t_recv.at[s - 1],
            device_id={"band": lax.rem(band + s, bands)},
            device_id_type=MESH,
        )

    def edge_p_copy(way, b):
        return pltpu.make_async_remote_copy(
            src_ref=edge_p.at[2 + way, band],
            dst_ref=edge_p.at[way, band],
            send_sem=edge_p_send.at[way, b],
            recv_sem=edge_p_recv.at[way, band],
            device_id={"phi": right if way == 0 else left, "band": b},
            device_id_type=MESH,
        )

    @pl.when(band < bands - 1)
    def _():
        wind_copy(0, 0, band).start()

    @pl.when(band > 0)
    def _():
        wind_copy(1, 0, band).start()

    for way in range(2):

        @pl.when(has(way))
        def _(way=way):
            fluid_copy(2 + way).start()

        fluid_copy(way).start()
    for s in range(1, bands):
        edge_t_copy(s).start()
    for b in range(bands):
        for way in range(2):
            edge_p_copy(way, b).start()

    def phi_copy(stage, way, block):
        part = pl.ds(pl.multiple_of(block * rows, rows), rows)
        sems = (next_send, next_recv)
        return pltpu.make_async_remote_copy(
            src_ref=send_phi.at[stage, way, :, part],
            dst_ref=recv_phi.at[stage, way, :, part],
            send_sem=sems[0].at[way, block],
            recv_sem=sems[1].at[way, block],
            device_id={"phi": right if way == 0 else left},
            device_id_type=MESH,
        )

    def bin_copy(stage, way, block):
        part = pl.ds(pl.multiple_of(block * rows, rows), rows)
        return pltpu.make_async_remote_copy(
            src_ref=send_bin.at[stage, way, :, part],
            dst_ref=recv_bin.at[stage, way, :, part],
            send_sem=next_send.at[2 + way, block],
            recv_sem=next_recv.at[2 + way, block],
            device_id={"band": band + (1 if way == 0 else -1)},
            device_id_type=MESH,
        )

    def whole_phi(way):
        return pltpu.make_async_remote_copy(
            src_ref=send_phi.at[0, way],
            dst_ref=recv_phi.at[0, way],
            send_sem=halo_send.at[way],
            recv_sem=halo_recv.at[way],
            device_id={"phi": right if way == 0 else left},
            device_id_type=MESH,
        )

    def whole_bin(way):
        return pltpu.make_async_remote_copy(
            src_ref=send_bin.at[0, way],
            dst_ref=recv_bin.at[0, way],
            send_sem=halo_send.at[2 + way],
            recv_sem=halo_recv.at[2 + way],
            device_id={"band": band + (1 if way == 0 else -1)},
            device_id_type=MESH,
        )

    def stage_out(stage, source, start, count):
        own = pl.ds(start, count)
        inner = pl.ds(PAD + start, count)

        def phi_part(k, _):
            send_phi[stage, 0, k, own] = source[k + 1, azim, inner].astype(jnp.bfloat16)
            send_phi[stage, 1, k, own] = source[k + 1, 1, inner].astype(jnp.bfloat16)
            return 0

        def bin_part(p, _):
            send_bin[stage, 0, p, own] = source[bins, p + 1, inner].astype(jnp.bfloat16)
            send_bin[stage, 1, p, own] = source[1, p + 1, inner].astype(jnp.bfloat16)
            return 0

        lax.fori_loop(0, bins, phi_part, 0)
        lax.fori_loop(0, azim, bin_part, 0)

    def stage_in_phi(stage, target, start, count):
        own = pl.ds(start, count)
        inner = pl.ds(PAD + start, count)

        def phi_part(k, _):
            target[k + 1, 0, inner] = recv_phi[stage, 0, k, own].astype(jnp.float32)
            target[k + 1, azim + 1, inner] = recv_phi[stage, 1, k, own].astype(jnp.float32)
            return 0

        lax.fori_loop(0, bins, phi_part, 0)

    def stage_in_bin(stage, target):
        inner = pl.ds(PAD, colat)
        for way, ghost, edge in ((0, 0, 1), (1, bins + 1, bins)):

            @pl.when(comes(way))
            def _(way=way, ghost=ghost):
                def bin_part(p, _):
                    target[ghost, p + 1, inner] = recv_bin[stage, way, p].astype(jnp.float32)
                    return 0

                lax.fori_loop(0, azim, bin_part, 0)

            @pl.when(jnp.logical_not(comes(way)))
            def _(ghost=ghost, edge=edge):
                def bin_part(p, _):
                    target[ghost, p + 1, inner] = target[edge, p + 1, inner]
                    return 0

                lax.fori_loop(0, azim, bin_part, 0)

    def pad_colat(target):
        def part(p, _):
            for k in range(bins):
                target[k + 1, p + 1, PAD - 1 : PAD] = target[k + 1, p + 1, PAD : PAD + 1]
                target[k + 1, p + 1, PAD + colat : PAD + colat + 1] = target[
                    k + 1, p + 1, PAD + colat - 1 : PAD + colat
                ]
            return 0

        lax.fori_loop(0, azim, part, 0)

    load.wait()
    stage_out(0, cells, 0, colat)
    for way in range(2):

        @pl.when(has(way))
        def _(way=way):
            whole_bin(way).start()

        whole_phi(way).start()
    pad_colat(cells)

    lane = lax.broadcasted_iota(jnp.int32, (rows, shells), 1)
    row = lax.broadcasted_iota(jnp.int32, (rows, shells), 0)
    tau = tau_ref[0]
    inv_r = jnp.broadcast_to(inv_r_ref[0:1, first_shell:], (rows, shells))
    inv_hr = inv_r * (1.0 / step_r)
    inv_ht = inv_r * (1.0 / step_t)

    def make_coefs(block):
        start = pl.multiple_of(block * rows, rows)
        part = pl.ds(start, rows)
        inv_hp = inv_r * inv_sin_ref[part, :shells] * (1.0 / step_p)
        cot_r = inv_r * cot_ref[part, :shells]
        below = jnp.maximum(block - 1, 0)
        above = jnp.minimum(block + 1, bands - 1)

        def one(p, _):
            u_r, u_t, u_p, b_r, b_t, b_p = [
                wind[block, c, p].astype(jnp.float32) for c in range(6)
            ]
            r_hi = jnp.where(lane == shells - 1, u_r, pltpu.roll(u_r, shells - 1, 1))
            r_lo = jnp.where(lane == 0, u_r, pltpu.roll(u_r, 1, 1))
            t_hi_row = jnp.where(
                block == bands - 1, u_t[rows - 1 : rows], edge_t[above, 0, pl.ds(p, 1), :]
            )
            t_lo_row = jnp.where(block == 0, u_t[0:1], edge_t[below, 1, pl.ds(p, 1), :])
            t_hi = jnp.where(row == rows - 1, t_hi_row, pltpu.roll(u_t, rows - 1, 0))
            t_lo = jnp.where(row == 0, t_lo_row, pltpu.roll(u_t, 1, 0))
            p_hi = jnp.where(
                p == azim - 1,
                edge_p[1, block],
                wind[block, 2, jnp.minimum(p + 1, azim - 1)].astype(jnp.float32),
            )
            p_lo = jnp.where(
                p == 0,
                edge_p[0, block],
                wind[block, 2, jnp.maximum(p - 1, 0)].astype(jnp.float32),
            )
            spread = (
                (r_hi - r_lo) * (0.5 * inv_hr)
                + 2.0 * u_r * inv_r
                + (t_hi - t_lo) * (0.5 * inv_ht)
                + cot_r * u_t
                + (p_hi - p_lo) * (0.5 * inv_hp)
            )
            spread = spread.astype(jnp.bfloat16).astype(jnp.float32)
            share = (1.0 - K_RATIO) / (b_r * b_r + b_t * b_t + b_p * b_p + B_FLOOR)
            c_r = tau * (K_RATIO + share * b_r * b_r) * inv_hr * inv_hr
            c_t = tau * (K_RATIO + share * b_t * b_t) * inv_ht * inv_ht
            c_p = tau * (K_RATIO + share * b_p * b_p) * inv_hp * inv_hp
            c_rp = jnp.where(lane == shells - 1, 0.0, c_r)
            c_rm = jnp.where(lane == 0, 0.0, c_r)
            a_r = tau * u_r * inv_hr
            a_r = jnp.where((lane == 0) & (a_r > 0.0), 0.0, a_r)
            a_r = jnp.where((lane == shells - 1) & (a_r < 0.0), 0.0, a_r)
            a_t = tau * u_t * inv_ht
            a_p = tau * u_p * inv_hp
            mu = tau * spread * (1.0 / (3.0 * step_m))
            c_sum = c_rp + c_rm + 2.0 * c_t + 2.0 * c_p
            a_sum = 1.0 - (jnp.abs(a_r) + jnp.abs(a_t) + jnp.abs(a_p) + jnp.abs(mu))
            for n, value in enumerate(
                (c_rp, c_rm, c_t, c_p, a_r, a_t, a_p, mu, c_sum, a_sum)
            ):
                coefs[n, p, part] = value
            return 0

        lax.fori_loop(0, azim, one, 0)

    def apply(source, p, start, finish, low_bin, high_bin):
        part = pl.ds(start, 8)
        mid = pl.ds(PAD + start, 8)
        low = pl.ds(PAD + start - 1, 8)
        high = pl.ds(PAD + start + 1, 8)
        c_rp, c_rm, c_t, c_p, a_r, a_t, a_p, mu, c_sum, a_sum = [
            coefs[n, p, part] for n in range(10)
        ]
        w_r, w_t, w_p, w_m = jnp.abs(a_r), jnp.abs(a_t), jnp.abs(a_p), jnp.abs(mu)
        out_r, out_t, out_p, up_m = a_r > 0.0, a_t > 0.0, a_p > 0.0, mu > 0.0
        before = source[low_bin, p + 1, mid]
        here = source[low_bin + 1, p + 1, mid]
        for k in range(low_bin, high_bin):
            after = source[k + 2, p + 1, mid]
            kappa = kappa_ref[band * bins + k]
            r_hi = pltpu.roll(here, shells - 1, 1)
            r_lo = pltpu.roll(here, 1, 1)
            t_hi = source[k + 1, p + 1, high]
            t_lo = source[k + 1, p + 1, low]
            p_hi = source[k + 1, p + 2, mid]
            p_lo = source[k + 1, p, mid]
            curve = (
                (c_rp * r_hi + c_rm * r_lo)
                + (c_t * (t_hi + t_lo) + c_p * (p_hi + p_lo))
                - c_sum * here
            )
            flow = (
                (w_r * jnp.where(out_r, r_lo, r_hi) + w_t * jnp.where(out_t, t_lo, t_hi))
                + (w_p * jnp.where(out_p, p_lo, p_hi) + w_m * jnp.where(up_m, after, before))
                + a_sum * here
            )
            finish(k, p, mid, kappa * curve + flow)
            before, here = here, after

    def finish_first(k, p, mid, value):
        firsts[k + 1, p + 1, mid] = value

    def finish_second(k, p, mid, value):
        cells[k + 1, p + 1, mid] = 1.5 * value - 0.5 * cells[k + 1, p + 1, mid]

    def fluid_in():
        for n in range(8):
            prims[n, 0, own_rows] = recv_f[0, n].astype(jnp.float32)
            prims[n, azim + 1, own_rows] = recv_f[1, n].astype(jnp.float32)
        for way, ghost, edge in ((0, PAD - 1, PAD), (1, PAD + rows, PAD + rows - 1)):
            at = pl.ds(ghost, 1)

            @pl.when(comes(way))
            def _(way=way, at=at):
                for n in range(8):
                    edge_f[way, n] = recv_f[2 + way, n].astype(jnp.float32).reshape(azim, 1, -1)

                def part(p, _):
                    for n in range(8):
                        prims[n, p + 1, at] = edge_f[way, n, p]
                    return 0

                lax.fori_loop(0, azim, part, 0)

            @pl.when(jnp.logical_not(comes(way)))
            def _(at=at, edge=edge):
                def part(p, _):
                    for n in range(8):
                        prims[n, p + 1, at] = prims[n, p + 1, pl.ds(edge, 1)]
                    return 0

                lax.fori_loop(0, azim, part, 0)

    def fluid_step():
        radial = vel_ref.shape[3]
        spot = lax.broadcasted_iota(jnp.int32, (8, radial), 1)
        scale = dt_ref[0] * inv_r_ref[0:8, :]

        for start in range(0, rows, 8):
            here_rows = pl.ds(pl.multiple_of(band * rows + start, 8), 8)
            scale_p = (1.0 / step_p) * scale * inv_sin_ref[here_rows, :]

            def load_cells(p, shift, start=start):
                return [prims[n, p, pl.ds(PAD + start + shift, 8)] for n in range(8)]

            def faces(p, lower, start=start, scale_p=scale_p, load_cells=load_cells):
                mine = load_cells(p + 1, 0)
                upper = face_flux(
                    fluid_cells(mine, 2), fluid_cells(load_cells(p + 2, 0), 2)
                )
                total = [scale_p * (upper[n] - lower[n]) for n in range(8)]
                here = fluid_cells(mine, 1)
                low = face_flux(fluid_cells(load_cells(p + 1, -1), 1), here)
                high = face_flux(here, fluid_cells(load_cells(p + 1, 1), 1))
                scale_t = (1.0 / step_t) * scale
                total = [total[n] + scale_t * (high[n] - low[n]) for n in range(8)]
                state, flux, speed = fluid_cells(mine, 0)

                def ahead(value):
                    return jnp.where(spot == radial - 1, value, pltpu.roll(value, radial - 1, 1))

                outer = face_flux(
                    (state, flux, speed),
                    ([ahead(x) for x in state], [ahead(x) for x in flux], ahead(speed)),
                )
                scale_r = (1.0 / step_r) * scale
                for n in range(8):
                    inner = jnp.where(spot == 0, flux[n], pltpu.roll(outer[n], 1, 1))
                    fluid[n, p, pl.ds(start, 8)] = state[n] - (
                        total[n] + scale_r * (outer[n] - inner)
                    )
                return upper

            first = face_flux(
                fluid_cells(load_cells(0, 0), 2), fluid_cells(load_cells(1, 0), 2)
            )
            lax.fori_loop(0, azim, faces, first)

    for way in range(2):

        @pl.when(has(way))
        def _(way=way):
            fluid_copy(2 + way).wait_send()

        @pl.when(comes(way))
        def _(way=way):
            fluid_copy(2 + way).wait_recv()

        fluid_copy(way).wait()
    fluid_in()
    fluid_step()
    fluid_store = pltpu.make_async_copy(fluid, fluid_hbm, fluid_sem)
    fluid_store.start()
    for s in range(1, bands):
        edge_t_copy(s).wait()
    for b in range(bands):
        for way in range(2):
            edge_p_copy(way, b).wait_send()
            pltpu.make_async_remote_copy(
                src_ref=edge_p.at[2 + way, b],
                dst_ref=edge_p.at[way, b],
                send_sem=edge_p_send.at[way, b],
                recv_sem=edge_p_recv.at[way, b],
                device_id={"phi": right if way == 0 else left, "band": b},
                device_id_type=MESH,
            ).wait_recv()
    make_coefs(band)
    for way in range(2):

        @pl.when(has(way))
        def _(way=way):
            whole_bin(way).wait_send()

        @pl.when(comes(way))
        def _(way=way):
            whole_bin(way).wait_recv()

        whole_phi(way).wait()
    stage_in_phi(0, cells, 0, colat)
    stage_in_bin(0, cells)

    def second_inner(block):
        start = pl.multiple_of(block * rows, rows)
        for way in range(2):
            phi_copy(1, way, block).wait_recv()
        stage_in_phi(1, firsts, start, rows)

        @pl.when((block == 0) | (block == bands - 1))
        def _():
            pad = jnp.where(block == 0, PAD - 1, PAD + colat)
            edge = jnp.where(block == 0, PAD, PAD + colat - 1)

            def part(p, _):
                for k in range(bins):
                    firsts[k + 1, p + 1, pl.ds(pad, 1)] = firsts[k + 1, p + 1, pl.ds(edge, 1)]
                return 0

            lax.fori_loop(0, azim, part, 0)

        def one(p, _):
            for part in range(rows // 8):
                apply(firsts, p, start + 8 * part, finish_second, 1, bins - 1)
            return 0

        lax.fori_loop(0, azim, one, 0)

    def visit(i, _):
        s = (i + 1) // 2
        below = lax.rem(i, 2) == 1
        block = jnp.where(below, band - s, band + s)
        valid = (block >= 0) & (block < bands)

        @pl.when(valid & below)
        def _():
            wind_copy(0, s - 1, block).wait_recv()

            @pl.when(band < bands - 1)
            def _():
                wind_copy(0, s, block).start()

        @pl.when(valid & jnp.logical_not(below) & (s > 0))
        def _():
            wind_copy(1, s - 1, block).wait_recv()

            @pl.when(band > 0)
            def _():
                wind_copy(1, s, block).start()

        @pl.when(valid)
        def _():
            @pl.when(s > 0)
            def _():
                make_coefs(block)

            start = pl.multiple_of(block * rows, rows)

            def one(p, _):
                for part in range(rows // 8):
                    apply(cells, p, start + 8 * part, finish_first, 0, bins)
                return 0

            lax.fori_loop(0, azim, one, 0)
            stage_out(1, firsts, start, rows)
            for way in range(2):

                @pl.when(has(way))
                def _(way=way):
                    bin_copy(1, way, block).start()

                phi_copy(1, way, block).start()

            inner = (s >= 2) | ((s == 1) & (jnp.logical_not(below) | (band == bands - 1)))
            outer = (s >= 1) & ((block == 0) | (block == bands - 1))

            def ready(t, _):
                @pl.when(jnp.where(t == 0, inner, outer))
                def _():
                    second_inner(jnp.where(t == 0, block + jnp.where(below, 1, -1), block))

                return 0

            lax.fori_loop(0, 2, ready, 0)

        return 0

    lax.fori_loop(0, 2 * bands - 1, visit, 0)
    for block in range(bands):
        for way in range(2):

            @pl.when(has(way))
            def _(way=way, block=block):
                bin_copy(1, way, block).wait_send()

            @pl.when(comes(way))
            def _(way=way, block=block):
                bin_copy(1, way, block).wait_recv()

            phi_copy(1, way, block).wait_send()
    stage_in_bin(1, firsts)

    def store(p):
        return pltpu.make_async_copy(
            cells.at[1 : bins + 1, p + 1, PAD : PAD + colat], out_hbm.at[:, p], store_sem.at[p]
        )

    def second(p, _):
        def one(j, _):
            start = pl.multiple_of(j * 8, 8)
            apply(firsts, p, start, finish_second, 0, 1)
            apply(firsts, p, start, finish_second, bins - 1, bins)
            return 0

        lax.fori_loop(0, colat // 8, one, 0)
        store(p).start()
        return 0

    lax.fori_loop(0, azim, second, 0)

    def stored(p, _):
        store(p).wait()
        return 0

    lax.fori_loop(0, azim, stored, 0)
    fluid_store.wait()
    for s in range(bands - 1):

        @pl.when((band - s >= 0) & (band < bands - 1))
        def _(s=s):
            wind_copy(0, s, band - s).wait_send()

        @pl.when((band + s < bands) & (band > 0))
        def _(s=s):
            wind_copy(1, s, band + s).wait_send()


def cosmic_ray_step(
    rho, velocity, mag, pres, density, kappa, tau, dt, bands, phis, spacing
):
    bins, azim, colat, shells = density.shape
    radial = velocity.shape[3]
    rows = colat // bands
    radius = INNER_RADIUS * np.exp(
        math.log(R_RATIO) / radial * (np.arange(radial) + 0.5)
    )
    theta = COLAT_LOW + COLAT_SPAN * (np.arange(colat) + 0.5) / colat
    wide = np.ones((colat, radial))
    inv_r = jnp.asarray(np.broadcast_to(1.0 / radius, (8, radial)), jnp.float32)
    inv_sin = jnp.asarray(wide / np.sin(theta)[:, None], jnp.float32)
    cot = jnp.asarray(wide * (np.cos(theta) / np.sin(theta))[:, None], jnp.float32)
    dma = pltpu.SemaphoreType.DMA
    vmem = pl.BlockSpec(memory_space=pltpu.VMEM)
    smem = pl.BlockSpec(memory_space=pltpu.SMEM)
    hbm = pl.BlockSpec(memory_space=pl.ANY)
    padded_shape = (bins + 2, azim + 2, colat + 2 * PAD, shells)
    return pl.pallas_call(
        functools.partial(cosmic_ray_kernel, bands, phis, spacing),
        out_shape=(
            jax.ShapeDtypeStruct(density.shape, jnp.float32),
            jax.ShapeDtypeStruct((8, azim, rows, radial), jnp.float32),
        ),
        in_specs=[smem, smem, smem, vmem, vmem, vmem, vmem, vmem, vmem, vmem, hbm],
        out_specs=(hbm, hbm),
        scratch_shapes=[
            pltpu.VMEM(padded_shape, jnp.float32),
            pltpu.VMEM(padded_shape, jnp.float32),
            pltpu.VMEM((10, azim, colat, shells), jnp.float32),
            pltpu.VMEM((bands, 6, azim, rows, shells), jnp.bfloat16),
            pltpu.VMEM((bands, 2, azim, shells), jnp.float32),
            pltpu.VMEM((4, bands, rows, shells), jnp.float32),
            pltpu.VMEM((2, 2, bins, colat, shells), jnp.bfloat16),
            pltpu.VMEM((2, 2, azim, colat, shells), jnp.bfloat16),
            pltpu.VMEM((2, 2, bins, colat, shells), jnp.bfloat16),
            pltpu.VMEM((2, 2, azim, colat, shells), jnp.bfloat16),
            pltpu.VMEM((8, azim + 2, rows + 2 * PAD, radial), jnp.float32),
            pltpu.VMEM((8, azim, rows, radial), jnp.float32),
            pltpu.VMEM((2, 8, azim, 1, radial), jnp.float32),
            pltpu.VMEM((4, 8, rows, radial), jnp.bfloat16),
            pltpu.VMEM((4, 8, rows, radial), jnp.bfloat16),
            dma,
            dma((4,)),
            dma((4,)),
            dma,
            dma((azim,)),
            dma((2, bands)),
            dma((2, bands)),
            dma((bands,)),
            dma((bands,)),
            dma((2, bands)),
            dma((2, bands)),
            dma((4,)),
            dma((4,)),
            dma((4, bands)),
            dma((4, bands)),
        ],
        compiler_params=pltpu.CompilerParams(
            collective_id=0, has_side_effects=True, vmem_limit_bytes=60 * 1024 * 1024
        ),
        cost_estimate=pl.CostEstimate(
            flops=80 * density.size, bytes_accessed=8 * density.size, transcendentals=0
        ),
        name="cosmic_ray",
    )(kappa, tau, dt, rho, velocity, mag, pres, inv_r, inv_sin, cot, density)


def body(
    density,
    velocity,
    magnetic_vector,
    pressure,
    fluid_courant_number,
    cosmic_ray_density,
    diffusion_per_bin,
    super_step_scale,
):
    azim_dev = density.shape[0]
    colat_dev = density.shape[1]
    radial_cell_count = density.shape[2]
    band_count = lax.axis_size("band")
    phi_count = lax.axis_size("phi")
    colatitude_count = colat_dev * band_count
    azimuth_cell_count = azim_dev * phi_count
    bin_dev = cosmic_ray_density.shape[0]
    momentum_bin_count = bin_dev * band_count
    outer_shell_count = cosmic_ray_density.shape[3]
    mesh_spacing = grid_steps(
        radial_cell_count, colatitude_count, azimuth_cell_count, momentum_bin_count
    )
    fluid_rate, cosmic_ray_rate = rate_limits(
        radial_cell_count,
        outer_shell_count,
        colatitude_count,
        azimuth_cell_count,
        momentum_bin_count,
    )
    cosmic_ray_next, fluid_state = cosmic_ray_step(
        density,
        velocity,
        magnetic_vector,
        pressure,
        cosmic_ray_density,
        diffusion_per_bin,
        (super_step_scale / (3.0 * cosmic_ray_rate)).reshape(1),
        (fluid_courant_number / fluid_rate).reshape(1),
        band_count,
        phi_count,
        mesh_spacing,
    )
    return (fluid_state, cosmic_ray_next)


def solution(mesh):
    placed = (
        P("phi", "band", None),
        P(None, "phi", "band", None),
        P(None, "phi", "band", None),
        P("phi", "band", None),
        P(),
        P("band", "phi", None, None),
        P(),
        P(),
    )
    return jax.shard_map(
        body,
        mesh=mesh,
        in_specs=placed,
        out_specs=(P(None, "phi", "band", None), P("band", "phi", None, None)),
        check_vma=False,
    )
```

```python
import functools
import math

import jax
import jax.numpy as jnp
import numpy as np
from jax import lax
from jax.experimental import pallas as pl
from jax.experimental.pallas import tpu as pltpu
from jax.sharding import PartitionSpec as P

ADIABATIC = 5.0 / 3.0
INNER_RADIUS = 0.1
R_RATIO = 30.0
COLAT_LOW = math.pi / 6.0
COLAT_SPAN = 2.0 * math.pi / 3.0
P_RATIO = 1000.0
K_RATIO = 0.1
B_FLOOR = 0.1
V_BOUND = 3.0
B_BOUND = 3.0
P_HIGH = 2.0
RHO_LOW = 0.5
KAPPA_HIGH = 0.5


def grid_steps(n_radial, n_colat, n_azim, n_bins):
    return (
        math.log(R_RATIO) / n_radial,
        COLAT_SPAN / n_colat,
        2.0 * math.pi / n_azim,
        math.log(P_RATIO) / n_bins,
    )


def rate_limits(n_radial, n_shells, n_colat, n_azim, n_bins):
    radial_spacing, colatitude_spacing, azimuth_spacing, step_m = grid_steps(
        n_radial, n_colat, n_azim, n_bins
    )
    sine_lower = math.sin(COLAT_LOW + 0.5 * colatitude_spacing)
    fluid_radius = INNER_RADIUS * math.exp(0.5 * radial_spacing)
    fastest_limit = V_BOUND + math.sqrt((ADIABATIC * P_HIGH + 3.0 * B_BOUND**2) / RHO_LOW)
    fluid_rate = fastest_limit * (
        1.0 / (fluid_radius * radial_spacing)
        + 1.0 / (fluid_radius * colatitude_spacing)
        + 1.0 / (fluid_radius * sine_lower * azimuth_spacing)
    )
    shell_low = INNER_RADIUS * math.exp(radial_spacing * (n_radial - n_shells + 0.5))
    inv_r = 1.0 / (shell_low * radial_spacing)
    inv_t = 1.0 / (shell_low * colatitude_spacing)
    inv_p = 1.0 / (shell_low * sine_lower * azimuth_spacing)
    cosmic_ray_rate = (
        2.0 * KAPPA_HIGH * (inv_r**2 + inv_t**2 + inv_p**2)
        + V_BOUND * (inv_r + inv_t + inv_p)
        + V_BOUND * (inv_r + inv_t + inv_p + 4.0 / shell_low) / (3.0 * step_m)
    )
    return (fluid_rate, cosmic_ray_rate)


def fluid_cells(prim, normal):
    rho, v, b, pres = prim[0], prim[1:4], prim[4:7], prim[7]
    v_n, b_n = v[normal], b[normal]
    b_sq = b[0] * b[0] + b[1] * b[1] + b[2] * b[2]
    v_sq = v[0] * v[0] + v[1] * v[1] + v[2] * v[2]
    energy = pres * (1.0 / (ADIABATIC - 1.0)) + 0.5 * rho * v_sq + 0.5 * b_sq
    total_p = pres + 0.5 * b_sq
    mom = [rho * v[k] for k in range(3)]
    state = [rho] + mom + list(b) + [energy]
    push = [mom[k] * v_n - b[k] * b_n for k in range(3)]
    push[normal] = push[normal] + total_p
    turn = [v_n * b[k] - b_n * v[k] for k in range(3)]
    work = (energy + total_p) * v_n - b_n * (v[0] * b[0] + v[1] * b[1] + v[2] * b[2])
    speed = jnp.abs(v_n) + jnp.sqrt((ADIABATIC * pres + b_sq) / rho)
    return state, [mom[normal]] + push + turn + [work], speed


def face_flux(low, high):
    wave = jnp.maximum(low[2], high[2])
    return [
        0.5 * ((low[1][n] + high[1][n]) - wave * (high[0][n] - low[0][n])) for n in range(8)
    ]


MESH = pl.DeviceIdType.MESH
PAD = 8


def cosmic_ray_kernel(
    bands,
    phis,
    spacing,
    kappa_ref,
    tau_ref,
    dt_ref,
    rho_ref,
    vel_ref,
    mag_ref,
    pres_ref,
    inv_r_ref,
    inv_sin_ref,
    cot_ref,
    f_hbm,
    out_hbm,
    fluid_hbm,
    cells,
    firsts,
    coefs,
    wind,
    edge_t,
    edge_p,
    send_phi,
    send_bin,
    recv_phi,
    recv_bin,
    prims,
    fluid,
    edge_f,
    send_f,
    recv_f,
    fluid_sem,
    fluid_send,
    fluid_recv,
    load_sem,
    store_sem,
    wind_send,
    wind_recv,
    edge_t_send,
    edge_t_recv,
    edge_p_send,
    edge_p_recv,
    halo_send,
    halo_recv,
    next_send,
    next_recv,
):
    bins = f_hbm.shape[0]
    azim = f_hbm.shape[1]
    colat = f_hbm.shape[2]
    shells = f_hbm.shape[3]
    rows = colat // bands
    first_shell = vel_ref.shape[3] - shells
    step_r, step_t, step_p, step_m = spacing
    band = lax.axis_index("band")
    phi = lax.axis_index("phi")
    right = lax.rem(phi + 1, phis)
    left = lax.rem(phi + phis - 1, phis)

    load = pltpu.make_async_copy(
        f_hbm, cells.at[1 : bins + 1, 1 : azim + 1, PAD : PAD + colat], load_sem
    )
    load.start()

    barrier = pltpu.get_barrier_semaphore()
    for b in range(bands):
        for side in (left, right):
            pl.semaphore_signal(
                barrier, inc=1, device_id={"phi": side, "band": b}, device_id_type=MESH
            )
    for s in range(1, bands):
        pl.semaphore_signal(
            barrier,
            inc=1,
            device_id={"band": lax.rem(band + s, bands)},
            device_id_type=MESH,
        )

    own_rows = pl.ds(PAD, rows)

    def take(p, _):
        v = [vel_ref[c, p] for c in range(3)]
        b = [mag_ref[c, p] for c in range(3)]
        prim = [rho_ref[p]] + v + b + [pres_ref[p]]
        shell = [x[:, first_shell:].astype(jnp.bfloat16) for x in v + b]
        for c in range(6):
            wind[band, c, p] = shell[c]
        for n in range(8):
            prims[n, p + 1, own_rows] = prim[n]
            edge_f[0, n, p] = prim[n][rows - 1 : rows]
            edge_f[1, n, p] = prim[n][0:1]
        u_t = shell[1].astype(jnp.float32)
        edge_t[band, 0, pl.ds(p, 1), :] = u_t[0:1]
        edge_t[band, 1, pl.ds(p, 1), :] = u_t[rows - 1 : rows]
        return 0

    lax.fori_loop(0, azim, take, 0)
    edge_p[2, band] = wind[band, 2, azim - 1].astype(jnp.float32)
    edge_p[3, band] = wind[band, 2, 0].astype(jnp.float32)
    for n in range(8):
        send_f[0, n] = prims[n, azim, own_rows].astype(jnp.bfloat16)
        send_f[1, n] = prims[n, 1, own_rows].astype(jnp.bfloat16)
        for way in range(2):
            send_f[2 + way, n] = edge_f[way, n].reshape(azim, -1).astype(jnp.bfloat16)
    pl.semaphore_wait(barrier, 3 * bands - 1)

    def fluid_copy(way):
        if way < 2:
            target = {"phi": right if way == 0 else left}
        else:
            target = {"band": band + (1 if way == 2 else -1)}
        return pltpu.make_async_remote_copy(
            src_ref=send_f.at[way],
            dst_ref=recv_f.at[way],
            send_sem=fluid_send.at[way],
            recv_sem=fluid_recv.at[way],
            device_id=target,
            device_id_type=MESH,
        )

    def has(way):
        return band < bands - 1 if way == 0 else band > 0

    def comes(way):
        return band > 0 if way == 0 else band < bands - 1

    def wind_copy(way, s, block):
        return pltpu.make_async_remote_copy(
            src_ref=wind.at[block],
            dst_ref=wind.at[block],
            send_sem=wind_send.at[way, s],
            recv_sem=wind_recv.at[way, s],
            device_id={"band": band + (1 if way == 0 else -1)},
            device_id_type=MESH,
        )

    def edge_t_copy(s):
        return pltpu.make_async_remote_copy(
            src_ref=edge_t.at[band],
            dst_ref=edge_t.at[band],
            send_sem=edge_t_send.at[s - 1],
            recv_sem=edge_t_recv.at[s - 1],
            device_id={"band": lax.rem(band + s, bands)},
            device_id_type=MESH,
        )

    def edge_p_copy(way, b):
        return pltpu.make_async_remote_copy(
            src_ref=edge_p.at[2 + way, band],
            dst_ref=edge_p.at[way, band],
            send_sem=edge_p_send.at[way, b],
            recv_sem=edge_p_recv.at[way, band],
            device_id={"phi": right if way == 0 else left, "band": b},
            device_id_type=MESH,
        )

    @pl.when(band < bands - 1)
    def _():
        wind_copy(0, 0, band).start()

    @pl.when(band > 0)
    def _():
        wind_copy(1, 0, band).start()

    for way in range(2):

        @pl.when(has(way))
        def _(way=way):
            fluid_copy(2 + way).start()

        fluid_copy(way).start()
    for s in range(1, bands):
        edge_t_copy(s).start()
    for b in range(bands):
        for way in range(2):
            edge_p_copy(way, b).start()

    def phi_copy(stage, way, block):
        part = pl.ds(pl.multiple_of(block * rows, rows), rows)
        sems = (next_send, next_recv)
        return pltpu.make_async_remote_copy(
            src_ref=send_phi.at[stage, way, :, part],
            dst_ref=recv_phi.at[stage, way, :, part],
            send_sem=sems[0].at[way, block],
            recv_sem=sems[1].at[way, block],
            device_id={"phi": right if way == 0 else left},
            device_id_type=MESH,
        )

    def bin_copy(stage, way, block):
        part = pl.ds(pl.multiple_of(block * rows, rows), rows)
        return pltpu.make_async_remote_copy(
            src_ref=send_bin.at[stage, way, :, part],
            dst_ref=recv_bin.at[stage, way, :, part],
            send_sem=next_send.at[2 + way, block],
            recv_sem=next_recv.at[2 + way, block],
            device_id={"band": band + (1 if way == 0 else -1)},
            device_id_type=MESH,
        )

    def whole_phi(way):
        return pltpu.make_async_remote_copy(
            src_ref=send_phi.at[0, way],
            dst_ref=recv_phi.at[0, way],
            send_sem=halo_send.at[way],
            recv_sem=halo_recv.at[way],
            device_id={"phi": right if way == 0 else left},
            device_id_type=MESH,
        )

    def whole_bin(way):
        return pltpu.make_async_remote_copy(
            src_ref=send_bin.at[0, way],
            dst_ref=recv_bin.at[0, way],
            send_sem=halo_send.at[2 + way],
            recv_sem=halo_recv.at[2 + way],
            device_id={"band": band + (1 if way == 0 else -1)},
            device_id_type=MESH,
        )

    def stage_out(stage, source, start, count):
        own = pl.ds(start, count)
        inner = pl.ds(PAD + start, count)

        def phi_part(k, _):
            last, lead = source[k + 1, azim, inner], source[k + 1, 1, inner]
            send_phi[stage, 0, k, own] = last.astype(jnp.bfloat16)
            send_phi[stage, 1, k, own] = lead.astype(jnp.bfloat16)
            return 0

        def bin_part(p, _):
            last, lead = source[bins, p + 1, inner], source[1, p + 1, inner]
            send_bin[stage, 0, p, own] = last.astype(jnp.bfloat16)
            send_bin[stage, 1, p, own] = lead.astype(jnp.bfloat16)
            return 0

        lax.fori_loop(0, bins, phi_part, 0)
        lax.fori_loop(0, azim, bin_part, 0)

    def stage_in_phi(stage, target, start, count):
        own = pl.ds(start, count)
        inner = pl.ds(PAD + start, count)

        def phi_part(k, _):
            target[k + 1, 0, inner] = recv_phi[stage, 0, k, own].astype(jnp.float32)
            target[k + 1, azim + 1, inner] = recv_phi[stage, 1, k, own].astype(jnp.float32)
            return 0

        lax.fori_loop(0, bins, phi_part, 0)

    def stage_in_bin(stage, target):
        inner = pl.ds(PAD, colat)
        for way, ghost, edge in ((0, 0, 1), (1, bins + 1, bins)):

            @pl.when(comes(way))
            def _(way=way, ghost=ghost):
                def bin_part(p, _):
                    target[ghost, p + 1, inner] = recv_bin[stage, way, p].astype(jnp.float32)
                    return 0

                lax.fori_loop(0, azim, bin_part, 0)

            @pl.when(jnp.logical_not(comes(way)))
            def _(ghost=ghost, edge=edge):
                def bin_part(p, _):
                    target[ghost, p + 1, inner] = target[edge, p + 1, inner]
                    return 0

                lax.fori_loop(0, azim, bin_part, 0)

    def pad_colat(target):
        def part(p, _):
            low = [target[k + 1, p + 1, PAD : PAD + 1] for k in range(bins)]
            high = [target[k + 1, p + 1, PAD + colat - 1 : PAD + colat] for k in range(bins)]
            for k in range(bins):
                target[k + 1, p + 1, PAD - 1 : PAD] = low[k]
                target[k + 1, p + 1, PAD + colat : PAD + colat + 1] = high[k]
            return 0

        lax.fori_loop(0, azim, part, 0)

    load.wait()
    stage_out(0, cells, 0, colat)
    for way in range(2):

        @pl.when(has(way))
        def _(way=way):
            whole_bin(way).start()

        whole_phi(way).start()
    pad_colat(cells)

    lane = lax.broadcasted_iota(jnp.int32, (rows, shells), 1)
    row = lax.broadcasted_iota(jnp.int32, (rows, shells), 0)
    tau = tau_ref[0]
    inv_r = jnp.broadcast_to(inv_r_ref[0:1, first_shell:], (rows, shells))
    inv_hr = inv_r * (1.0 / step_r)
    inv_ht = inv_r * (1.0 / step_t)

    def make_coefs(block):
        start = pl.multiple_of(block * rows, rows)
        part = pl.ds(start, rows)
        inv_hp = inv_r * inv_sin_ref[part, :shells] * (1.0 / step_p)
        cot_r = inv_r * cot_ref[part, :shells]
        below = jnp.maximum(block - 1, 0)
        above = jnp.minimum(block + 1, bands - 1)

        def one(p, _):
            u_r, u_t, u_p, b_r, b_t, b_p = [
                wind[block, c, p].astype(jnp.float32) for c in range(6)
            ]
            r_hi = jnp.where(lane == shells - 1, u_r, pltpu.roll(u_r, shells - 1, 1))
            r_lo = jnp.where(lane == 0, u_r, pltpu.roll(u_r, 1, 1))
            t_hi_row = jnp.where(
                block == bands - 1, u_t[rows - 1 : rows], edge_t[above, 0, pl.ds(p, 1), :]
            )
            t_lo_row = jnp.where(block == 0, u_t[0:1], edge_t[below, 1, pl.ds(p, 1), :])
            t_hi = jnp.where(row == rows - 1, t_hi_row, pltpu.roll(u_t, rows - 1, 0))
            t_lo = jnp.where(row == 0, t_lo_row, pltpu.roll(u_t, 1, 0))
            p_hi = jnp.where(
                p == azim - 1,
                edge_p[1, block],
                wind[block, 2, jnp.minimum(p + 1, azim - 1)].astype(jnp.float32),
            )
            p_lo = jnp.where(
                p == 0,
                edge_p[0, block],
                wind[block, 2, jnp.maximum(p - 1, 0)].astype(jnp.float32),
            )
            spread = (
                (r_hi - r_lo) * (0.5 * inv_hr)
                + 2.0 * u_r * inv_r
                + (t_hi - t_lo) * (0.5 * inv_ht)
                + cot_r * u_t
                + (p_hi - p_lo) * (0.5 * inv_hp)
            )
            spread = spread.astype(jnp.bfloat16).astype(jnp.float32)
            share = (1.0 - K_RATIO) / (b_r * b_r + b_t * b_t + b_p * b_p + B_FLOOR)
            c_r = tau * (K_RATIO + share * b_r * b_r) * inv_hr * inv_hr
            c_t = tau * (K_RATIO + share * b_t * b_t) * inv_ht * inv_ht
            c_p = tau * (K_RATIO + share * b_p * b_p) * inv_hp * inv_hp
            c_rp = jnp.where(lane == shells - 1, 0.0, c_r)
            c_rm = jnp.where(lane == 0, 0.0, c_r)
            a_r = tau * u_r * inv_hr
            a_r = jnp.where((lane == 0) & (a_r > 0.0), 0.0, a_r)
            a_r = jnp.where((lane == shells - 1) & (a_r < 0.0), 0.0, a_r)
            a_t = tau * u_t * inv_ht
            a_p = tau * u_p * inv_hp
            mu = tau * spread * (1.0 / (3.0 * step_m))
            c_sum = c_rp + c_rm + 2.0 * c_t + 2.0 * c_p
            a_sum = 1.0 - (jnp.abs(a_r) + jnp.abs(a_t) + jnp.abs(a_p) + jnp.abs(mu))
            for n, value in enumerate(
                (c_rp, c_rm, c_t, c_p, a_r, a_t, a_p, mu, c_sum, a_sum)
            ):
                coefs[n, p, part] = value
            return 0

        lax.fori_loop(0, azim, one, 0)

    def apply(source, p, start, finish, low_bin, high_bin):
        part = pl.ds(start, 8)
        mid = pl.ds(PAD + start, 8)
        low = pl.ds(PAD + start - 1, 8)
        high = pl.ds(PAD + start + 1, 8)
        c_rp, c_rm, c_t, c_p, a_r, a_t, a_p, mu, c_sum, a_sum = [
            coefs[n, p, part] for n in range(10)
        ]
        w_r, w_t, w_p, w_m = jnp.abs(a_r), jnp.abs(a_t), jnp.abs(a_p), jnp.abs(mu)
        out_r, out_t, out_p, up_m = a_r > 0.0, a_t > 0.0, a_p > 0.0, mu > 0.0
        values = []
        before = source[low_bin, p + 1, mid]
        here = source[low_bin + 1, p + 1, mid]
        for k in range(low_bin, high_bin):
            after = source[k + 2, p + 1, mid]
            kappa = kappa_ref[band * bins + k]
            r_hi = pltpu.roll(here, shells - 1, 1)
            r_lo = pltpu.roll(here, 1, 1)
            t_hi = source[k + 1, p + 1, high]
            t_lo = source[k + 1, p + 1, low]
            p_hi = source[k + 1, p + 2, mid]
            p_lo = source[k + 1, p, mid]
            curve = (
                (c_rp * r_hi + c_rm * r_lo)
                + (c_t * (t_hi + t_lo) + c_p * (p_hi + p_lo))
                - c_sum * here
            )
            flow = (
                (w_r * jnp.where(out_r, r_lo, r_hi) + w_t * jnp.where(out_t, t_lo, t_hi))
                + (w_p * jnp.where(out_p, p_lo, p_hi) + w_m * jnp.where(up_m, after, before))
                + a_sum * here
            )
            values.append(finish(k, p, mid, kappa * curve + flow))
            before, here = here, after
        target = firsts if source is cells else cells
        for k in range(low_bin, high_bin):
            target[k + 1, p + 1, mid] = values[k - low_bin]

    def finish_first(k, p, mid, value):
        return value

    def finish_second(k, p, mid, value):
        return 1.5 * value - 0.5 * cells[k + 1, p + 1, mid]

    def fluid_in():
        for n in range(8):
            prims[n, 0, own_rows] = recv_f[0, n].astype(jnp.float32)
            prims[n, azim + 1, own_rows] = recv_f[1, n].astype(jnp.float32)
        for way, ghost, edge in ((0, PAD - 1, PAD), (1, PAD + rows, PAD + rows - 1)):
            at = pl.ds(ghost, 1)

            @pl.when(comes(way))
            def _(way=way, at=at):
                for n in range(8):
                    edge_f[way, n] = recv_f[2 + way, n].astype(jnp.float32).reshape(azim, 1, -1)

                def part(p, _):
                    for n in range(8):
                        prims[n, p + 1, at] = edge_f[way, n, p]
                    return 0

                lax.fori_loop(0, azim, part, 0)

            @pl.when(jnp.logical_not(comes(way)))
            def _(at=at, edge=edge):
                def part(p, _):
                    for n in range(8):
                        prims[n, p + 1, at] = prims[n, p + 1, pl.ds(edge, 1)]
                    return 0

                lax.fori_loop(0, azim, part, 0)

    def fluid_step():
        radial = vel_ref.shape[3]
        spot = lax.broadcasted_iota(jnp.int32, (8, radial), 1)
        scale = dt_ref[0] * inv_r_ref[0:8, :]

        for start in range(0, rows, 8):
            here_rows = pl.ds(pl.multiple_of(band * rows + start, 8), 8)
            scale_p = (1.0 / step_p) * scale * inv_sin_ref[here_rows, :]

            def load_cells(p, shift, start=start):
                return [prims[n, p, pl.ds(PAD + start + shift, 8)] for n in range(8)]

            def faces(p, lower, start=start, scale_p=scale_p, load_cells=load_cells):
                mine = load_cells(p + 1, 0)
                upper = face_flux(
                    fluid_cells(mine, 2), fluid_cells(load_cells(p + 2, 0), 2)
                )
                total = [scale_p * (upper[n] - lower[n]) for n in range(8)]
                here = fluid_cells(mine, 1)
                low = face_flux(fluid_cells(load_cells(p + 1, -1), 1), here)
                high = face_flux(here, fluid_cells(load_cells(p + 1, 1), 1))
                scale_t = (1.0 / step_t) * scale
                total = [total[n] + scale_t * (high[n] - low[n]) for n in range(8)]
                state, flux, speed = fluid_cells(mine, 0)

                def ahead(value):
                    return jnp.where(spot == radial - 1, value, pltpu.roll(value, radial - 1, 1))

                outer = face_flux(
                    (state, flux, speed),
                    ([ahead(x) for x in state], [ahead(x) for x in flux], ahead(speed)),
                )
                scale_r = (1.0 / step_r) * scale
                for n in range(8):
                    inner = jnp.where(spot == 0, flux[n], pltpu.roll(outer[n], 1, 1))
                    fluid[n, p, pl.ds(start, 8)] = state[n] - (
                        total[n] + scale_r * (outer[n] - inner)
                    )
                return upper

            first = face_flux(
                fluid_cells(load_cells(0, 0), 2), fluid_cells(load_cells(1, 0), 2)
            )
            lax.fori_loop(0, azim, faces, first)

    for way in range(2):

        @pl.when(has(way))
        def _(way=way):
            fluid_copy(2 + way).wait_send()

        @pl.when(comes(way))
        def _(way=way):
            fluid_copy(2 + way).wait_recv()

        fluid_copy(way).wait()
    fluid_in()
    fluid_step()
    fluid_store = pltpu.make_async_copy(fluid, fluid_hbm, fluid_sem)
    fluid_store.start()
    for s in range(1, bands):
        edge_t_copy(s).wait()
    for b in range(bands):
        for way in range(2):
            edge_p_copy(way, b).wait_send()
            pltpu.make_async_remote_copy(
                src_ref=edge_p.at[2 + way, b],
                dst_ref=edge_p.at[way, b],
                send_sem=edge_p_send.at[way, b],
                recv_sem=edge_p_recv.at[way, b],
                device_id={"phi": right if way == 0 else left, "band": b},
                device_id_type=MESH,
            ).wait_recv()
    make_coefs(band)
    for way in range(2):

        @pl.when(has(way))
        def _(way=way):
            whole_bin(way).wait_send()

        @pl.when(comes(way))
        def _(way=way):
            whole_bin(way).wait_recv()

        whole_phi(way).wait()
    stage_in_phi(0, cells, 0, colat)
    stage_in_bin(0, cells)

    def second_inner(block):
        start = pl.multiple_of(block * rows, rows)
        for way in range(2):
            phi_copy(1, way, block).wait_recv()
        stage_in_phi(1, firsts, start, rows)

        @pl.when((block == 0) | (block == bands - 1))
        def _():
            pad = jnp.where(block == 0, PAD - 1, PAD + colat)
            edge = jnp.where(block == 0, PAD, PAD + colat - 1)

            def part(p, _):
                rim = [firsts[k + 1, p + 1, pl.ds(edge, 1)] for k in range(bins)]
                for k in range(bins):
                    firsts[k + 1, p + 1, pl.ds(pad, 1)] = rim[k]
                return 0

            lax.fori_loop(0, azim, part, 0)

        def one(p, _):
            for part in range(rows // 8):
                apply(firsts, p, start + 8 * part, finish_second, 1, bins - 1)
            return 0

        lax.fori_loop(0, azim, one, 0)

    def visit(i, _):
        s = (i + 1) // 2
        below = lax.rem(i, 2) == 1
        block = jnp.where(below, band - s, band + s)
        valid = (block >= 0) & (block < bands)

        @pl.when(valid & below)
        def _():
            wind_copy(0, s - 1, block).wait_recv()

            @pl.when(band < bands - 1)
            def _():
                wind_copy(0, s, block).start()

        @pl.when(valid & jnp.logical_not(below) & (s > 0))
        def _():
            wind_copy(1, s - 1, block).wait_recv()

            @pl.when(band > 0)
            def _():
                wind_copy(1, s, block).start()

        @pl.when(valid)
        def _():
            @pl.when(s > 0)
            def _():
                make_coefs(block)

            start = pl.multiple_of(block * rows, rows)

            def one(p, _):
                for part in range(rows // 8):
                    apply(cells, p, start + 8 * part, finish_first, 0, bins)
                return 0

            lax.fori_loop(0, azim, one, 0)
            stage_out(1, firsts, start, rows)
            for way in range(2):

                @pl.when(has(way))
                def _(way=way):
                    bin_copy(1, way, block).start()

                phi_copy(1, way, block).start()

            inner = (s >= 2) | ((s == 1) & (jnp.logical_not(below) | (band == bands - 1)))
            outer = (s >= 1) & ((block == 0) | (block == bands - 1))

            def ready(t, _):
                @pl.when(jnp.where(t == 0, inner, outer))
                def _():
                    second_inner(jnp.where(t == 0, block + jnp.where(below, 1, -1), block))

                return 0

            lax.fori_loop(0, 2, ready, 0)

        return 0

    lax.fori_loop(0, 2 * bands - 1, visit, 0)
    for block in range(bands):
        for way in range(2):

            @pl.when(has(way))
            def _(way=way, block=block):
                bin_copy(1, way, block).wait_send()

            @pl.when(comes(way))
            def _(way=way, block=block):
                bin_copy(1, way, block).wait_recv()

            phi_copy(1, way, block).wait_send()
    stage_in_bin(1, firsts)

    def store(p):
        return pltpu.make_async_copy(
            cells.at[1 : bins + 1, p + 1, PAD : PAD + colat], out_hbm.at[:, p], store_sem.at[p]
        )

    def second(p, _):
        def one(j, _):
            start = pl.multiple_of(j * 8, 8)
            apply(firsts, p, start, finish_second, 0, 1)
            apply(firsts, p, start, finish_second, bins - 1, bins)
            return 0

        lax.fori_loop(0, colat // 8, one, 0)
        store(p).start()
        return 0

    lax.fori_loop(0, azim, second, 0)

    def stored(p, _):
        store(p).wait()
        return 0

    lax.fori_loop(0, azim, stored, 0)
    fluid_store.wait()
    for s in range(bands - 1):

        @pl.when((band - s >= 0) & (band < bands - 1))
        def _(s=s):
            wind_copy(0, s, band - s).wait_send()

        @pl.when((band + s < bands) & (band > 0))
        def _(s=s):
            wind_copy(1, s, band + s).wait_send()


def deliver_kernel(ray_in, fluid_in, ray_out, fluid_out, ray, fluid, in_sem, out_sem):
    parts = [(fluid_in, fluid, fluid_out, n) for n in range(8)]
    parts += [(ray_in, ray, ray_out, k) for k in range(ray.shape[0])]
    loads = [
        pltpu.make_async_copy(a.at[n], b.at[n], in_sem.at[i])
        for i, (a, b, _, n) in enumerate(parts)
    ]
    stores = [
        pltpu.make_async_copy(b.at[n], c.at[n], out_sem.at[i])
        for i, (_, b, c, n) in enumerate(parts)
    ]
    for copy in loads:
        copy.start()
    for load, store in zip(loads, stores):
        load.wait()
        store.start()
    for copy in stores:
        copy.wait()


def cosmic_ray_step(
    rho, velocity, mag, pres, density, kappa, tau, dt, bands, phis, spacing
):
    bins, azim, colat, shells = density.shape
    radial = velocity.shape[3]
    rows = colat // bands
    radius = INNER_RADIUS * np.exp(
        math.log(R_RATIO) / radial * (np.arange(radial) + 0.5)
    )
    theta = COLAT_LOW + COLAT_SPAN * (np.arange(colat) + 0.5) / colat
    wide = np.ones((colat, radial))
    inv_r = jnp.asarray(np.broadcast_to(1.0 / radius, (8, radial)), jnp.float32)
    inv_sin = jnp.asarray(wide / np.sin(theta)[:, None], jnp.float32)
    cot = jnp.asarray(wide * (np.cos(theta) / np.sin(theta))[:, None], jnp.float32)
    dma = pltpu.SemaphoreType.DMA
    vmem = pl.BlockSpec(memory_space=pltpu.VMEM)
    smem = pl.BlockSpec(memory_space=pltpu.SMEM)
    hbm = pl.BlockSpec(memory_space=pl.ANY)
    padded_shape = (bins + 2, azim + 2, colat + 2 * PAD, shells)
    stepped, fluid = pl.pallas_call(
        functools.partial(cosmic_ray_kernel, bands, phis, spacing),
        out_shape=(
            jax.ShapeDtypeStruct(density.shape, jnp.float32),
            jax.ShapeDtypeStruct((8, azim, rows, radial), jnp.float32),
        ),
        in_specs=[smem, smem, smem, vmem, vmem, vmem, vmem, vmem, vmem, vmem, hbm],
        out_specs=(hbm, hbm),
        scratch_shapes=[
            pltpu.VMEM(padded_shape, jnp.float32),
            pltpu.VMEM(padded_shape, jnp.float32),
            pltpu.VMEM((10, azim, colat, shells), jnp.float32),
            pltpu.VMEM((bands, 6, azim, rows, shells), jnp.bfloat16),
            pltpu.VMEM((bands, 2, azim, shells), jnp.float32),
            pltpu.VMEM((4, bands, rows, shells), jnp.float32),
            pltpu.VMEM((2, 2, bins, colat, shells), jnp.bfloat16),
            pltpu.VMEM((2, 2, azim, colat, shells), jnp.bfloat16),
            pltpu.VMEM((2, 2, bins, colat, shells), jnp.bfloat16),
            pltpu.VMEM((2, 2, azim, colat, shells), jnp.bfloat16),
            pltpu.VMEM((8, azim + 2, rows + 2 * PAD, radial), jnp.float32),
            pltpu.VMEM((8, azim, rows, radial), jnp.float32),
            pltpu.VMEM((2, 8, azim, 1, radial), jnp.float32),
            pltpu.VMEM((4, 8, rows, radial), jnp.bfloat16),
            pltpu.VMEM((4, 8, rows, radial), jnp.bfloat16),
            dma,
            dma((4,)),
            dma((4,)),
            dma,
            dma((azim,)),
            dma((2, bands)),
            dma((2, bands)),
            dma((bands,)),
            dma((bands,)),
            dma((2, bands)),
            dma((2, bands)),
            dma((4,)),
            dma((4,)),
            dma((4, bands)),
            dma((4, bands)),
        ],
        compiler_params=pltpu.CompilerParams(
            collective_id=0, has_side_effects=True, vmem_limit_bytes=60 * 1024 * 1024
        ),
        cost_estimate=pl.CostEstimate(
            flops=80 * density.size, bytes_accessed=8 * density.size, transcendentals=0
        ),
        name="cosmic_ray",
    )(kappa, tau, dt, rho, velocity, mag, pres, inv_r, inv_sin, cot, density)
    return pl.pallas_call(
        deliver_kernel,
        out_shape=(
            jax.ShapeDtypeStruct(stepped.shape, jnp.float32),
            jax.ShapeDtypeStruct(fluid.shape, jnp.float32),
        ),
        in_specs=[hbm, hbm],
        out_specs=(hbm, hbm),
        scratch_shapes=[
            pltpu.VMEM(stepped.shape, jnp.float32),
            pltpu.VMEM(fluid.shape, jnp.float32),
            dma((bins + 8,)),
            dma((bins + 8,)),
        ],
        compiler_params=pltpu.CompilerParams(vmem_limit_bytes=32 * 1024 * 1024),
        name="deliver",
    )(stepped, fluid)


def body(
    density,
    velocity,
    magnetic_vector,
    pressure,
    fluid_courant_number,
    cosmic_ray_density,
    diffusion_per_bin,
    super_step_scale,
):
    azim_dev = density.shape[0]
    colat_dev = density.shape[1]
    radial_cell_count = density.shape[2]
    band_count = lax.axis_size("band")
    phi_count = lax.axis_size("phi")
    colatitude_count = colat_dev * band_count
    azimuth_cell_count = azim_dev * phi_count
    bin_dev = cosmic_ray_density.shape[0]
    momentum_bin_count = bin_dev * band_count
    outer_shell_count = cosmic_ray_density.shape[3]
    mesh_spacing = grid_steps(
        radial_cell_count, colatitude_count, azimuth_cell_count, momentum_bin_count
    )
    fluid_rate, cosmic_ray_rate = rate_limits(
        radial_cell_count,
        outer_shell_count,
        colatitude_count,
        azimuth_cell_count,
        momentum_bin_count,
    )
    cosmic_ray_next, fluid_state = cosmic_ray_step(
        density,
        velocity,
        magnetic_vector,
        pressure,
        cosmic_ray_density,
        diffusion_per_bin,
        (super_step_scale / (3.0 * cosmic_ray_rate)).reshape(1),
        (fluid_courant_number / fluid_rate).reshape(1),
        band_count,
        phi_count,
        mesh_spacing,
    )
    return (fluid_state, cosmic_ray_next)


def solution(mesh):
    placed = (
        P("phi", "band", None),
        P(None, "phi", "band", None),
        P(None, "phi", "band", None),
        P("phi", "band", None),
        P(),
        P("band", "phi", None, None),
        P(),
        P(),
    )
    return jax.shard_map(
        body,
        mesh=mesh,
        in_specs=placed,
        out_specs=(P(None, "phi", "band", None), P("band", "phi", None, None)),
        check_vma=False,
    )
```

```python
import functools
import math

import jax
import jax.numpy as jnp
import numpy as np
from jax import lax
from jax.experimental import pallas as pl
from jax.experimental.pallas import tpu as pltpu
from jax.sharding import PartitionSpec as P

ADIABATIC = 5.0 / 3.0
INNER_RADIUS = 0.1
R_RATIO = 30.0
COLAT_LOW = math.pi / 6.0
COLAT_SPAN = 2.0 * math.pi / 3.0
P_RATIO = 1000.0
K_RATIO = 0.1
B_FLOOR = 0.1
V_BOUND = 3.0
B_BOUND = 3.0
P_HIGH = 2.0
RHO_LOW = 0.5
KAPPA_HIGH = 0.5


def grid_steps(n_radial, n_colat, n_azim, n_bins):
    return (
        math.log(R_RATIO) / n_radial,
        COLAT_SPAN / n_colat,
        2.0 * math.pi / n_azim,
        math.log(P_RATIO) / n_bins,
    )


def rate_limits(n_radial, n_shells, n_colat, n_azim, n_bins):
    radial_spacing, colatitude_spacing, azimuth_spacing, step_m = grid_steps(
        n_radial, n_colat, n_azim, n_bins
    )
    sine_lower = math.sin(COLAT_LOW + 0.5 * colatitude_spacing)
    fluid_radius = INNER_RADIUS * math.exp(0.5 * radial_spacing)
    fastest_limit = V_BOUND + math.sqrt((ADIABATIC * P_HIGH + 3.0 * B_BOUND**2) / RHO_LOW)
    fluid_rate = fastest_limit * (
        1.0 / (fluid_radius * radial_spacing)
        + 1.0 / (fluid_radius * colatitude_spacing)
        + 1.0 / (fluid_radius * sine_lower * azimuth_spacing)
    )
    shell_low = INNER_RADIUS * math.exp(radial_spacing * (n_radial - n_shells + 0.5))
    inv_r = 1.0 / (shell_low * radial_spacing)
    inv_t = 1.0 / (shell_low * colatitude_spacing)
    inv_p = 1.0 / (shell_low * sine_lower * azimuth_spacing)
    cosmic_ray_rate = (
        2.0 * KAPPA_HIGH * (inv_r**2 + inv_t**2 + inv_p**2)
        + V_BOUND * (inv_r + inv_t + inv_p)
        + V_BOUND * (inv_r + inv_t + inv_p + 4.0 / shell_low) / (3.0 * step_m)
    )
    return (fluid_rate, cosmic_ray_rate)


def fluid_cells(prim, normal):
    rho, v, b, pres = prim[0], prim[1:4], prim[4:7], prim[7]
    v_n, b_n = v[normal], b[normal]
    b_sq = b[0] * b[0] + b[1] * b[1] + b[2] * b[2]
    v_sq = v[0] * v[0] + v[1] * v[1] + v[2] * v[2]
    energy = pres * (1.0 / (ADIABATIC - 1.0)) + 0.5 * rho * v_sq + 0.5 * b_sq
    total_p = pres + 0.5 * b_sq
    mom = [rho * v[k] for k in range(3)]
    state = [rho] + mom + list(b) + [energy]
    push = [mom[k] * v_n - b[k] * b_n for k in range(3)]
    push[normal] = push[normal] + total_p
    turn = [v_n * b[k] - b_n * v[k] for k in range(3)]
    work = (energy + total_p) * v_n - b_n * (v[0] * b[0] + v[1] * b[1] + v[2] * b[2])
    speed = jnp.abs(v_n) + jnp.sqrt((ADIABATIC * pres + b_sq) / rho)
    return state, [mom[normal]] + push + turn + [work], speed


def face_flux(low, high):
    wave = jnp.maximum(low[2], high[2])
    return [
        0.5 * ((low[1][n] + high[1][n]) - wave * (high[0][n] - low[0][n])) for n in range(8)
    ]


MESH = pl.DeviceIdType.MESH
PAD = 8


def cosmic_ray_kernel(
    bands,
    phis,
    spacing,
    kappa_ref,
    tau_ref,
    dt_ref,
    rho_ref,
    vel_ref,
    mag_ref,
    pres_ref,
    inv_r_ref,
    inv_sin_ref,
    cot_ref,
    f_hbm,
    out_hbm,
    fluid_hbm,
    cells,
    firsts,
    coefs,
    wind,
    edge_t,
    edge_p,
    send_phi,
    send_bin,
    recv_phi,
    recv_bin,
    prims,
    fluid,
    edge_f,
    send_f,
    recv_f,
    fluid_sem,
    fluid_send,
    fluid_recv,
    load_sem,
    store_sem,
    wind_send,
    wind_recv,
    edge_t_send,
    edge_t_recv,
    edge_p_send,
    edge_p_recv,
    halo_send,
    halo_recv,
    next_send,
    next_recv,
):
    bins = f_hbm.shape[0]
    azim = f_hbm.shape[1]
    colat = f_hbm.shape[2]
    shells = f_hbm.shape[3]
    rows = colat // bands
    first_shell = vel_ref.shape[3] - shells
    step_r, step_t, step_p, step_m = spacing
    band = lax.axis_index("band")
    phi = lax.axis_index("phi")
    right = lax.rem(phi + 1, phis)
    left = lax.rem(phi + phis - 1, phis)

    load = pltpu.make_async_copy(
        f_hbm, cells.at[1 : bins + 1, 1 : azim + 1, PAD : PAD + colat], load_sem
    )
    load.start()

    barrier = pltpu.get_barrier_semaphore()
    for b in range(bands):
        for side in (left, right):
            pl.semaphore_signal(
                barrier, inc=1, device_id={"phi": side, "band": b}, device_id_type=MESH
            )
    for s in range(1, bands):
        pl.semaphore_signal(
            barrier,
            inc=1,
            device_id={"band": lax.rem(band + s, bands)},
            device_id_type=MESH,
        )

    own_rows = pl.ds(PAD, rows)

    def take(p, _):
        v = [vel_ref[c, p] for c in range(3)]
        b = [mag_ref[c, p] for c in range(3)]
        prim = [rho_ref[p]] + v + b + [pres_ref[p]]
        shell = [x[:, first_shell:].astype(jnp.bfloat16) for x in v + b]
        for c in range(6):
            wind[band, c, p] = shell[c]
        for n in range(8):
            prims[n, p + 1, own_rows] = prim[n]
            edge_f[0, n, p] = prim[n][rows - 1 : rows]
            edge_f[1, n, p] = prim[n][0:1]
        u_t = shell[1].astype(jnp.float32)
        edge_t[band, 0, pl.ds(p, 1), :] = u_t[0:1]
        edge_t[band, 1, pl.ds(p, 1), :] = u_t[rows - 1 : rows]
        return 0

    lax.fori_loop(0, azim, take, 0)
    edge_p[2, band] = wind[band, 2, azim - 1].astype(jnp.float32)
    edge_p[3, band] = wind[band, 2, 0].astype(jnp.float32)
    for n in range(8):
        send_f[0, n] = prims[n, azim, own_rows].astype(jnp.bfloat16)
        send_f[1, n] = prims[n, 1, own_rows].astype(jnp.bfloat16)
        for way in range(2):
            send_f[2 + way, n] = edge_f[way, n].reshape(azim, -1).astype(jnp.bfloat16)
    pl.semaphore_wait(barrier, 3 * bands - 1)

    def fluid_copy(way):
        if way < 2:
            target = {"phi": right if way == 0 else left}
        else:
            target = {"band": band + (1 if way == 2 else -1)}
        return pltpu.make_async_remote_copy(
            src_ref=send_f.at[way],
            dst_ref=recv_f.at[way],
            send_sem=fluid_send.at[way],
            recv_sem=fluid_recv.at[way],
            device_id=target,
            device_id_type=MESH,
        )

    def has(way):
        return band < bands - 1 if way == 0 else band > 0

    def comes(way):
        return band > 0 if way == 0 else band < bands - 1

    def wind_copy(way, s, block):
        return pltpu.make_async_remote_copy(
            src_ref=wind.at[block],
            dst_ref=wind.at[block],
            send_sem=wind_send.at[way, s],
            recv_sem=wind_recv.at[way, s],
            device_id={"band": band + (1 if way == 0 else -1)},
            device_id_type=MESH,
        )

    def edge_t_copy(s):
        return pltpu.make_async_remote_copy(
            src_ref=edge_t.at[band],
            dst_ref=edge_t.at[band],
            send_sem=edge_t_send.at[s - 1],
            recv_sem=edge_t_recv.at[s - 1],
            device_id={"band": lax.rem(band + s, bands)},
            device_id_type=MESH,
        )

    def edge_p_copy(way, b):
        return pltpu.make_async_remote_copy(
            src_ref=edge_p.at[2 + way, band],
            dst_ref=edge_p.at[way, band],
            send_sem=edge_p_send.at[way, b],
            recv_sem=edge_p_recv.at[way, band],
            device_id={"phi": right if way == 0 else left, "band": b},
            device_id_type=MESH,
        )

    @pl.when(band < bands - 1)
    def _():
        wind_copy(0, 0, band).start()

    @pl.when(band > 0)
    def _():
        wind_copy(1, 0, band).start()

    for way in range(2):

        @pl.when(has(way))
        def _(way=way):
            fluid_copy(2 + way).start()

        fluid_copy(way).start()
    for s in range(1, bands):
        edge_t_copy(s).start()
    for b in range(bands):
        for way in range(2):
            edge_p_copy(way, b).start()

    def phi_copy(stage, way, block):
        part = pl.ds(pl.multiple_of(block * rows, rows), rows)
        sems = (next_send, next_recv)
        return pltpu.make_async_remote_copy(
            src_ref=send_phi.at[stage, way, :, part],
            dst_ref=recv_phi.at[stage, way, :, part],
            send_sem=sems[0].at[way, block],
            recv_sem=sems[1].at[way, block],
            device_id={"phi": right if way == 0 else left},
            device_id_type=MESH,
        )

    def bin_copy(stage, way, block):
        part = pl.ds(pl.multiple_of(block * rows, rows), rows)
        return pltpu.make_async_remote_copy(
            src_ref=send_bin.at[stage, way, :, part],
            dst_ref=recv_bin.at[stage, way, :, part],
            send_sem=next_send.at[2 + way, block],
            recv_sem=next_recv.at[2 + way, block],
            device_id={"band": band + (1 if way == 0 else -1)},
            device_id_type=MESH,
        )

    def whole_phi(way):
        return pltpu.make_async_remote_copy(
            src_ref=send_phi.at[0, way],
            dst_ref=recv_phi.at[0, way],
            send_sem=halo_send.at[way],
            recv_sem=halo_recv.at[way],
            device_id={"phi": right if way == 0 else left},
            device_id_type=MESH,
        )

    def whole_bin(way):
        return pltpu.make_async_remote_copy(
            src_ref=send_bin.at[0, way],
            dst_ref=recv_bin.at[0, way],
            send_sem=halo_send.at[2 + way],
            recv_sem=halo_recv.at[2 + way],
            device_id={"band": band + (1 if way == 0 else -1)},
            device_id_type=MESH,
        )

    def stage_out(stage, source, start, count):
        own = pl.ds(start, count)
        inner = pl.ds(PAD + start, count)

        def phi_part(k, _):
            last, lead = source[k + 1, azim, inner], source[k + 1, 1, inner]
            send_phi[stage, 0, k, own] = last.astype(jnp.bfloat16)
            send_phi[stage, 1, k, own] = lead.astype(jnp.bfloat16)
            return 0

        def bin_part(p, _):
            last, lead = source[bins, p + 1, inner], source[1, p + 1, inner]
            send_bin[stage, 0, p, own] = last.astype(jnp.bfloat16)
            send_bin[stage, 1, p, own] = lead.astype(jnp.bfloat16)
            return 0

        lax.fori_loop(0, bins, phi_part, 0)
        lax.fori_loop(0, azim, bin_part, 0)

    def stage_in_phi(stage, target, start, count):
        own = pl.ds(start, count)
        inner = pl.ds(PAD + start, count)

        def phi_part(k, _):
            target[k + 1, 0, inner] = recv_phi[stage, 0, k, own].astype(jnp.float32)
            target[k + 1, azim + 1, inner] = recv_phi[stage, 1, k, own].astype(jnp.float32)
            return 0

        lax.fori_loop(0, bins, phi_part, 0)

    def stage_in_bin(stage, target):
        inner = pl.ds(PAD, colat)
        for way, ghost, edge in ((0, 0, 1), (1, bins + 1, bins)):

            @pl.when(comes(way))
            def _(way=way, ghost=ghost):
                def bin_part(p, _):
                    target[ghost, p + 1, inner] = recv_bin[stage, way, p].astype(jnp.float32)
                    return 0

                lax.fori_loop(0, azim, bin_part, 0)

            @pl.when(jnp.logical_not(comes(way)))
            def _(ghost=ghost, edge=edge):
                def bin_part(p, _):
                    target[ghost, p + 1, inner] = target[edge, p + 1, inner]
                    return 0

                lax.fori_loop(0, azim, bin_part, 0)

    def pad_colat(target):
        def part(p, _):
            low = [target[k + 1, p + 1, PAD : PAD + 1] for k in range(bins)]
            high = [target[k + 1, p + 1, PAD + colat - 1 : PAD + colat] for k in range(bins)]
            for k in range(bins):
                target[k + 1, p + 1, PAD - 1 : PAD] = low[k]
                target[k + 1, p + 1, PAD + colat : PAD + colat + 1] = high[k]
            return 0

        lax.fori_loop(0, azim, part, 0)

    load.wait()
    stage_out(0, cells, 0, colat)
    for way in range(2):

        @pl.when(has(way))
        def _(way=way):
            whole_bin(way).start()

        whole_phi(way).start()
    pad_colat(cells)

    lane = lax.broadcasted_iota(jnp.int32, (rows, shells), 1)
    row = lax.broadcasted_iota(jnp.int32, (rows, shells), 0)
    tau = tau_ref[0]
    inv_r = jnp.broadcast_to(inv_r_ref[0:1, first_shell:], (rows, shells))
    inv_hr = inv_r * (1.0 / step_r)
    inv_ht = inv_r * (1.0 / step_t)

    def make_coefs(block):
        start = pl.multiple_of(block * rows, rows)
        part = pl.ds(start, rows)
        inv_hp = inv_r * inv_sin_ref[part, :shells] * (1.0 / step_p)
        cot_r = inv_r * cot_ref[part, :shells]
        below = jnp.maximum(block - 1, 0)
        above = jnp.minimum(block + 1, bands - 1)

        def one(p):
            u_r, u_t, u_p, b_r, b_t, b_p = [
                wind[block, c, p].astype(jnp.float32) for c in range(6)
            ]
            r_hi = jnp.where(lane == shells - 1, u_r, pltpu.roll(u_r, shells - 1, 1))
            r_lo = jnp.where(lane == 0, u_r, pltpu.roll(u_r, 1, 1))
            t_hi_row = jnp.where(
                block == bands - 1, u_t[rows - 1 : rows], edge_t[above, 0, pl.ds(p, 1), :]
            )
            t_lo_row = jnp.where(block == 0, u_t[0:1], edge_t[below, 1, pl.ds(p, 1), :])
            t_hi = jnp.where(row == rows - 1, t_hi_row, pltpu.roll(u_t, rows - 1, 0))
            t_lo = jnp.where(row == 0, t_lo_row, pltpu.roll(u_t, 1, 0))
            p_hi = jnp.where(
                p == azim - 1,
                edge_p[1, block],
                wind[block, 2, jnp.minimum(p + 1, azim - 1)].astype(jnp.float32),
            )
            p_lo = jnp.where(
                p == 0,
                edge_p[0, block],
                wind[block, 2, jnp.maximum(p - 1, 0)].astype(jnp.float32),
            )
            spread = (
                (r_hi - r_lo) * (0.5 * inv_hr)
                + 2.0 * u_r * inv_r
                + (t_hi - t_lo) * (0.5 * inv_ht)
                + cot_r * u_t
                + (p_hi - p_lo) * (0.5 * inv_hp)
            )
            spread = spread.astype(jnp.bfloat16).astype(jnp.float32)
            share = (1.0 - K_RATIO) / (b_r * b_r + b_t * b_t + b_p * b_p + B_FLOOR)
            c_r = tau * (K_RATIO + share * b_r * b_r) * inv_hr * inv_hr
            c_t = tau * (K_RATIO + share * b_t * b_t) * inv_ht * inv_ht
            c_p = tau * (K_RATIO + share * b_p * b_p) * inv_hp * inv_hp
            c_rp = jnp.where(lane == shells - 1, 0.0, c_r)
            c_rm = jnp.where(lane == 0, 0.0, c_r)
            a_r = tau * u_r * inv_hr
            a_r = jnp.where((lane == 0) & (a_r > 0.0), 0.0, a_r)
            a_r = jnp.where((lane == shells - 1) & (a_r < 0.0), 0.0, a_r)
            a_t = tau * u_t * inv_ht
            a_p = tau * u_p * inv_hp
            mu = tau * spread * (1.0 / (3.0 * step_m))
            c_sum = c_rp + c_rm + 2.0 * c_t + 2.0 * c_p
            a_sum = 1.0 - (jnp.abs(a_r) + jnp.abs(a_t) + jnp.abs(a_p) + jnp.abs(mu))
            return (c_rp, c_rm, c_t, c_p, a_r, a_t, a_p, mu, c_sum, a_sum)

        def pair(i, _):
            both = [one(2 * i), one(2 * i + 1)]
            for j in range(2):
                for n, value in enumerate(both[j]):
                    coefs[n, 2 * i + j, part] = value
            return 0

        lax.fori_loop(0, azim // 2, pair, 0)

    def apply(source, p, start, finish, low_bin, high_bin):
        part = pl.ds(start, 8)
        mid = pl.ds(PAD + start, 8)
        low = pl.ds(PAD + start - 1, 8)
        high = pl.ds(PAD + start + 1, 8)
        c_rp, c_rm, c_t, c_p, a_r, a_t, a_p, mu, c_sum, a_sum = [
            coefs[n, p, part] for n in range(10)
        ]
        w_r, w_t, w_p, w_m = jnp.abs(a_r), jnp.abs(a_t), jnp.abs(a_p), jnp.abs(mu)
        out_r, out_t, out_p, up_m = a_r > 0.0, a_t > 0.0, a_p > 0.0, mu > 0.0
        values = []
        before = source[low_bin, p + 1, mid]
        here = source[low_bin + 1, p + 1, mid]
        for k in range(low_bin, high_bin):
            after = source[k + 2, p + 1, mid]
            kappa = kappa_ref[band * bins + k]
            r_hi = pltpu.roll(here, shells - 1, 1)
            r_lo = pltpu.roll(here, 1, 1)
            t_hi = source[k + 1, p + 1, high]
            t_lo = source[k + 1, p + 1, low]
            p_hi = source[k + 1, p + 2, mid]
            p_lo = source[k + 1, p, mid]
            curve = (
                (c_rp * r_hi + c_rm * r_lo)
                + (c_t * (t_hi + t_lo) + c_p * (p_hi + p_lo))
                - c_sum * here
            )
            flow = (
                (w_r * jnp.where(out_r, r_lo, r_hi) + w_t * jnp.where(out_t, t_lo, t_hi))
                + (w_p * jnp.where(out_p, p_lo, p_hi) + w_m * jnp.where(up_m, after, before))
                + a_sum * here
            )
            values.append(finish(k, p, mid, kappa * curve + flow))
            before, here = here, after
        return [
            (k + 1, mid, value) for k, value in zip(range(low_bin, high_bin), values)
        ]

    def keep(target, p, results):
        for k, mid, value in results:
            target[k, p + 1, mid] = value

    def finish_first(k, p, mid, value):
        return value

    def finish_second(k, p, mid, value):
        return 1.5 * value - 0.5 * cells[k + 1, p + 1, mid]

    def fluid_in():
        for n in range(8):
            prims[n, 0, own_rows] = recv_f[0, n].astype(jnp.float32)
            prims[n, azim + 1, own_rows] = recv_f[1, n].astype(jnp.float32)
        for way, ghost, edge in ((0, PAD - 1, PAD), (1, PAD + rows, PAD + rows - 1)):
            at = pl.ds(ghost, 1)

            @pl.when(comes(way))
            def _(way=way, at=at):
                for n in range(8):
                    edge_f[way, n] = recv_f[2 + way, n].astype(jnp.float32).reshape(azim, 1, -1)

                def part(p, _):
                    for n in range(8):
                        prims[n, p + 1, at] = edge_f[way, n, p]
                    return 0

                lax.fori_loop(0, azim, part, 0)

            @pl.when(jnp.logical_not(comes(way)))
            def _(at=at, edge=edge):
                def part(p, _):
                    for n in range(8):
                        prims[n, p + 1, at] = prims[n, p + 1, pl.ds(edge, 1)]
                    return 0

                lax.fori_loop(0, azim, part, 0)

    def fluid_step():
        radial = vel_ref.shape[3]
        spot = lax.broadcasted_iota(jnp.int32, (8, radial), 1)
        scale = dt_ref[0] * inv_r_ref[0:8, :]

        for start in range(0, rows, 8):
            here_rows = pl.ds(pl.multiple_of(band * rows + start, 8), 8)
            scale_p = (1.0 / step_p) * scale * inv_sin_ref[here_rows, :]

            def load_cells(p, shift, start=start):
                return [prims[n, p, pl.ds(PAD + start + shift, 8)] for n in range(8)]

            def faces(p, lower, start=start, scale_p=scale_p, load_cells=load_cells):
                mine = load_cells(p + 1, 0)
                upper = face_flux(
                    fluid_cells(mine, 2), fluid_cells(load_cells(p + 2, 0), 2)
                )
                total = [scale_p * (upper[n] - lower[n]) for n in range(8)]
                here = fluid_cells(mine, 1)
                low = face_flux(fluid_cells(load_cells(p + 1, -1), 1), here)
                high = face_flux(here, fluid_cells(load_cells(p + 1, 1), 1))
                scale_t = (1.0 / step_t) * scale
                total = [total[n] + scale_t * (high[n] - low[n]) for n in range(8)]
                state, flux, speed = fluid_cells(mine, 0)

                def ahead(value):
                    return jnp.where(spot == radial - 1, value, pltpu.roll(value, radial - 1, 1))

                outer = face_flux(
                    (state, flux, speed),
                    ([ahead(x) for x in state], [ahead(x) for x in flux], ahead(speed)),
                )
                scale_r = (1.0 / step_r) * scale
                for n in range(8):
                    inner = jnp.where(spot == 0, flux[n], pltpu.roll(outer[n], 1, 1))
                    fluid[n, p, pl.ds(start, 8)] = state[n] - (
                        total[n] + scale_r * (outer[n] - inner)
                    )
                return upper

            first = face_flux(
                fluid_cells(load_cells(0, 0), 2), fluid_cells(load_cells(1, 0), 2)
            )
            lax.fori_loop(0, azim, faces, first)

    for way in range(2):

        @pl.when(has(way))
        def _(way=way):
            fluid_copy(2 + way).wait_send()

        @pl.when(comes(way))
        def _(way=way):
            fluid_copy(2 + way).wait_recv()

        fluid_copy(way).wait()
    fluid_in()
    fluid_step()
    fluid_store = pltpu.make_async_copy(fluid, fluid_hbm, fluid_sem)
    fluid_store.start()
    for s in range(1, bands):
        edge_t_copy(s).wait()
    for b in range(bands):
        for way in range(2):
            edge_p_copy(way, b).wait_send()
            pltpu.make_async_remote_copy(
                src_ref=edge_p.at[2 + way, b],
                dst_ref=edge_p.at[way, b],
                send_sem=edge_p_send.at[way, b],
                recv_sem=edge_p_recv.at[way, b],
                device_id={"phi": right if way == 0 else left, "band": b},
                device_id_type=MESH,
            ).wait_recv()
    make_coefs(band)
    for way in range(2):

        @pl.when(has(way))
        def _(way=way):
            whole_bin(way).wait_send()

        @pl.when(comes(way))
        def _(way=way):
            whole_bin(way).wait_recv()

        whole_phi(way).wait()
    stage_in_phi(0, cells, 0, colat)
    stage_in_bin(0, cells)

    def second_inner(block):
        start = pl.multiple_of(block * rows, rows)
        for way in range(2):
            phi_copy(1, way, block).wait_recv()
        stage_in_phi(1, firsts, start, rows)

        @pl.when((block == 0) | (block == bands - 1))
        def _():
            pad = jnp.where(block == 0, PAD - 1, PAD + colat)
            edge = jnp.where(block == 0, PAD, PAD + colat - 1)

            def part(p, _):
                rim = [firsts[k + 1, p + 1, pl.ds(edge, 1)] for k in range(bins)]
                for k in range(bins):
                    firsts[k + 1, p + 1, pl.ds(pad, 1)] = rim[k]
                return 0

            lax.fori_loop(0, azim, part, 0)

        def one(p, _):
            results = []
            for part in range(rows // 8):
                results += apply(firsts, p, start + 8 * part, finish_second, 1, bins - 1)
            keep(cells, p, results)
            return 0

        lax.fori_loop(0, azim, one, 0)

    def visit(i, _):
        s = (i + 1) // 2
        below = lax.rem(i, 2) == 1
        block = jnp.where(below, band - s, band + s)
        valid = (block >= 0) & (block < bands)

        @pl.when(valid & below)
        def _():
            wind_copy(0, s - 1, block).wait_recv()

            @pl.when(band < bands - 1)
            def _():
                wind_copy(0, s, block).start()

        @pl.when(valid & jnp.logical_not(below) & (s > 0))
        def _():
            wind_copy(1, s - 1, block).wait_recv()

            @pl.when(band > 0)
            def _():
                wind_copy(1, s, block).start()

        @pl.when(valid)
        def _():
            @pl.when(s > 0)
            def _():
                make_coefs(block)

            start = pl.multiple_of(block * rows, rows)

            def one(p, _):
                results = []
                for part in range(rows // 8):
                    results += apply(cells, p, start + 8 * part, finish_first, 0, bins)
                keep(firsts, p, results)
                return 0

            lax.fori_loop(0, azim, one, 0)
            stage_out(1, firsts, start, rows)
            for way in range(2):

                @pl.when(has(way))
                def _(way=way):
                    bin_copy(1, way, block).start()

                phi_copy(1, way, block).start()

            inner = (s >= 2) | ((s == 1) & (jnp.logical_not(below) | (band == bands - 1)))
            outer = (s >= 1) & ((block == 0) | (block == bands - 1))

            def ready(t, _):
                @pl.when(jnp.where(t == 0, inner, outer))
                def _():
                    second_inner(jnp.where(t == 0, block + jnp.where(below, 1, -1), block))

                return 0

            lax.fori_loop(0, 2, ready, 0)

        return 0

    lax.fori_loop(0, 2 * bands - 1, visit, 0)
    for block in range(bands):
        for way in range(2):

            @pl.when(has(way))
            def _(way=way, block=block):
                bin_copy(1, way, block).wait_send()

            @pl.when(comes(way))
            def _(way=way, block=block):
                bin_copy(1, way, block).wait_recv()

            phi_copy(1, way, block).wait_send()
    stage_in_bin(1, firsts)

    def store(p):
        return pltpu.make_async_copy(
            cells.at[1 : bins + 1, p + 1, PAD : PAD + colat], out_hbm.at[:, p], store_sem.at[p]
        )

    group = math.gcd(colat // 8, 8)

    def second(p, _):
        def one(j, _):
            results = []
            for part in range(group):
                start = pl.multiple_of((j * group + part) * 8, 8)
                results += apply(firsts, p, start, finish_second, 0, 1)
                results += apply(firsts, p, start, finish_second, bins - 1, bins)
            keep(cells, p, results)
            return 0

        lax.fori_loop(0, colat // (8 * group), one, 0)
        store(p).start()
        return 0

    lax.fori_loop(0, azim, second, 0)

    def stored(p, _):
        store(p).wait()
        return 0

    lax.fori_loop(0, azim, stored, 0)
    fluid_store.wait()
    for s in range(bands - 1):

        @pl.when((band - s >= 0) & (band < bands - 1))
        def _(s=s):
            wind_copy(0, s, band - s).wait_send()

        @pl.when((band + s < bands) & (band > 0))
        def _(s=s):
            wind_copy(1, s, band + s).wait_send()


def deliver_kernel(ray_in, fluid_in, ray_out, fluid_out, ray, fluid, in_sem, out_sem):
    parts = [(fluid_in, fluid, fluid_out, n) for n in range(8)]
    parts += [(ray_in, ray, ray_out, k) for k in range(ray.shape[0])]
    loads = [
        pltpu.make_async_copy(a.at[n], b.at[n], in_sem.at[i])
        for i, (a, b, _, n) in enumerate(parts)
    ]
    stores = [
        pltpu.make_async_copy(b.at[n], c.at[n], out_sem.at[i])
        for i, (_, b, c, n) in enumerate(parts)
    ]
    for copy in loads:
        copy.start()
    for load, store in zip(loads, stores):
        load.wait()
        store.start()
    for copy in stores:
        copy.wait()


def cosmic_ray_step(
    rho, velocity, mag, pres, density, kappa, tau, dt, bands, phis, spacing
):
    bins, azim, colat, shells = density.shape
    radial = velocity.shape[3]
    rows = colat // bands
    radius = INNER_RADIUS * np.exp(
        math.log(R_RATIO) / radial * (np.arange(radial) + 0.5)
    )
    theta = COLAT_LOW + COLAT_SPAN * (np.arange(colat) + 0.5) / colat
    wide = np.ones((colat, radial))
    inv_r = jnp.asarray(np.broadcast_to(1.0 / radius, (8, radial)), jnp.float32)
    inv_sin = jnp.asarray(wide / np.sin(theta)[:, None], jnp.float32)
    cot = jnp.asarray(wide * (np.cos(theta) / np.sin(theta))[:, None], jnp.float32)
    dma = pltpu.SemaphoreType.DMA
    vmem = pl.BlockSpec(memory_space=pltpu.VMEM)
    smem = pl.BlockSpec(memory_space=pltpu.SMEM)
    hbm = pl.BlockSpec(memory_space=pl.ANY)
    padded_shape = (bins + 2, azim + 2, colat + 2 * PAD, shells)
    stepped, fluid = pl.pallas_call(
        functools.partial(cosmic_ray_kernel, bands, phis, spacing),
        out_shape=(
            jax.ShapeDtypeStruct(density.shape, jnp.float32),
            jax.ShapeDtypeStruct((8, azim, rows, radial), jnp.float32),
        ),
        in_specs=[smem, smem, smem, vmem, vmem, vmem, vmem, vmem, vmem, vmem, hbm],
        out_specs=(hbm, hbm),
        scratch_shapes=[
            pltpu.VMEM(padded_shape, jnp.float32),
            pltpu.VMEM(padded_shape, jnp.float32),
            pltpu.VMEM((10, azim, colat, shells), jnp.float32),
            pltpu.VMEM((bands, 6, azim, rows, shells), jnp.bfloat16),
            pltpu.VMEM((bands, 2, azim, shells), jnp.float32),
            pltpu.VMEM((4, bands, rows, shells), jnp.float32),
            pltpu.VMEM((2, 2, bins, colat, shells), jnp.bfloat16),
            pltpu.VMEM((2, 2, azim, colat, shells), jnp.bfloat16),
            pltpu.VMEM((2, 2, bins, colat, shells), jnp.bfloat16),
            pltpu.VMEM((2, 2, azim, colat, shells), jnp.bfloat16),
            pltpu.VMEM((8, azim + 2, rows + 2 * PAD, radial), jnp.float32),
            pltpu.VMEM((8, azim, rows, radial), jnp.float32),
            pltpu.VMEM((2, 8, azim, 1, radial), jnp.float32),
            pltpu.VMEM((4, 8, rows, radial), jnp.bfloat16),
            pltpu.VMEM((4, 8, rows, radial), jnp.bfloat16),
            dma,
            dma((4,)),
            dma((4,)),
            dma,
            dma((azim,)),
            dma((2, bands)),
            dma((2, bands)),
            dma((bands,)),
            dma((bands,)),
            dma((2, bands)),
            dma((2, bands)),
            dma((4,)),
            dma((4,)),
            dma((4, bands)),
            dma((4, bands)),
        ],
        compiler_params=pltpu.CompilerParams(
            collective_id=0, has_side_effects=True, vmem_limit_bytes=60 * 1024 * 1024
        ),
        cost_estimate=pl.CostEstimate(
            flops=80 * density.size, bytes_accessed=8 * density.size, transcendentals=0
        ),
        name="cosmic_ray",
    )(kappa, tau, dt, rho, velocity, mag, pres, inv_r, inv_sin, cot, density)
    return pl.pallas_call(
        deliver_kernel,
        out_shape=(
            jax.ShapeDtypeStruct(stepped.shape, jnp.float32),
            jax.ShapeDtypeStruct(fluid.shape, jnp.float32),
        ),
        in_specs=[hbm, hbm],
        out_specs=(hbm, hbm),
        scratch_shapes=[
            pltpu.VMEM(stepped.shape, jnp.float32),
            pltpu.VMEM(fluid.shape, jnp.float32),
            dma((bins + 8,)),
            dma((bins + 8,)),
        ],
        compiler_params=pltpu.CompilerParams(vmem_limit_bytes=60 * 1024 * 1024),
        name="deliver",
    )(stepped, fluid)


def body(
    density,
    velocity,
    magnetic_vector,
    pressure,
    fluid_courant_number,
    cosmic_ray_density,
    diffusion_per_bin,
    super_step_scale,
):
    azim_dev = density.shape[0]
    colat_dev = density.shape[1]
    radial_cell_count = density.shape[2]
    band_count = lax.axis_size("band")
    phi_count = lax.axis_size("phi")
    colatitude_count = colat_dev * band_count
    azimuth_cell_count = azim_dev * phi_count
    bin_dev = cosmic_ray_density.shape[0]
    momentum_bin_count = bin_dev * band_count
    outer_shell_count = cosmic_ray_density.shape[3]
    mesh_spacing = grid_steps(
        radial_cell_count, colatitude_count, azimuth_cell_count, momentum_bin_count
    )
    fluid_rate, cosmic_ray_rate = rate_limits(
        radial_cell_count,
        outer_shell_count,
        colatitude_count,
        azimuth_cell_count,
        momentum_bin_count,
    )
    cosmic_ray_next, fluid_state = cosmic_ray_step(
        density,
        velocity,
        magnetic_vector,
        pressure,
        cosmic_ray_density,
        diffusion_per_bin,
        (super_step_scale / (3.0 * cosmic_ray_rate)).reshape(1),
        (fluid_courant_number / fluid_rate).reshape(1),
        band_count,
        phi_count,
        mesh_spacing,
    )
    return (fluid_state, cosmic_ray_next)


def solution(mesh):
    placed = (
        P("phi", "band", None),
        P(None, "phi", "band", None),
        P(None, "phi", "band", None),
        P("phi", "band", None),
        P(),
        P("band", "phi", None, None),
        P(),
        P(),
    )
    return jax.shard_map(
        body,
        mesh=mesh,
        in_specs=placed,
        out_specs=(P(None, "phi", "band", None), P("band", "phi", None, None)),
        check_vma=False,
    )
```

```python
import functools
import math

import jax
import jax.numpy as jnp
import numpy as np
from jax import lax
from jax.experimental import pallas as pl
from jax.experimental.pallas import tpu as pltpu
from jax.sharding import PartitionSpec as P

ADIABATIC = 5.0 / 3.0
INNER_RADIUS = 0.1
R_RATIO = 30.0
COLAT_LOW = math.pi / 6.0
COLAT_SPAN = 2.0 * math.pi / 3.0
P_RATIO = 1000.0
K_RATIO = 0.1
B_FLOOR = 0.1
V_BOUND = 3.0
B_BOUND = 3.0
P_HIGH = 2.0
RHO_LOW = 0.5
KAPPA_HIGH = 0.5


def grid_steps(n_radial, n_colat, n_azim, n_bins):
    return (
        math.log(R_RATIO) / n_radial,
        COLAT_SPAN / n_colat,
        2.0 * math.pi / n_azim,
        math.log(P_RATIO) / n_bins,
    )


def rate_limits(n_radial, n_shells, n_colat, n_azim, n_bins):
    radial_spacing, colatitude_spacing, azimuth_spacing, step_m = grid_steps(
        n_radial, n_colat, n_azim, n_bins
    )
    sine_lower = math.sin(COLAT_LOW + 0.5 * colatitude_spacing)
    fluid_radius = INNER_RADIUS * math.exp(0.5 * radial_spacing)
    fastest_limit = V_BOUND + math.sqrt((ADIABATIC * P_HIGH + 3.0 * B_BOUND**2) / RHO_LOW)
    fluid_rate = fastest_limit * (
        1.0 / (fluid_radius * radial_spacing)
        + 1.0 / (fluid_radius * colatitude_spacing)
        + 1.0 / (fluid_radius * sine_lower * azimuth_spacing)
    )
    shell_low = INNER_RADIUS * math.exp(radial_spacing * (n_radial - n_shells + 0.5))
    inv_r = 1.0 / (shell_low * radial_spacing)
    inv_t = 1.0 / (shell_low * colatitude_spacing)
    inv_p = 1.0 / (shell_low * sine_lower * azimuth_spacing)
    cosmic_ray_rate = (
        2.0 * KAPPA_HIGH * (inv_r**2 + inv_t**2 + inv_p**2)
        + V_BOUND * (inv_r + inv_t + inv_p)
        + V_BOUND * (inv_r + inv_t + inv_p + 4.0 / shell_low) / (3.0 * step_m)
    )
    return (fluid_rate, cosmic_ray_rate)


def fluid_cells(prim, normal):
    rho, v, b, pres = prim[0], prim[1:4], prim[4:7], prim[7]
    v_n, b_n = v[normal], b[normal]
    b_sq = b[0] * b[0] + b[1] * b[1] + b[2] * b[2]
    v_sq = v[0] * v[0] + v[1] * v[1] + v[2] * v[2]
    energy = pres * (1.0 / (ADIABATIC - 1.0)) + 0.5 * rho * v_sq + 0.5 * b_sq
    total_p = pres + 0.5 * b_sq
    mom = [rho * v[k] for k in range(3)]
    state = [rho] + mom + list(b) + [energy]
    push = [mom[k] * v_n - b[k] * b_n for k in range(3)]
    push[normal] = push[normal] + total_p
    turn = [v_n * b[k] - b_n * v[k] for k in range(3)]
    work = (energy + total_p) * v_n - b_n * (v[0] * b[0] + v[1] * b[1] + v[2] * b[2])
    speed = jnp.abs(v_n) + jnp.sqrt((ADIABATIC * pres + b_sq) / rho)
    return state, [mom[normal]] + push + turn + [work], speed


def face_flux(low, high):
    wave = jnp.maximum(low[2], high[2])
    return [
        0.5 * ((low[1][n] + high[1][n]) - wave * (high[0][n] - low[0][n])) for n in range(8)
    ]


MESH = pl.DeviceIdType.MESH
PAD = 8


def cosmic_ray_kernel(
    bands,
    phis,
    spacing,
    kappa_ref,
    tau_ref,
    dt_ref,
    rho_ref,
    vel_ref,
    mag_ref,
    pres_ref,
    inv_r_ref,
    inv_sin_ref,
    cot_ref,
    f_hbm,
    out_hbm,
    fluid_hbm,
    cells,
    firsts,
    coefs,
    wind,
    edge_t,
    edge_p,
    send_phi,
    send_bin,
    recv_phi,
    recv_bin,
    prims,
    fluid,
    edge_f,
    send_f,
    recv_f,
    fluid_sem,
    fluid_send,
    fluid_recv,
    load_sem,
    store_sem,
    wind_send,
    wind_recv,
    edge_t_send,
    edge_t_recv,
    edge_p_send,
    edge_p_recv,
    halo_send,
    halo_recv,
    next_send,
    next_recv,
):
    bins = f_hbm.shape[0]
    azim = f_hbm.shape[1]
    colat = f_hbm.shape[2]
    shells = f_hbm.shape[3]
    rows = colat // bands
    first_shell = vel_ref.shape[3] - shells
    step_r, step_t, step_p, step_m = spacing
    band = lax.axis_index("band")
    phi = lax.axis_index("phi")
    right = lax.rem(phi + 1, phis)
    left = lax.rem(phi + phis - 1, phis)

    load = pltpu.make_async_copy(
        f_hbm, cells.at[1 : bins + 1, 1 : azim + 1, PAD : PAD + colat], load_sem
    )
    load.start()

    barrier = pltpu.get_barrier_semaphore()
    for b in range(bands):
        for side in (left, right):
            pl.semaphore_signal(
                barrier, inc=1, device_id={"phi": side, "band": b}, device_id_type=MESH
            )
    for s in range(1, bands):
        pl.semaphore_signal(
            barrier,
            inc=1,
            device_id={"band": lax.rem(band + s, bands)},
            device_id_type=MESH,
        )

    own_rows = pl.ds(PAD, rows)

    def take(p, _):
        v = [vel_ref[c, p] for c in range(3)]
        b = [mag_ref[c, p] for c in range(3)]
        prim = [rho_ref[p]] + v + b + [pres_ref[p]]
        shell = [x[:, first_shell:].astype(jnp.bfloat16) for x in v + b]
        for c in range(6):
            wind[band, c, p] = shell[c]
        for n in range(8):
            prims[n, p + 1, own_rows] = prim[n]
            edge_f[0, n, p] = prim[n][rows - 1 : rows]
            edge_f[1, n, p] = prim[n][0:1]
        u_t = shell[1].astype(jnp.float32)
        edge_t[band, 0, pl.ds(p, 1), :] = u_t[0:1]
        edge_t[band, 1, pl.ds(p, 1), :] = u_t[rows - 1 : rows]
        return 0

    lax.fori_loop(0, azim, take, 0)
    edge_p[2, band] = wind[band, 2, azim - 1].astype(jnp.float32)
    edge_p[3, band] = wind[band, 2, 0].astype(jnp.float32)
    for n in range(8):
        send_f[0, n] = prims[n, azim, own_rows].astype(jnp.bfloat16)
        send_f[1, n] = prims[n, 1, own_rows].astype(jnp.bfloat16)
        for way in range(2):
            send_f[2 + way, n] = edge_f[way, n].reshape(azim, -1).astype(jnp.bfloat16)
    pl.semaphore_wait(barrier, 3 * bands - 1)

    def fluid_copy(way):
        if way < 2:
            target = {"phi": right if way == 0 else left}
        else:
            target = {"band": band + (1 if way == 2 else -1)}
        return pltpu.make_async_remote_copy(
            src_ref=send_f.at[way],
            dst_ref=recv_f.at[way],
            send_sem=fluid_send.at[way],
            recv_sem=fluid_recv.at[way],
            device_id=target,
            device_id_type=MESH,
        )

    def has(way):
        return band < bands - 1 if way == 0 else band > 0

    def comes(way):
        return band > 0 if way == 0 else band < bands - 1

    def wind_copy(way, s, block):
        return pltpu.make_async_remote_copy(
            src_ref=wind.at[block],
            dst_ref=wind.at[block],
            send_sem=wind_send.at[way, s],
            recv_sem=wind_recv.at[way, s],
            device_id={"band": band + (1 if way == 0 else -1)},
            device_id_type=MESH,
        )

    def edge_t_copy(s):
        return pltpu.make_async_remote_copy(
            src_ref=edge_t.at[band],
            dst_ref=edge_t.at[band],
            send_sem=edge_t_send.at[s - 1],
            recv_sem=edge_t_recv.at[s - 1],
            device_id={"band": lax.rem(band + s, bands)},
            device_id_type=MESH,
        )

    def edge_p_copy(way, b):
        return pltpu.make_async_remote_copy(
            src_ref=edge_p.at[2 + way, band],
            dst_ref=edge_p.at[way, band],
            send_sem=edge_p_send.at[way, b],
            recv_sem=edge_p_recv.at[way, band],
            device_id={"phi": right if way == 0 else left, "band": b},
            device_id_type=MESH,
        )

    @pl.when(band < bands - 1)
    def _():
        wind_copy(0, 0, band).start()

    @pl.when(band > 0)
    def _():
        wind_copy(1, 0, band).start()

    for way in range(2):

        @pl.when(has(way))
        def _(way=way):
            fluid_copy(2 + way).start()

        fluid_copy(way).start()
    for s in range(1, bands):
        edge_t_copy(s).start()
    for b in range(bands):
        for way in range(2):
            edge_p_copy(way, b).start()

    def phi_copy(stage, way, block):
        part = pl.ds(pl.multiple_of(block * rows, rows), rows)
        sems = (next_send, next_recv)
        return pltpu.make_async_remote_copy(
            src_ref=send_phi.at[stage, way, :, part],
            dst_ref=recv_phi.at[stage, way, :, part],
            send_sem=sems[0].at[way, block],
            recv_sem=sems[1].at[way, block],
            device_id={"phi": right if way == 0 else left},
            device_id_type=MESH,
        )

    def bin_copy(stage, way, block):
        part = pl.ds(pl.multiple_of(block * rows, rows), rows)
        return pltpu.make_async_remote_copy(
            src_ref=send_bin.at[stage, way, :, part],
            dst_ref=recv_bin.at[stage, way, :, part],
            send_sem=next_send.at[2 + way, block],
            recv_sem=next_recv.at[2 + way, block],
            device_id={"band": band + (1 if way == 0 else -1)},
            device_id_type=MESH,
        )

    def whole_phi(way):
        return pltpu.make_async_remote_copy(
            src_ref=send_phi.at[0, way],
            dst_ref=recv_phi.at[0, way],
            send_sem=halo_send.at[way],
            recv_sem=halo_recv.at[way],
            device_id={"phi": right if way == 0 else left},
            device_id_type=MESH,
        )

    def whole_bin(way):
        return pltpu.make_async_remote_copy(
            src_ref=send_bin.at[0, way],
            dst_ref=recv_bin.at[0, way],
            send_sem=halo_send.at[2 + way],
            recv_sem=halo_recv.at[2 + way],
            device_id={"band": band + (1 if way == 0 else -1)},
            device_id_type=MESH,
        )

    def stage_out(stage, source, start, count):
        own = pl.ds(start, count)
        inner = pl.ds(PAD + start, count)

        def phi_part(k, _):
            last, lead = source[k + 1, azim, inner], source[k + 1, 1, inner]
            send_phi[stage, 0, k, own] = last.astype(jnp.bfloat16)
            send_phi[stage, 1, k, own] = lead.astype(jnp.bfloat16)
            return 0

        def bin_part(p, _):
            last, lead = source[bins, p + 1, inner], source[1, p + 1, inner]
            send_bin[stage, 0, p, own] = last.astype(jnp.bfloat16)
            send_bin[stage, 1, p, own] = lead.astype(jnp.bfloat16)
            return 0

        lax.fori_loop(0, bins, phi_part, 0, unroll=2)
        lax.fori_loop(0, azim, bin_part, 0, unroll=2)

    def stage_in_phi(stage, target, start, count):
        own = pl.ds(start, count)
        inner = pl.ds(PAD + start, count)

        def phi_part(k, _):
            target[k + 1, 0, inner] = recv_phi[stage, 0, k, own].astype(jnp.float32)
            target[k + 1, azim + 1, inner] = recv_phi[stage, 1, k, own].astype(jnp.float32)
            return 0

        lax.fori_loop(0, bins, phi_part, 0, unroll=2)

    def stage_in_bin(stage, target):
        inner = pl.ds(PAD, colat)
        for way, ghost, edge in ((0, 0, 1), (1, bins + 1, bins)):

            @pl.when(comes(way))
            def _(way=way, ghost=ghost):
                def bin_part(p, _):
                    target[ghost, p + 1, inner] = recv_bin[stage, way, p].astype(jnp.float32)
                    return 0

                lax.fori_loop(0, azim, bin_part, 0, unroll=2)

            @pl.when(jnp.logical_not(comes(way)))
            def _(ghost=ghost, edge=edge):
                def bin_part(p, _):
                    target[ghost, p + 1, inner] = target[edge, p + 1, inner]
                    return 0

                lax.fori_loop(0, azim, bin_part, 0, unroll=2)

    def pad_colat(target):
        def part(p, _):
            low = [target[k + 1, p + 1, PAD : PAD + 1] for k in range(bins)]
            high = [target[k + 1, p + 1, PAD + colat - 1 : PAD + colat] for k in range(bins)]
            for k in range(bins):
                target[k + 1, p + 1, PAD - 1 : PAD] = low[k]
                target[k + 1, p + 1, PAD + colat : PAD + colat + 1] = high[k]
            return 0

        lax.fori_loop(0, azim, part, 0)

    load.wait()
    stage_out(0, cells, 0, colat)
    for way in range(2):

        @pl.when(has(way))
        def _(way=way):
            whole_bin(way).start()

        whole_phi(way).start()
    pad_colat(cells)

    lane = lax.broadcasted_iota(jnp.int32, (rows, shells), 1)
    row = lax.broadcasted_iota(jnp.int32, (rows, shells), 0)
    tau = tau_ref[0]
    inv_r = jnp.broadcast_to(inv_r_ref[0:1, first_shell:], (rows, shells))
    inv_hr = inv_r * (1.0 / step_r)
    inv_ht = inv_r * (1.0 / step_t)

    def make_coefs(block):
        start = pl.multiple_of(block * rows, rows)
        part = pl.ds(start, rows)
        inv_hp = inv_r * inv_sin_ref[part, :shells] * (1.0 / step_p)
        cot_r = inv_r * cot_ref[part, :shells]
        below = jnp.maximum(block - 1, 0)
        above = jnp.minimum(block + 1, bands - 1)

        def one(p):
            u_r, u_t, u_p, b_r, b_t, b_p = [
                wind[block, c, p].astype(jnp.float32) for c in range(6)
            ]
            r_hi = jnp.where(lane == shells - 1, u_r, pltpu.roll(u_r, shells - 1, 1))
            r_lo = jnp.where(lane == 0, u_r, pltpu.roll(u_r, 1, 1))
            t_hi_row = jnp.where(
                block == bands - 1, u_t[rows - 1 : rows], edge_t[above, 0, pl.ds(p, 1), :]
            )
            t_lo_row = jnp.where(block == 0, u_t[0:1], edge_t[below, 1, pl.ds(p, 1), :])
            t_hi = jnp.where(row == rows - 1, t_hi_row, pltpu.roll(u_t, rows - 1, 0))
            t_lo = jnp.where(row == 0, t_lo_row, pltpu.roll(u_t, 1, 0))
            p_hi = jnp.where(
                p == azim - 1,
                edge_p[1, block],
                wind[block, 2, jnp.minimum(p + 1, azim - 1)].astype(jnp.float32),
            )
            p_lo = jnp.where(
                p == 0,
                edge_p[0, block],
                wind[block, 2, jnp.maximum(p - 1, 0)].astype(jnp.float32),
            )
            spread = (
                (r_hi - r_lo) * (0.5 * inv_hr)
                + 2.0 * u_r * inv_r
                + (t_hi - t_lo) * (0.5 * inv_ht)
                + cot_r * u_t
                + (p_hi - p_lo) * (0.5 * inv_hp)
            )
            spread = spread.astype(jnp.bfloat16).astype(jnp.float32)
            share = (1.0 - K_RATIO) / (b_r * b_r + b_t * b_t + b_p * b_p + B_FLOOR)
            c_r = tau * (K_RATIO + share * b_r * b_r) * inv_hr * inv_hr
            c_t = tau * (K_RATIO + share * b_t * b_t) * inv_ht * inv_ht
            c_p = tau * (K_RATIO + share * b_p * b_p) * inv_hp * inv_hp
            c_rp = jnp.where(lane == shells - 1, 0.0, c_r)
            c_rm = jnp.where(lane == 0, 0.0, c_r)
            a_r = tau * u_r * inv_hr
            a_r = jnp.where((lane == 0) & (a_r > 0.0), 0.0, a_r)
            a_r = jnp.where((lane == shells - 1) & (a_r < 0.0), 0.0, a_r)
            a_t = tau * u_t * inv_ht
            a_p = tau * u_p * inv_hp
            mu = tau * spread * (1.0 / (3.0 * step_m))
            c_sum = c_rp + c_rm + 2.0 * c_t + 2.0 * c_p
            a_sum = 1.0 - (jnp.abs(a_r) + jnp.abs(a_t) + jnp.abs(a_p) + jnp.abs(mu))
            return (c_rp, c_rm, c_t, c_p, a_r, a_t, a_p, mu, c_sum, a_sum)

        def pair(i, _):
            several = [one(4 * i + j) for j in range(4)]
            for j in range(4):
                for n, value in enumerate(several[j]):
                    coefs[n, 4 * i + j, part] = value
            return 0

        lax.fori_loop(0, azim // 4, pair, 0)

    def apply(source, p, start, finish, low_bin, high_bin):
        part = pl.ds(start, 8)
        mid = pl.ds(PAD + start, 8)
        low = pl.ds(PAD + start - 1, 8)
        high = pl.ds(PAD + start + 1, 8)
        c_rp, c_rm, c_t, c_p, a_r, a_t, a_p, mu, c_sum, a_sum = [
            coefs[n, p, part] for n in range(10)
        ]
        w_r, w_t, w_p, w_m = jnp.abs(a_r), jnp.abs(a_t), jnp.abs(a_p), jnp.abs(mu)
        out_r, out_t, out_p, up_m = a_r > 0.0, a_t > 0.0, a_p > 0.0, mu > 0.0
        values = []
        before = source[low_bin, p + 1, mid]
        here = source[low_bin + 1, p + 1, mid]
        for k in range(low_bin, high_bin):
            after = source[k + 2, p + 1, mid]
            kappa = kappa_ref[band * bins + k]
            r_hi = pltpu.roll(here, shells - 1, 1)
            r_lo = pltpu.roll(here, 1, 1)
            t_hi = source[k + 1, p + 1, high]
            t_lo = source[k + 1, p + 1, low]
            p_hi = source[k + 1, p + 2, mid]
            p_lo = source[k + 1, p, mid]
            curve = (
                (c_rp * r_hi + c_rm * r_lo)
                + (c_t * (t_hi + t_lo) + c_p * (p_hi + p_lo))
                - c_sum * here
            )
            flow = (
                (w_r * jnp.where(out_r, r_lo, r_hi) + w_t * jnp.where(out_t, t_lo, t_hi))
                + (w_p * jnp.where(out_p, p_lo, p_hi) + w_m * jnp.where(up_m, after, before))
                + a_sum * here
            )
            values.append(finish(k, p, mid, kappa * curve + flow))
            before, here = here, after
        return [
            (k + 1, mid, value) for k, value in zip(range(low_bin, high_bin), values)
        ]

    def keep(target, p, results):
        for k, mid, value in results:
            target[k, p + 1, mid] = value

    def finish_first(k, p, mid, value):
        return value

    def finish_second(k, p, mid, value):
        return 1.5 * value - 0.5 * cells[k + 1, p + 1, mid]

    def fluid_in():
        for n in range(8):
            prims[n, 0, own_rows] = recv_f[0, n].astype(jnp.float32)
            prims[n, azim + 1, own_rows] = recv_f[1, n].astype(jnp.float32)
        for way, ghost, edge in ((0, PAD - 1, PAD), (1, PAD + rows, PAD + rows - 1)):
            at = pl.ds(ghost, 1)

            @pl.when(comes(way))
            def _(way=way, at=at):
                for n in range(8):
                    edge_f[way, n] = recv_f[2 + way, n].astype(jnp.float32).reshape(azim, 1, -1)

                def part(p, _):
                    rim = [edge_f[way, n, p] for n in range(8)]
                    for n in range(8):
                        prims[n, p + 1, at] = rim[n]
                    return 0

                lax.fori_loop(0, azim, part, 0)

            @pl.when(jnp.logical_not(comes(way)))
            def _(at=at, edge=edge):
                def part(p, _):
                    rim = [prims[n, p + 1, pl.ds(edge, 1)] for n in range(8)]
                    for n in range(8):
                        prims[n, p + 1, at] = rim[n]
                    return 0

                lax.fori_loop(0, azim, part, 0)

    def fluid_step():
        radial = vel_ref.shape[3]
        spot = lax.broadcasted_iota(jnp.int32, (8, radial), 1)
        scale = dt_ref[0] * inv_r_ref[0:8, :]

        for start in range(0, rows, 8):
            here_rows = pl.ds(pl.multiple_of(band * rows + start, 8), 8)
            scale_p = (1.0 / step_p) * scale * inv_sin_ref[here_rows, :]

            def load_cells(p, shift, start=start):
                return [prims[n, p, pl.ds(PAD + start + shift, 8)] for n in range(8)]

            def faces(p, lower, start=start, scale_p=scale_p, load_cells=load_cells):
                mine = load_cells(p + 1, 0)
                upper = face_flux(
                    fluid_cells(mine, 2), fluid_cells(load_cells(p + 2, 0), 2)
                )
                total = [scale_p * (upper[n] - lower[n]) for n in range(8)]
                here = fluid_cells(mine, 1)
                low = face_flux(fluid_cells(load_cells(p + 1, -1), 1), here)
                high = face_flux(here, fluid_cells(load_cells(p + 1, 1), 1))
                scale_t = (1.0 / step_t) * scale
                total = [total[n] + scale_t * (high[n] - low[n]) for n in range(8)]
                state, flux, speed = fluid_cells(mine, 0)

                def ahead(value):
                    return jnp.where(spot == radial - 1, value, pltpu.roll(value, radial - 1, 1))

                outer = face_flux(
                    (state, flux, speed),
                    ([ahead(x) for x in state], [ahead(x) for x in flux], ahead(speed)),
                )
                scale_r = (1.0 / step_r) * scale
                for n in range(8):
                    inner = jnp.where(spot == 0, flux[n], pltpu.roll(outer[n], 1, 1))
                    fluid[n, p, pl.ds(start, 8)] = state[n] - (
                        total[n] + scale_r * (outer[n] - inner)
                    )
                return upper

            first = face_flux(
                fluid_cells(load_cells(0, 0), 2), fluid_cells(load_cells(1, 0), 2)
            )
            lax.fori_loop(0, azim, faces, first)

    for way in range(2):

        @pl.when(has(way))
        def _(way=way):
            fluid_copy(2 + way).wait_send()

        @pl.when(comes(way))
        def _(way=way):
            fluid_copy(2 + way).wait_recv()

        fluid_copy(way).wait()
    fluid_in()
    fluid_step()
    fluid_store = pltpu.make_async_copy(fluid, fluid_hbm, fluid_sem)
    fluid_store.start()
    for s in range(1, bands):
        edge_t_copy(s).wait()
    for b in range(bands):
        for way in range(2):
            edge_p_copy(way, b).wait_send()
            pltpu.make_async_remote_copy(
                src_ref=edge_p.at[2 + way, b],
                dst_ref=edge_p.at[way, b],
                send_sem=edge_p_send.at[way, b],
                recv_sem=edge_p_recv.at[way, b],
                device_id={"phi": right if way == 0 else left, "band": b},
                device_id_type=MESH,
            ).wait_recv()
    make_coefs(band)
    for way in range(2):

        @pl.when(has(way))
        def _(way=way):
            whole_bin(way).wait_send()

        @pl.when(comes(way))
        def _(way=way):
            whole_bin(way).wait_recv()

        whole_phi(way).wait()
    stage_in_phi(0, cells, 0, colat)
    stage_in_bin(0, cells)

    def second_inner(block):
        start = pl.multiple_of(block * rows, rows)
        for way in range(2):
            phi_copy(1, way, block).wait_recv()
        stage_in_phi(1, firsts, start, rows)

        @pl.when((block == 0) | (block == bands - 1))
        def _():
            pad = jnp.where(block == 0, PAD - 1, PAD + colat)
            edge = jnp.where(block == 0, PAD, PAD + colat - 1)

            def part(p, _):
                rim = [firsts[k + 1, p + 1, pl.ds(edge, 1)] for k in range(bins)]
                for k in range(bins):
                    firsts[k + 1, p + 1, pl.ds(pad, 1)] = rim[k]
                return 0

            lax.fori_loop(0, azim, part, 0)

        def one(i, _):
            for p in (2 * i, 2 * i + 1):
                for part in range(rows // 8):
                    keep(
                        cells, p, apply(firsts, p, start + 8 * part, finish_second, 1, bins - 1)
                    )
            return 0

        lax.fori_loop(0, azim // 2, one, 0)

    def visit(i, _):
        s = (i + 1) // 2
        below = lax.rem(i, 2) == 1
        block = jnp.where(below, band - s, band + s)
        valid = (block >= 0) & (block < bands)

        @pl.when(valid & below)
        def _():
            wind_copy(0, s - 1, block).wait_recv()

            @pl.when(band < bands - 1)
            def _():
                wind_copy(0, s, block).start()

        @pl.when(valid & jnp.logical_not(below) & (s > 0))
        def _():
            wind_copy(1, s - 1, block).wait_recv()

            @pl.when(band > 0)
            def _():
                wind_copy(1, s, block).start()

        @pl.when(valid)
        def _():
            @pl.when(s > 0)
            def _():
                make_coefs(block)

            start = pl.multiple_of(block * rows, rows)

            def one(i, _):
                for p in (2 * i, 2 * i + 1):
                    for part in range(rows // 8):
                        keep(firsts, p, apply(cells, p, start + 8 * part, finish_first, 0, bins))
                return 0

            lax.fori_loop(0, azim // 2, one, 0)
            stage_out(1, firsts, start, rows)
            for way in range(2):

                @pl.when(has(way))
                def _(way=way):
                    bin_copy(1, way, block).start()

                phi_copy(1, way, block).start()

            inner = (s >= 2) | ((s == 1) & (jnp.logical_not(below) | (band == bands - 1)))
            outer = (s >= 1) & ((block == 0) | (block == bands - 1))

            def ready(t, _):
                @pl.when(jnp.where(t == 0, inner, outer))
                def _():
                    second_inner(jnp.where(t == 0, block + jnp.where(below, 1, -1), block))

                return 0

            lax.fori_loop(0, 2, ready, 0)

        return 0

    lax.fori_loop(0, 2 * bands - 1, visit, 0)
    for block in range(bands):
        for way in range(2):

            @pl.when(has(way))
            def _(way=way, block=block):
                bin_copy(1, way, block).wait_send()

            @pl.when(comes(way))
            def _(way=way, block=block):
                bin_copy(1, way, block).wait_recv()

            phi_copy(1, way, block).wait_send()
    stage_in_bin(1, firsts)

    def store(p):
        return pltpu.make_async_copy(
            cells.at[1 : bins + 1, p + 1, PAD : PAD + colat], out_hbm.at[:, p], store_sem.at[p]
        )

    group = math.gcd(colat // 8, 8)

    def second(p, _):
        def one(j, _):
            results = []
            for part in range(group):
                start = pl.multiple_of((j * group + part) * 8, 8)
                results += apply(firsts, p, start, finish_second, 0, 1)
                results += apply(firsts, p, start, finish_second, bins - 1, bins)
            keep(cells, p, results)
            return 0

        lax.fori_loop(0, colat // (8 * group), one, 0)
        store(p).start()
        return 0

    lax.fori_loop(0, azim, second, 0)

    def stored(p, _):
        store(p).wait()
        return 0

    lax.fori_loop(0, azim, stored, 0)
    fluid_store.wait()
    for s in range(bands - 1):

        @pl.when((band - s >= 0) & (band < bands - 1))
        def _(s=s):
            wind_copy(0, s, band - s).wait_send()

        @pl.when((band + s < bands) & (band > 0))
        def _(s=s):
            wind_copy(1, s, band + s).wait_send()


def deliver_kernel(ray_in, fluid_in, ray_out, fluid_out, ray, fluid, in_sem, out_sem):
    parts = [(fluid_in, fluid, fluid_out, n) for n in range(8)]
    parts += [(ray_in, ray, ray_out, k) for k in range(ray.shape[0])]
    loads = [
        pltpu.make_async_copy(a.at[n], b.at[n], in_sem.at[i])
        for i, (a, b, _, n) in enumerate(parts)
    ]
    stores = [
        pltpu.make_async_copy(b.at[n], c.at[n], out_sem.at[i])
        for i, (_, b, c, n) in enumerate(parts)
    ]
    for copy in loads:
        copy.start()
    for load, store in zip(loads, stores):
        load.wait()
        store.start()
    for copy in stores:
        copy.wait()


def cosmic_ray_step(
    rho, velocity, mag, pres, density, kappa, tau, dt, bands, phis, spacing
):
    bins, azim, colat, shells = density.shape
    radial = velocity.shape[3]
    rows = colat // bands
    radius = INNER_RADIUS * np.exp(
        math.log(R_RATIO) / radial * (np.arange(radial) + 0.5)
    )
    theta = COLAT_LOW + COLAT_SPAN * (np.arange(colat) + 0.5) / colat
    wide = np.ones((colat, radial))
    inv_r = jnp.asarray(np.broadcast_to(1.0 / radius, (8, radial)), jnp.float32)
    inv_sin = jnp.asarray(wide / np.sin(theta)[:, None], jnp.float32)
    cot = jnp.asarray(wide * (np.cos(theta) / np.sin(theta))[:, None], jnp.float32)
    dma = pltpu.SemaphoreType.DMA
    vmem = pl.BlockSpec(memory_space=pltpu.VMEM)
    smem = pl.BlockSpec(memory_space=pltpu.SMEM)
    hbm = pl.BlockSpec(memory_space=pl.ANY)
    padded_shape = (bins + 2, azim + 2, colat + 2 * PAD, shells)
    stepped, fluid = pl.pallas_call(
        functools.partial(cosmic_ray_kernel, bands, phis, spacing),
        out_shape=(
            jax.ShapeDtypeStruct(density.shape, jnp.float32),
            jax.ShapeDtypeStruct((8, azim, rows, radial), jnp.float32),
        ),
        in_specs=[smem, smem, smem, vmem, vmem, vmem, vmem, vmem, vmem, vmem, hbm],
        out_specs=(hbm, hbm),
        scratch_shapes=[
            pltpu.VMEM(padded_shape, jnp.float32),
            pltpu.VMEM(padded_shape, jnp.float32),
            pltpu.VMEM((10, azim, colat, shells), jnp.float32),
            pltpu.VMEM((bands, 6, azim, rows, shells), jnp.bfloat16),
            pltpu.VMEM((bands, 2, azim, shells), jnp.float32),
            pltpu.VMEM((4, bands, rows, shells), jnp.float32),
            pltpu.VMEM((2, 2, bins, colat, shells), jnp.bfloat16),
            pltpu.VMEM((2, 2, azim, colat, shells), jnp.bfloat16),
            pltpu.VMEM((2, 2, bins, colat, shells), jnp.bfloat16),
            pltpu.VMEM((2, 2, azim, colat, shells), jnp.bfloat16),
            pltpu.VMEM((8, azim + 2, rows + 2 * PAD, radial), jnp.float32),
            pltpu.VMEM((8, azim, rows, radial), jnp.float32),
            pltpu.VMEM((2, 8, azim, 1, radial), jnp.float32),
            pltpu.VMEM((4, 8, rows, radial), jnp.bfloat16),
            pltpu.VMEM((4, 8, rows, radial), jnp.bfloat16),
            dma,
            dma((4,)),
            dma((4,)),
            dma,
            dma((azim,)),
            dma((2, bands)),
            dma((2, bands)),
            dma((bands,)),
            dma((bands,)),
            dma((2, bands)),
            dma((2, bands)),
            dma((4,)),
            dma((4,)),
            dma((4, bands)),
            dma((4, bands)),
        ],
        compiler_params=pltpu.CompilerParams(
            collective_id=0, has_side_effects=True, vmem_limit_bytes=60 * 1024 * 1024
        ),
        cost_estimate=pl.CostEstimate(
            flops=80 * density.size, bytes_accessed=8 * density.size, transcendentals=0
        ),
        name="cosmic_ray",
    )(kappa, tau, dt, rho, velocity, mag, pres, inv_r, inv_sin, cot, density)
    return pl.pallas_call(
        deliver_kernel,
        out_shape=(
            jax.ShapeDtypeStruct(stepped.shape, jnp.float32),
            jax.ShapeDtypeStruct(fluid.shape, jnp.float32),
        ),
        in_specs=[hbm, hbm],
        out_specs=(hbm, hbm),
        scratch_shapes=[
            pltpu.VMEM(stepped.shape, jnp.float32),
            pltpu.VMEM(fluid.shape, jnp.float32),
            dma((bins + 8,)),
            dma((bins + 8,)),
        ],
        compiler_params=pltpu.CompilerParams(vmem_limit_bytes=60 * 1024 * 1024),
        name="deliver",
    )(stepped, fluid)


def body(
    density,
    velocity,
    magnetic_vector,
    pressure,
    fluid_courant_number,
    cosmic_ray_density,
    diffusion_per_bin,
    super_step_scale,
):
    azim_dev = density.shape[0]
    colat_dev = density.shape[1]
    radial_cell_count = density.shape[2]
    band_count = lax.axis_size("band")
    phi_count = lax.axis_size("phi")
    colatitude_count = colat_dev * band_count
    azimuth_cell_count = azim_dev * phi_count
    bin_dev = cosmic_ray_density.shape[0]
    momentum_bin_count = bin_dev * band_count
    outer_shell_count = cosmic_ray_density.shape[3]
    mesh_spacing = grid_steps(
        radial_cell_count, colatitude_count, azimuth_cell_count, momentum_bin_count
    )
    fluid_rate, cosmic_ray_rate = rate_limits(
        radial_cell_count,
        outer_shell_count,
        colatitude_count,
        azimuth_cell_count,
        momentum_bin_count,
    )
    cosmic_ray_next, fluid_state = cosmic_ray_step(
        density,
        velocity,
        magnetic_vector,
        pressure,
        cosmic_ray_density,
        diffusion_per_bin,
        (super_step_scale / (3.0 * cosmic_ray_rate)).reshape(1),
        (fluid_courant_number / fluid_rate).reshape(1),
        band_count,
        phi_count,
        mesh_spacing,
    )
    return (fluid_state, cosmic_ray_next)


def solution(mesh):
    placed = (
        P("phi", "band", None),
        P(None, "phi", "band", None),
        P(None, "phi", "band", None),
        P("phi", "band", None),
        P(),
        P("band", "phi", None, None),
        P(),
        P(),
    )
    return jax.shard_map(
        body,
        mesh=mesh,
        in_specs=placed,
        out_specs=(P(None, "phi", "band", None), P("band", "phi", None, None)),
        check_vma=False,
    )
```

```python
import functools
import math

import jax
import jax.numpy as jnp
import numpy as np
from jax import lax
from jax.experimental import pallas as pl
from jax.experimental.pallas import tpu as pltpu
from jax.sharding import PartitionSpec as P

ADIABATIC = 5.0 / 3.0
INNER_RADIUS = 0.1
R_RATIO = 30.0
COLAT_LOW = math.pi / 6.0
COLAT_SPAN = 2.0 * math.pi / 3.0
P_RATIO = 1000.0
K_RATIO = 0.1
B_FLOOR = 0.1
V_BOUND = 3.0
B_BOUND = 3.0
P_HIGH = 2.0
RHO_LOW = 0.5
KAPPA_HIGH = 0.5


def grid_steps(n_radial, n_colat, n_azim, n_bins):
    return (
        math.log(R_RATIO) / n_radial,
        COLAT_SPAN / n_colat,
        2.0 * math.pi / n_azim,
        math.log(P_RATIO) / n_bins,
    )


def rate_limits(n_radial, n_shells, n_colat, n_azim, n_bins):
    radial_spacing, colatitude_spacing, azimuth_spacing, step_m = grid_steps(
        n_radial, n_colat, n_azim, n_bins
    )
    sine_lower = math.sin(COLAT_LOW + 0.5 * colatitude_spacing)
    fluid_radius = INNER_RADIUS * math.exp(0.5 * radial_spacing)
    fastest_limit = V_BOUND + math.sqrt((ADIABATIC * P_HIGH + 3.0 * B_BOUND**2) / RHO_LOW)
    fluid_rate = fastest_limit * (
        1.0 / (fluid_radius * radial_spacing)
        + 1.0 / (fluid_radius * colatitude_spacing)
        + 1.0 / (fluid_radius * sine_lower * azimuth_spacing)
    )
    shell_low = INNER_RADIUS * math.exp(radial_spacing * (n_radial - n_shells + 0.5))
    inv_r = 1.0 / (shell_low * radial_spacing)
    inv_t = 1.0 / (shell_low * colatitude_spacing)
    inv_p = 1.0 / (shell_low * sine_lower * azimuth_spacing)
    cosmic_ray_rate = (
        2.0 * KAPPA_HIGH * (inv_r**2 + inv_t**2 + inv_p**2)
        + V_BOUND * (inv_r + inv_t + inv_p)
        + V_BOUND * (inv_r + inv_t + inv_p + 4.0 / shell_low) / (3.0 * step_m)
    )
    return (fluid_rate, cosmic_ray_rate)


def fluid_cells(prim, normal):
    rho, v, b, pres = prim[0], prim[1:4], prim[4:7], prim[7]
    v_n, b_n = v[normal], b[normal]
    b_sq = b[0] * b[0] + b[1] * b[1] + b[2] * b[2]
    v_sq = v[0] * v[0] + v[1] * v[1] + v[2] * v[2]
    energy = pres * (1.0 / (ADIABATIC - 1.0)) + 0.5 * rho * v_sq + 0.5 * b_sq
    total_p = pres + 0.5 * b_sq
    mom = [rho * v[k] for k in range(3)]
    state = [rho] + mom + list(b) + [energy]
    push = [mom[k] * v_n - b[k] * b_n for k in range(3)]
    push[normal] = push[normal] + total_p
    turn = [None if k == normal else v_n * b[k] - b_n * v[k] for k in range(3)]
    work = (energy + total_p) * v_n - b_n * (v[0] * b[0] + v[1] * b[1] + v[2] * b[2])
    stiff = ADIABATIC * pres + b_sq
    speed = jnp.abs(v_n) + stiff * lax.rsqrt(stiff * rho)
    return state, [mom[normal]] + push + turn + [work], speed


def face_flux(low, high):
    wave = jnp.maximum(low[2], high[2])
    jump = [wave * (high[0][n] - low[0][n]) for n in range(8)]
    return [
        -jump[n] if low[1][n] is None else (low[1][n] + high[1][n]) - jump[n] for n in range(8)
    ]


MESH = pl.DeviceIdType.MESH
PAD = 8


def cosmic_ray_kernel(
    bands,
    phis,
    spacing,
    kappa_ref,
    tau_ref,
    dt_ref,
    rho_ref,
    vel_ref,
    mag_ref,
    pres_ref,
    inv_r_ref,
    inv_sin_ref,
    cot_ref,
    f_hbm,
    out_hbm,
    fluid_hbm,
    cells,
    firsts,
    coefs,
    wind,
    edge_t,
    edge_p,
    send_phi,
    send_bin,
    recv_phi,
    recv_bin,
    prims,
    fluid,
    edge_f,
    send_f,
    recv_f,
    fluid_sem,
    fluid_send,
    fluid_recv,
    load_sem,
    store_sem,
    wind_send,
    wind_recv,
    edge_t_send,
    edge_t_recv,
    edge_p_send,
    edge_p_recv,
    halo_send,
    halo_recv,
    next_send,
    next_recv,
):
    bins = f_hbm.shape[0]
    azim = f_hbm.shape[1]
    colat = f_hbm.shape[2]
    shells = f_hbm.shape[3]
    rows = colat // bands
    first_shell = vel_ref.shape[3] - shells
    step_r, step_t, step_p, step_m = spacing
    band = lax.axis_index("band")
    phi = lax.axis_index("phi")
    right = lax.rem(phi + 1, phis)
    left = lax.rem(phi + phis - 1, phis)

    load = pltpu.make_async_copy(
        f_hbm, cells.at[1 : bins + 1, 1 : azim + 1, PAD : PAD + colat], load_sem
    )
    load.start()

    barrier = pltpu.get_barrier_semaphore()
    for b in range(bands):
        for side in (left, right):
            pl.semaphore_signal(
                barrier, inc=1, device_id={"phi": side, "band": b}, device_id_type=MESH
            )
    for s in range(1, bands):
        pl.semaphore_signal(
            barrier,
            inc=1,
            device_id={"band": lax.rem(band + s, bands)},
            device_id_type=MESH,
        )

    own_rows = pl.ds(PAD, rows)

    def take(p, _):
        v = [vel_ref[c, p] for c in range(3)]
        b = [mag_ref[c, p] for c in range(3)]
        prim = [rho_ref[p]] + v + b + [pres_ref[p]]
        shell = [x[:, first_shell:].astype(jnp.bfloat16) for x in v + b]
        for c in range(6):
            wind[band, c, p] = shell[c]
        for n in range(8):
            prims[n, p + 1, own_rows] = prim[n]
            edge_f[0, n, p] = prim[n][rows - 1 : rows]
            edge_f[1, n, p] = prim[n][0:1]
        u_t = shell[1].astype(jnp.float32)
        edge_t[band, 0, pl.ds(p, 1), :] = u_t[0:1]
        edge_t[band, 1, pl.ds(p, 1), :] = u_t[rows - 1 : rows]
        return 0

    lax.fori_loop(0, azim, take, 0)
    edge_p[2, band] = wind[band, 2, azim - 1].astype(jnp.float32)
    edge_p[3, band] = wind[band, 2, 0].astype(jnp.float32)
    for n in range(8):
        send_f[0, n] = prims[n, azim, own_rows].astype(jnp.bfloat16)
        send_f[1, n] = prims[n, 1, own_rows].astype(jnp.bfloat16)
        for way in range(2):
            send_f[2 + way, n] = edge_f[way, n].reshape(azim, -1).astype(jnp.bfloat16)
    pl.semaphore_wait(barrier, 3 * bands - 1)

    def fluid_copy(way):
        if way < 2:
            target = {"phi": right if way == 0 else left}
        else:
            target = {"band": band + (1 if way == 2 else -1)}
        return pltpu.make_async_remote_copy(
            src_ref=send_f.at[way],
            dst_ref=recv_f.at[way],
            send_sem=fluid_send.at[way],
            recv_sem=fluid_recv.at[way],
            device_id=target,
            device_id_type=MESH,
        )

    def has(way):
        return band < bands - 1 if way == 0 else band > 0

    def comes(way):
        return band > 0 if way == 0 else band < bands - 1

    def wind_copy(way, s, block):
        return pltpu.make_async_remote_copy(
            src_ref=wind.at[block],
            dst_ref=wind.at[block],
            send_sem=wind_send.at[way, s],
            recv_sem=wind_recv.at[way, s],
            device_id={"band": band + (1 if way == 0 else -1)},
            device_id_type=MESH,
        )

    def edge_t_copy(s):
        return pltpu.make_async_remote_copy(
            src_ref=edge_t.at[band],
            dst_ref=edge_t.at[band],
            send_sem=edge_t_send.at[s - 1],
            recv_sem=edge_t_recv.at[s - 1],
            device_id={"band": lax.rem(band + s, bands)},
            device_id_type=MESH,
        )

    def edge_p_copy(way, b):
        return pltpu.make_async_remote_copy(
            src_ref=edge_p.at[2 + way, band],
            dst_ref=edge_p.at[way, band],
            send_sem=edge_p_send.at[way, b],
            recv_sem=edge_p_recv.at[way, band],
            device_id={"phi": right if way == 0 else left, "band": b},
            device_id_type=MESH,
        )

    @pl.when(band < bands - 1)
    def _():
        wind_copy(0, 0, band).start()

    @pl.when(band > 0)
    def _():
        wind_copy(1, 0, band).start()

    for way in range(2):

        @pl.when(has(way))
        def _(way=way):
            fluid_copy(2 + way).start()

        fluid_copy(way).start()
    for s in range(1, bands):
        edge_t_copy(s).start()
    for b in range(bands):
        for way in range(2):
            edge_p_copy(way, b).start()

    def phi_copy(stage, way, block):
        part = pl.ds(pl.multiple_of(block * rows, rows), rows)
        sems = (next_send, next_recv)
        return pltpu.make_async_remote_copy(
            src_ref=send_phi.at[stage, way, :, part],
            dst_ref=recv_phi.at[stage, way, :, part],
            send_sem=sems[0].at[way, block],
            recv_sem=sems[1].at[way, block],
            device_id={"phi": right if way == 0 else left},
            device_id_type=MESH,
        )

    def bin_copy(stage, way, block):
        part = pl.ds(pl.multiple_of(block * rows, rows), rows)
        return pltpu.make_async_remote_copy(
            src_ref=send_bin.at[stage, way, :, part],
            dst_ref=recv_bin.at[stage, way, :, part],
            send_sem=next_send.at[2 + way, block],
            recv_sem=next_recv.at[2 + way, block],
            device_id={"band": band + (1 if way == 0 else -1)},
            device_id_type=MESH,
        )

    def whole_phi(way):
        return pltpu.make_async_remote_copy(
            src_ref=send_phi.at[0, way],
            dst_ref=recv_phi.at[0, way],
            send_sem=halo_send.at[way],
            recv_sem=halo_recv.at[way],
            device_id={"phi": right if way == 0 else left},
            device_id_type=MESH,
        )

    def whole_bin(way):
        return pltpu.make_async_remote_copy(
            src_ref=send_bin.at[0, way],
            dst_ref=recv_bin.at[0, way],
            send_sem=halo_send.at[2 + way],
            recv_sem=halo_recv.at[2 + way],
            device_id={"band": band + (1 if way == 0 else -1)},
            device_id_type=MESH,
        )

    def stage_out(stage, source, start, count):
        own = pl.ds(start, count)
        inner = pl.ds(PAD + start, count)

        def phi_part(k, _):
            last, lead = source[k + 1, azim, inner], source[k + 1, 1, inner]
            send_phi[stage, 0, k, own] = last.astype(jnp.bfloat16)
            send_phi[stage, 1, k, own] = lead.astype(jnp.bfloat16)
            return 0

        def bin_part(p, _):
            last, lead = source[bins, p + 1, inner], source[1, p + 1, inner]
            send_bin[stage, 0, p, own] = last.astype(jnp.bfloat16)
            send_bin[stage, 1, p, own] = lead.astype(jnp.bfloat16)
            return 0

        lax.fori_loop(0, bins, phi_part, 0, unroll=2)
        lax.fori_loop(0, azim, bin_part, 0, unroll=2)

    def stage_in_phi(stage, target, start, count):
        own = pl.ds(start, count)
        inner = pl.ds(PAD + start, count)

        def phi_part(k, _):
            target[k + 1, 0, inner] = recv_phi[stage, 0, k, own].astype(jnp.float32)
            target[k + 1, azim + 1, inner] = recv_phi[stage, 1, k, own].astype(jnp.float32)
            return 0

        lax.fori_loop(0, bins, phi_part, 0, unroll=2)

    def stage_in_bin(stage, target):
        inner = pl.ds(PAD, colat)
        for way, ghost, edge in ((0, 0, 1), (1, bins + 1, bins)):

            @pl.when(comes(way))
            def _(way=way, ghost=ghost):
                def bin_part(p, _):
                    target[ghost, p + 1, inner] = recv_bin[stage, way, p].astype(jnp.float32)
                    return 0

                lax.fori_loop(0, azim, bin_part, 0, unroll=2)

            @pl.when(jnp.logical_not(comes(way)))
            def _(ghost=ghost, edge=edge):
                def bin_part(p, _):
                    target[ghost, p + 1, inner] = target[edge, p + 1, inner]
                    return 0

                lax.fori_loop(0, azim, bin_part, 0, unroll=2)

    def pad_colat(target):
        def part(p, _):
            low = [target[k + 1, p + 1, PAD : PAD + 1] for k in range(bins)]
            high = [target[k + 1, p + 1, PAD + colat - 1 : PAD + colat] for k in range(bins)]
            for k in range(bins):
                target[k + 1, p + 1, PAD - 1 : PAD] = low[k]
                target[k + 1, p + 1, PAD + colat : PAD + colat + 1] = high[k]
            return 0

        lax.fori_loop(0, azim, part, 0)

    load.wait()
    stage_out(0, cells, 0, colat)
    for way in range(2):

        @pl.when(has(way))
        def _(way=way):
            whole_bin(way).start()

        whole_phi(way).start()
    pad_colat(cells)

    lane = lax.broadcasted_iota(jnp.int32, (rows, shells), 1)
    row = lax.broadcasted_iota(jnp.int32, (rows, shells), 0)
    tau = tau_ref[0]
    inv_r = jnp.broadcast_to(inv_r_ref[0:1, first_shell:], (rows, shells))
    inv_hr = inv_r * (1.0 / step_r)
    inv_ht = inv_r * (1.0 / step_t)

    def make_coefs(block):
        start = pl.multiple_of(block * rows, rows)
        part = pl.ds(start, rows)
        inv_hp = inv_r * inv_sin_ref[part, :shells] * (1.0 / step_p)
        cot_r = inv_r * cot_ref[part, :shells]
        below = jnp.maximum(block - 1, 0)
        above = jnp.minimum(block + 1, bands - 1)

        def one(p):
            u_r, u_t, u_p, b_r, b_t, b_p = [
                wind[block, c, p].astype(jnp.float32) for c in range(6)
            ]
            r_hi = jnp.where(lane == shells - 1, u_r, pltpu.roll(u_r, shells - 1, 1))
            r_lo = jnp.where(lane == 0, u_r, pltpu.roll(u_r, 1, 1))
            t_hi_row = jnp.where(
                block == bands - 1, u_t[rows - 1 : rows], edge_t[above, 0, pl.ds(p, 1), :]
            )
            t_lo_row = jnp.where(block == 0, u_t[0:1], edge_t[below, 1, pl.ds(p, 1), :])
            t_hi = jnp.where(row == rows - 1, t_hi_row, pltpu.roll(u_t, rows - 1, 0))
            t_lo = jnp.where(row == 0, t_lo_row, pltpu.roll(u_t, 1, 0))
            p_hi = jnp.where(
                p == azim - 1,
                edge_p[1, block],
                wind[block, 2, jnp.minimum(p + 1, azim - 1)].astype(jnp.float32),
            )
            p_lo = jnp.where(
                p == 0,
                edge_p[0, block],
                wind[block, 2, jnp.maximum(p - 1, 0)].astype(jnp.float32),
            )
            spread = (
                (r_hi - r_lo) * (0.5 * inv_hr)
                + 2.0 * u_r * inv_r
                + (t_hi - t_lo) * (0.5 * inv_ht)
                + cot_r * u_t
                + (p_hi - p_lo) * (0.5 * inv_hp)
            )
            spread = spread.astype(jnp.bfloat16).astype(jnp.float32)
            share = (1.0 - K_RATIO) / (b_r * b_r + b_t * b_t + b_p * b_p + B_FLOOR)
            c_r = tau * (K_RATIO + share * b_r * b_r) * inv_hr * inv_hr
            c_t = tau * (K_RATIO + share * b_t * b_t) * inv_ht * inv_ht
            c_p = tau * (K_RATIO + share * b_p * b_p) * inv_hp * inv_hp
            c_rp = jnp.where(lane == shells - 1, 0.0, c_r)
            c_rm = jnp.where(lane == 0, 0.0, c_r)
            a_r = tau * u_r * inv_hr
            a_r = jnp.where((lane == 0) & (a_r > 0.0), 0.0, a_r)
            a_r = jnp.where((lane == shells - 1) & (a_r < 0.0), 0.0, a_r)
            a_t = tau * u_t * inv_ht
            a_p = tau * u_p * inv_hp
            mu = tau * spread * (1.0 / (3.0 * step_m))
            c_sum = c_rp + c_rm + 2.0 * c_t + 2.0 * c_p
            a_sum = 1.0 - (jnp.abs(a_r) + jnp.abs(a_t) + jnp.abs(a_p) + jnp.abs(mu))
            return (c_rp, c_rm, c_t, c_p, a_r, a_t, a_p, mu, c_sum, a_sum)

        def pair(i, _):
            several = [one(4 * i + j) for j in range(4)]
            for j in range(4):
                for n, value in enumerate(several[j]):
                    coefs[n, 4 * i + j, part] = value
            return 0

        lax.fori_loop(0, azim // 4, pair, 0)

    def apply(source, p, start, finish, low_bin, high_bin):
        part = pl.ds(start, 8)
        mid = pl.ds(PAD + start, 8)
        low = pl.ds(PAD + start - 1, 8)
        high = pl.ds(PAD + start + 1, 8)
        c_rp, c_rm, c_t, c_p, a_r, a_t, a_p, mu, c_sum, a_sum = [
            coefs[n, p, part] for n in range(10)
        ]
        w_r, w_t, w_p, w_m = jnp.abs(a_r), jnp.abs(a_t), jnp.abs(a_p), jnp.abs(mu)
        out_r, out_t, out_p, up_m = a_r > 0.0, a_t > 0.0, a_p > 0.0, mu > 0.0
        values = []
        before = source[low_bin, p + 1, mid]
        here = source[low_bin + 1, p + 1, mid]
        for k in range(low_bin, high_bin):
            after = source[k + 2, p + 1, mid]
            kappa = kappa_ref[band * bins + k]
            r_hi = pltpu.roll(here, shells - 1, 1)
            r_lo = pltpu.roll(here, 1, 1)
            t_hi = source[k + 1, p + 1, high]
            t_lo = source[k + 1, p + 1, low]
            p_hi = source[k + 1, p + 2, mid]
            p_lo = source[k + 1, p, mid]
            curve = (
                (c_rp * r_hi + c_rm * r_lo)
                + (c_t * (t_hi + t_lo) + c_p * (p_hi + p_lo))
                - c_sum * here
            )
            flow = (
                (w_r * jnp.where(out_r, r_lo, r_hi) + w_t * jnp.where(out_t, t_lo, t_hi))
                + (w_p * jnp.where(out_p, p_lo, p_hi) + w_m * jnp.where(up_m, after, before))
                + a_sum * here
            )
            values.append(finish(k, p, mid, kappa * curve + flow))
            before, here = here, after
        return [
            (k + 1, mid, value) for k, value in zip(range(low_bin, high_bin), values)
        ]

    def keep(target, p, results):
        for k, mid, value in results:
            target[k, p + 1, mid] = value

    def finish_first(k, p, mid, value):
        return value

    def finish_second(k, p, mid, value):
        return 1.5 * value - 0.5 * cells[k + 1, p + 1, mid]

    def fluid_in():
        for n in range(8):
            prims[n, 0, own_rows] = recv_f[0, n].astype(jnp.float32)
            prims[n, azim + 1, own_rows] = recv_f[1, n].astype(jnp.float32)
        for way, ghost, edge in ((0, PAD - 1, PAD), (1, PAD + rows, PAD + rows - 1)):
            at = pl.ds(ghost, 1)

            @pl.when(comes(way))
            def _(way=way, at=at):
                for n in range(8):
                    edge_f[way, n] = recv_f[2 + way, n].astype(jnp.float32).reshape(azim, 1, -1)

                def part(p, _):
                    rim = [edge_f[way, n, p] for n in range(8)]
                    for n in range(8):
                        prims[n, p + 1, at] = rim[n]
                    return 0

                lax.fori_loop(0, azim, part, 0)

            @pl.when(jnp.logical_not(comes(way)))
            def _(at=at, edge=edge):
                def part(p, _):
                    rim = [prims[n, p + 1, pl.ds(edge, 1)] for n in range(8)]
                    for n in range(8):
                        prims[n, p + 1, at] = rim[n]
                    return 0

                lax.fori_loop(0, azim, part, 0)

    def fluid_step():
        radial = vel_ref.shape[3]
        spot = lax.broadcasted_iota(jnp.int32, (8, radial), 1)
        scale = 0.5 * dt_ref[0] * inv_r_ref[0:8, :]

        for start in range(0, rows, 8):
            here_rows = pl.ds(pl.multiple_of(band * rows + start, 8), 8)
            scale_p = (1.0 / step_p) * scale * inv_sin_ref[here_rows, :]

            def load_cells(p, shift, start=start):
                return [prims[n, p, pl.ds(PAD + start + shift, 8)] for n in range(8)]

            def faces(p, lower, start=start, scale_p=scale_p, load_cells=load_cells):
                mine = load_cells(p + 1, 0)
                upper = face_flux(
                    fluid_cells(mine, 2), fluid_cells(load_cells(p + 2, 0), 2)
                )
                total = [scale_p * (upper[n] - lower[n]) for n in range(8)]
                here = fluid_cells(mine, 1)
                low = face_flux(fluid_cells(load_cells(p + 1, -1), 1), here)
                high = face_flux(here, fluid_cells(load_cells(p + 1, 1), 1))
                scale_t = (1.0 / step_t) * scale
                total = [total[n] + scale_t * (high[n] - low[n]) for n in range(8)]
                state, flux, speed = fluid_cells(mine, 0)

                def ahead(value):
                    return jnp.where(spot == radial - 1, value, pltpu.roll(value, radial - 1, 1))

                outer = face_flux(
                    (state, flux, speed),
                    (
                        [ahead(x) for x in state],
                        [None if x is None else ahead(x) for x in flux],
                        ahead(speed),
                    ),
                )
                scale_r = (1.0 / step_r) * scale
                for n in range(8):
                    rim = 0.0 if flux[n] is None else 2.0 * flux[n]
                    inner = jnp.where(spot == 0, rim, pltpu.roll(outer[n], 1, 1))
                    fluid[n, p, pl.ds(start, 8)] = state[n] - (
                        total[n] + scale_r * (outer[n] - inner)
                    )
                return upper

            first = face_flux(
                fluid_cells(load_cells(0, 0), 2), fluid_cells(load_cells(1, 0), 2)
            )
            lax.fori_loop(0, azim, faces, first)

    for way in range(2):

        @pl.when(has(way))
        def _(way=way):
            fluid_copy(2 + way).wait_send()

        @pl.when(comes(way))
        def _(way=way):
            fluid_copy(2 + way).wait_recv()

        fluid_copy(way).wait()
    fluid_in()
    fluid_step()
    fluid_store = pltpu.make_async_copy(fluid, fluid_hbm, fluid_sem)
    fluid_store.start()
    for s in range(1, bands):
        edge_t_copy(s).wait()
    for b in range(bands):
        for way in range(2):
            edge_p_copy(way, b).wait_send()
            pltpu.make_async_remote_copy(
                src_ref=edge_p.at[2 + way, b],
                dst_ref=edge_p.at[way, b],
                send_sem=edge_p_send.at[way, b],
                recv_sem=edge_p_recv.at[way, b],
                device_id={"phi": right if way == 0 else left, "band": b},
                device_id_type=MESH,
            ).wait_recv()
    make_coefs(band)
    for way in range(2):

        @pl.when(has(way))
        def _(way=way):
            whole_bin(way).wait_send()

        @pl.when(comes(way))
        def _(way=way):
            whole_bin(way).wait_recv()

        whole_phi(way).wait()
    stage_in_phi(0, cells, 0, colat)
    stage_in_bin(0, cells)

    def second_inner(block):
        start = pl.multiple_of(block * rows, rows)
        for way in range(2):
            phi_copy(1, way, block).wait_recv()
        stage_in_phi(1, firsts, start, rows)

        @pl.when((block == 0) | (block == bands - 1))
        def _():
            pad = jnp.where(block == 0, PAD - 1, PAD + colat)
            edge = jnp.where(block == 0, PAD, PAD + colat - 1)

            def part(p, _):
                rim = [firsts[k + 1, p + 1, pl.ds(edge, 1)] for k in range(bins)]
                for k in range(bins):
                    firsts[k + 1, p + 1, pl.ds(pad, 1)] = rim[k]
                return 0

            lax.fori_loop(0, azim, part, 0)

        def one(i, _):
            for p in [4 * i + j for j in range(4)]:
                for part in range(rows // 8):
                    keep(
                        cells, p, apply(firsts, p, start + 8 * part, finish_second, 1, bins - 1)
                    )
            return 0

        lax.fori_loop(0, azim // 4, one, 0)

    def visit(i, _):
        s = (i + 1) // 2
        below = lax.rem(i, 2) == 1
        block = jnp.where(below, band - s, band + s)
        valid = (block >= 0) & (block < bands)

        @pl.when(valid & below)
        def _():
            wind_copy(0, s - 1, block).wait_recv()

            @pl.when(band < bands - 1)
            def _():
                wind_copy(0, s, block).start()

        @pl.when(valid & jnp.logical_not(below) & (s > 0))
        def _():
            wind_copy(1, s - 1, block).wait_recv()

            @pl.when(band > 0)
            def _():
                wind_copy(1, s, block).start()

        @pl.when(valid)
        def _():
            @pl.when(s > 0)
            def _():
                make_coefs(block)

            start = pl.multiple_of(block * rows, rows)

            def one(i, _):
                for p in [4 * i + j for j in range(4)]:
                    for part in range(rows // 8):
                        keep(firsts, p, apply(cells, p, start + 8 * part, finish_first, 0, bins))
                return 0

            lax.fori_loop(0, azim // 4, one, 0)
            stage_out(1, firsts, start, rows)
            for way in range(2):

                @pl.when(has(way))
                def _(way=way):
                    bin_copy(1, way, block).start()

                phi_copy(1, way, block).start()

            inner = (s >= 2) | ((s == 1) & (jnp.logical_not(below) | (band == bands - 1)))
            outer = (s >= 1) & ((block == 0) | (block == bands - 1))

            def ready(t, _):
                @pl.when(jnp.where(t == 0, inner, outer))
                def _():
                    second_inner(jnp.where(t == 0, block + jnp.where(below, 1, -1), block))

                return 0

            lax.fori_loop(0, 2, ready, 0)

        return 0

    lax.fori_loop(0, 2 * bands - 1, visit, 0)
    for block in range(bands):
        for way in range(2):

            @pl.when(has(way))
            def _(way=way, block=block):
                bin_copy(1, way, block).wait_send()

            @pl.when(comes(way))
            def _(way=way, block=block):
                bin_copy(1, way, block).wait_recv()

            phi_copy(1, way, block).wait_send()
    stage_in_bin(1, firsts)

    def store(p):
        return pltpu.make_async_copy(
            cells.at[1 : bins + 1, p + 1, PAD : PAD + colat], out_hbm.at[:, p], store_sem.at[p]
        )

    group = math.gcd(colat // 8, 8)

    def second(p, _):
        def one(j, _):
            results = []
            for part in range(group):
                start = pl.multiple_of((j * group + part) * 8, 8)
                results += apply(firsts, p, start, finish_second, 0, 1)
                results += apply(firsts, p, start, finish_second, bins - 1, bins)
            keep(cells, p, results)
            return 0

        lax.fori_loop(0, colat // (8 * group), one, 0)
        store(p).start()
        return 0

    lax.fori_loop(0, azim, second, 0)

    def stored(p, _):
        store(p).wait()
        return 0

    lax.fori_loop(0, azim, stored, 0)
    fluid_store.wait()
    for s in range(bands - 1):

        @pl.when((band - s >= 0) & (band < bands - 1))
        def _(s=s):
            wind_copy(0, s, band - s).wait_send()

        @pl.when((band + s < bands) & (band > 0))
        def _(s=s):
            wind_copy(1, s, band + s).wait_send()


def deliver_kernel(ray_in, fluid_in, ray_out, fluid_out, ray, fluid, in_sem, out_sem):
    parts = [(fluid_in, fluid, fluid_out, n) for n in range(8)]
    parts += [(ray_in, ray, ray_out, k) for k in range(ray.shape[0])]
    loads = [
        pltpu.make_async_copy(a.at[n], b.at[n], in_sem.at[i])
        for i, (a, b, _, n) in enumerate(parts)
    ]
    stores = [
        pltpu.make_async_copy(b.at[n], c.at[n], out_sem.at[i])
        for i, (_, b, c, n) in enumerate(parts)
    ]
    for copy in loads:
        copy.start()
    for load, store in zip(loads, stores):
        load.wait()
        store.start()
    for copy in stores:
        copy.wait()


def cosmic_ray_step(
    rho, velocity, mag, pres, density, kappa, tau, dt, bands, phis, spacing
):
    bins, azim, colat, shells = density.shape
    radial = velocity.shape[3]
    rows = colat // bands
    radius = INNER_RADIUS * np.exp(
        math.log(R_RATIO) / radial * (np.arange(radial) + 0.5)
    )
    theta = COLAT_LOW + COLAT_SPAN * (np.arange(colat) + 0.5) / colat
    wide = np.ones((colat, radial))
    inv_r = jnp.asarray(np.broadcast_to(1.0 / radius, (8, radial)), jnp.float32)
    inv_sin = jnp.asarray(wide / np.sin(theta)[:, None], jnp.float32)
    cot = jnp.asarray(wide * (np.cos(theta) / np.sin(theta))[:, None], jnp.float32)
    dma = pltpu.SemaphoreType.DMA
    vmem = pl.BlockSpec(memory_space=pltpu.VMEM)
    smem = pl.BlockSpec(memory_space=pltpu.SMEM)
    hbm = pl.BlockSpec(memory_space=pl.ANY)
    padded_shape = (bins + 2, azim + 2, colat + 2 * PAD, shells)
    stepped, fluid = pl.pallas_call(
        functools.partial(cosmic_ray_kernel, bands, phis, spacing),
        out_shape=(
            jax.ShapeDtypeStruct(density.shape, jnp.float32),
            jax.ShapeDtypeStruct((8, azim, rows, radial), jnp.float32),
        ),
        in_specs=[smem, smem, smem, vmem, vmem, vmem, vmem, vmem, vmem, vmem, hbm],
        out_specs=(hbm, hbm),
        scratch_shapes=[
            pltpu.VMEM(padded_shape, jnp.float32),
            pltpu.VMEM(padded_shape, jnp.float32),
            pltpu.VMEM((10, azim, colat, shells), jnp.float32),
            pltpu.VMEM((bands, 6, azim, rows, shells), jnp.bfloat16),
            pltpu.VMEM((bands, 2, azim, shells), jnp.float32),
            pltpu.VMEM((4, bands, rows, shells), jnp.float32),
            pltpu.VMEM((2, 2, bins, colat, shells), jnp.bfloat16),
            pltpu.VMEM((2, 2, azim, colat, shells), jnp.bfloat16),
            pltpu.VMEM((2, 2, bins, colat, shells), jnp.bfloat16),
            pltpu.VMEM((2, 2, azim, colat, shells), jnp.bfloat16),
            pltpu.VMEM((8, azim + 2, rows + 2 * PAD, radial), jnp.float32),
            pltpu.VMEM((8, azim, rows, radial), jnp.float32),
            pltpu.VMEM((2, 8, azim, 1, radial), jnp.float32),
            pltpu.VMEM((4, 8, rows, radial), jnp.bfloat16),
            pltpu.VMEM((4, 8, rows, radial), jnp.bfloat16),
            dma,
            dma((4,)),
            dma((4,)),
            dma,
            dma((azim,)),
            dma((2, bands)),
            dma((2, bands)),
            dma((bands,)),
            dma((bands,)),
            dma((2, bands)),
            dma((2, bands)),
            dma((4,)),
            dma((4,)),
            dma((4, bands)),
            dma((4, bands)),
        ],
        compiler_params=pltpu.CompilerParams(
            collective_id=0, has_side_effects=True, vmem_limit_bytes=60 * 1024 * 1024
        ),
        cost_estimate=pl.CostEstimate(
            flops=80 * density.size, bytes_accessed=8 * density.size, transcendentals=0
        ),
        name="cosmic_ray",
    )(kappa, tau, dt, rho, velocity, mag, pres, inv_r, inv_sin, cot, density)
    return pl.pallas_call(
        deliver_kernel,
        out_shape=(
            jax.ShapeDtypeStruct(stepped.shape, jnp.float32),
            jax.ShapeDtypeStruct(fluid.shape, jnp.float32),
        ),
        in_specs=[hbm, hbm],
        out_specs=(hbm, hbm),
        scratch_shapes=[
            pltpu.VMEM(stepped.shape, jnp.float32),
            pltpu.VMEM(fluid.shape, jnp.float32),
            dma((bins + 8,)),
            dma((bins + 8,)),
        ],
        compiler_params=pltpu.CompilerParams(vmem_limit_bytes=60 * 1024 * 1024),
        name="deliver",
    )(stepped, fluid)


def body(
    density,
    velocity,
    magnetic_vector,
    pressure,
    fluid_courant_number,
    cosmic_ray_density,
    diffusion_per_bin,
    super_step_scale,
):
    azim_dev = density.shape[0]
    colat_dev = density.shape[1]
    radial_cell_count = density.shape[2]
    band_count = lax.axis_size("band")
    phi_count = lax.axis_size("phi")
    colatitude_count = colat_dev * band_count
    azimuth_cell_count = azim_dev * phi_count
    bin_dev = cosmic_ray_density.shape[0]
    momentum_bin_count = bin_dev * band_count
    outer_shell_count = cosmic_ray_density.shape[3]
    mesh_spacing = grid_steps(
        radial_cell_count, colatitude_count, azimuth_cell_count, momentum_bin_count
    )
    fluid_rate, cosmic_ray_rate = rate_limits(
        radial_cell_count,
        outer_shell_count,
        colatitude_count,
        azimuth_cell_count,
        momentum_bin_count,
    )
    cosmic_ray_next, fluid_state = cosmic_ray_step(
        density,
        velocity,
        magnetic_vector,
        pressure,
        cosmic_ray_density,
        diffusion_per_bin,
        (super_step_scale / (3.0 * cosmic_ray_rate)).reshape(1),
        (fluid_courant_number / fluid_rate).reshape(1),
        band_count,
        phi_count,
        mesh_spacing,
    )
    return (fluid_state, cosmic_ray_next)


def solution(mesh):
    placed = (
        P("phi", "band", None),
        P(None, "phi", "band", None),
        P(None, "phi", "band", None),
        P("phi", "band", None),
        P(),
        P("band", "phi", None, None),
        P(),
        P(),
    )
    return jax.shard_map(
        body,
        mesh=mesh,
        in_specs=placed,
        out_specs=(P(None, "phi", "band", None), P("band", "phi", None, None)),
        check_vma=False,
    )
```
